32 devices in a mesh: graph: 32 (over z, y, x, core).
Axes of the slice: x: 2, y: 2, z: 4, core: 2. Of those that a mesh axis runs over, the one named last changes fastest.
Arguments:
- states: bfloat16 [16384, 128], P('graph'), may hold values from -6 to 6
- node_count: int32 [32], P('graph'), may hold values from 256 to 512, as said below
- edge_features: bfloat16 [131072, 16], P('graph'), may hold values from -6 to 6
- edge_count: int32 [32], P('graph'), may hold values from 2048 to 4096, as said below
- target_rows: int32 [131072], P('graph'), may hold values from 0 to 511, as said below
- source_slots: int32 [131072], P('graph'), may hold values from 0 to 2047, as said below
- send_rows: int32 [32, 2048], P('graph'), may hold values from 0 to 511, as said below
- send_count: int32 [32, 32], P('graph'), may hold values from 32 to 64, as said below
- edge_weight_in: bfloat16 [16, 128], replicated, may hold values from -1.5 to 1.5
- edge_bias_in: float32 [128], replicated, may hold values from -3 to 3
- edge_weight_out: bfloat16 [128, 16384], replicated, may hold values from -0.0234375 to 0.0234375
- edge_bias_out: bfloat16 [16384], replicated, may hold values from -0.25 to 0.25
- input_weights: bfloat16 [128, 384], replicated, may hold values from -0.5 to 0.5
- state_weights: bfloat16 [128, 384], replicated, may hold values from -0.5 to 0.5
- input_bias: float32 [384], replicated, may hold values from -3 to 3
- state_bias: float32 [384], replicated, may hold values from -3 to 3
- grad_output: float32 [16384, 128], P('graph'), may hold values from -6 to 6
Outputs:
- new_states: float32 [16384, 128], P('graph')
- grad_states: float32 [16384, 128], P('graph')
- grad_edge_features: float32 [131072, 16], P('graph')
- grad_edge_weight_in: float32 [16, 128], replicated
- grad_edge_bias_in: float32 [128], replicated
- grad_edge_weight_out: float32 [128, 16384], replicated
- grad_edge_bias_out: float32 [16384], replicated
- grad_input_weights: float32 [128, 384], replicated
- grad_state_weights: float32 [128, 384], replicated
- grad_input_bias: float32 [384], replicated
- grad_state_bias: float32 [384], replicated
The draws below stay inside these ranges and needn't reach their ends.
Inputs may be any that keep to these rules, and one draw needn't show every extreme that they name: `node_count`: each device has at least half of its node slots alive, and one device has all. `edge_count`: each device has at least half of its edge slots alive, and one device has all. `target_rows`: below the node count of the edge's own device. `source_slots`: slot p * 64 + c names the c-th state sent by device p, with c below send_count[p, d] for the edge's device d. `send_rows`: row p, entry d * 64 + c is a row of device p below p's node count. `send_count`: entry [p, d] is the number of live slots among the 64 that device p sends to device d; pairs at most one apart along the axis, counted in a loop, have all 64.
All inputs are finite; a program needn't handle non-finite values.
Results may differ from the reference program's by a relative error of at most 0.012.
Values may be sent and summed in bfloat16 or wider, within the bound.
No kernel may reach another device: no remote copies, remote signals or barrier semaphores. Data moves between devices by JAX's collectives and lax.ppermute only.
A program may use at most 192 MiB of HBM per device.

```python
import jax
import jax.numpy as jnp
from jax import lax

HIDDEN_SIZE = 128
EDGE_NET = 128
EDGE_IN = 16
EDGE_DEV = 4096
NODE_DEV = 512
RECV_DEV = 2048
PER_PEER = 64
EDGES = 131072
NODES = 16384
N_GRAPH = 32


def layout(key):
    subkeys = jax.random.split(key, 9)
    device_ids = jnp.arange(N_GRAPH, dtype=jnp.int32)
    full_nodes = jax.random.randint(subkeys[0], (), 0, N_GRAPH)
    node_count = jax.random.randint(subkeys[1], (N_GRAPH,), NODE_DEV // 2, NODE_DEV + 1)
    node_count = jnp.where(device_ids == full_nodes, NODE_DEV, node_count)
    full_edges = jax.random.randint(subkeys[2], (), 0, N_GRAPH)
    edge_count = jax.random.randint(subkeys[3], (N_GRAPH,), EDGE_DEV // 2, EDGE_DEV + 1)
    edge_count = jnp.where(device_ids == full_edges, EDGE_DEV, edge_count)
    first_slot = jnp.arange(RECV_DEV, dtype=jnp.int32)[None, :] == 0
    send_rows = jax.random.randint(subkeys[4], (N_GRAPH, RECV_DEV), 0, node_count[:, None])
    send_rows = jnp.where((device_ids[:, None] == full_nodes) & first_slot, NODE_DEV - 1, send_rows)
    gap = jnp.abs(device_ids[:, None] - device_ids[None, :])
    gap = jnp.minimum(gap, N_GRAPH - gap)
    send_count = jax.random.randint(subkeys[7], (N_GRAPH, N_GRAPH), PER_PEER // 2, PER_PEER + 1)
    send_count = jnp.where(gap <= 1, PER_PEER, send_count)
    first_edge = jnp.arange(EDGE_DEV, dtype=jnp.int32)[None, :] == 0
    target_rows = jax.random.randint(subkeys[5], (N_GRAPH, EDGE_DEV), 0, node_count[:, None])
    target_rows = jnp.where((device_ids[:, None] == full_nodes) & first_edge, NODE_DEV - 1, target_rows)
    peers = jax.random.randint(subkeys[6], (N_GRAPH, EDGE_DEV), 0, N_GRAPH)
    limits = send_count[peers, device_ids[:, None]]
    offsets = jax.random.randint(subkeys[8], (N_GRAPH, EDGE_DEV), 0, limits)
    source_slots = peers * PER_PEER + offsets
    source_slots = jnp.where((device_ids[:, None] == 0) & first_edge, RECV_DEV - 1, source_slots)
    return (node_count, edge_count, send_rows, target_rows.reshape(EDGES), source_slots.reshape(EDGES), send_count)


def draw_node_count(key, part):
    return layout(key)[0]


def draw_edge_count(key, part):
    return layout(key)[1]


def draw_send_rows(key, part):
    return layout(key)[2]


def draw_target_rows(key, part):
    return layout(key)[3]


def draw_source_slots(key, part):
    return layout(key)[4]


def draw_send_count(key, part):
    return layout(key)[5]


def block_levels(rng, shape, cuts, low, top_value):
    factor_of = 1.0
    for position, shards_of in cuts:
        draws = jax.random.uniform(jax.random.fold_in(jax.random.fold_in(rng, 6), position), (shards_of,), jnp.float32, low / len(cuts), top_value / len(cuts))
        factor_of = factor_of * jnp.repeat(jnp.exp(draws), shape[position] // shards_of).reshape((-1,) + (1,) * (len(shape) - 1 - position))
    return factor_of


def noise(key, extent, width, most, cuts=(), kind=jnp.bfloat16):
    result = width * jax.random.normal(key, extent, jnp.float32)
    if cuts:
        result = result * block_levels(key, extent, cuts, -0.22, 0.18)
    return jnp.clip(result, -most, most).astype(kind)


def setup_inputs(seed: int = 0) -> dict:
    splits = jax.random.split(jax.random.key(seed), 18)
    states = noise(splits[0], (NODES, HIDDEN_SIZE), 1.0, 6.0, ((0, 32),))
    node_count = draw_node_count(jax.random.fold_in(splits[17], 71), 0)
    edge_features = noise(splits[2], (EDGES, EDGE_IN), 1.0, 6.0, ((0, 32),))
    edge_count = draw_edge_count(jax.random.fold_in(splits[17], 71), 0)
    target_rows = draw_target_rows(jax.random.fold_in(splits[17], 71), 0)
    source_slots = draw_source_slots(jax.random.fold_in(splits[17], 71), 0)
    send_rows = draw_send_rows(jax.random.fold_in(splits[17], 71), 0)
    send_count = draw_send_count(jax.random.fold_in(splits[17], 71), 0)
    edge_weight_in = noise(splits[8], (EDGE_IN, EDGE_NET), EDGE_IN ** -0.5, 1.5)
    edge_bias_in = noise(splits[9], (EDGE_NET,), 0.5, 3.0, (), jnp.float32)
    edge_weight_out = noise(splits[10], (EDGE_NET, HIDDEN_SIZE * HIDDEN_SIZE), (4 * EDGE_NET * HIDDEN_SIZE) ** -0.5, 0.0234375)
    edge_bias_out = noise(splits[11], (HIDDEN_SIZE * HIDDEN_SIZE,), (4 * HIDDEN_SIZE) ** -0.5, 0.25)
    input_weights = noise(splits[12], (HIDDEN_SIZE, 3 * HIDDEN_SIZE), HIDDEN_SIZE ** -0.5, 0.5)
    state_weights = noise(splits[13], (HIDDEN_SIZE, 3 * HIDDEN_SIZE), HIDDEN_SIZE ** -0.5, 0.5)
    input_bias = noise(splits[14], (3 * HIDDEN_SIZE,), 0.5, 3.0, (), jnp.float32)
    state_bias = noise(splits[15], (3 * HIDDEN_SIZE,), 0.5, 3.0, (), jnp.float32)
    grad_output = noise(splits[16], (NODES, HIDDEN_SIZE), 1.0, 6.0, ((0, 32),), jnp.float32)
    return dict(states=states, node_count=node_count, edge_features=edge_features, edge_count=edge_count, target_rows=target_rows, source_slots=source_slots, send_rows=send_rows, send_count=send_count, edge_weight_in=edge_weight_in, edge_bias_in=edge_bias_in, edge_weight_out=edge_weight_out, edge_bias_out=edge_bias_out, input_weights=input_weights, state_weights=state_weights, input_bias=input_bias, state_bias=state_bias, grad_output=grad_output)


@jax.custom_vjp
def low(v):
    return lax.optimization_barrier(v.astype(jnp.bfloat16)).astype(jnp.float32)

@jax.custom_vjp
def low_back(v):
    return v

def low_keep(v):
    return (low(v), None)

def low_pass(kept, grad):
    return (grad,)

def back_keep(v):
    return (v, None)

def back_low(kept, grad):
    return (low(grad),)
low.defvjp(low_keep, low_pass)
low_back.defvjp(back_keep, back_low)

def reference(states, node_count, edge_features, edge_count, target_rows, source_slots, send_rows, send_count, edge_weight_in, edge_bias_in, edge_weight_out, edge_bias_out, input_weights, state_weights, input_bias, state_bias, grad_output):
    highest = lax.Precision.HIGHEST
    per_peer = RECV_DEV // N_GRAPH
    edge_ids = jnp.arange(EDGES, dtype=jnp.int32)
    node_ids = jnp.arange(NODES, dtype=jnp.int32)
    edge_device = edge_ids // EDGE_DEV
    peer_ids = source_slots // per_peer
    within = source_slots % per_peer
    column = edge_device * per_peer + within
    source_node = peer_ids * NODE_DEV + send_rows[peer_ids, column]
    target_node = edge_device * NODE_DEV + target_rows
    edge_alive = (edge_ids % EDGE_DEV < edge_count[edge_device]).astype(jnp.float32)
    slot_alive = (within < send_count[peer_ids, edge_device]).astype(jnp.float32)[:, None]
    node_alive = (node_ids % NODE_DEV < node_count[node_ids // NODE_DEV]).astype(jnp.float32)[:, None]

    def forward(state_vals, feature_vals, weight_in, bias_in, weight_out, bias_out, input_mat, state_mat, input_vec, state_vec):
        kernel = weight_out.reshape(EDGE_NET * HIDDEN_SIZE, HIDDEN_SIZE)
        bias_matrix = bias_out.reshape(HIDDEN_SIZE, HIDDEN_SIZE)
        sources = state_vals[source_node] * slot_alive

        def edge_messages(pieces):
            features, source, alive = pieces
            preact = low_back(jnp.dot(features, weight_in, precision=highest)) + bias_in
            hidden = jax.nn.silu(preact)
            product = low((hidden[:, :, None] * source[:, None, :]).reshape(EDGE_DEV, EDGE_NET * HIDDEN_SIZE))
            message = jnp.dot(product, kernel, precision=highest) + jnp.dot(source, bias_matrix, precision=highest)
            return low_back(message * alive[:, None])
        messages = lax.map(jax.checkpoint(edge_messages), (feature_vals.reshape(N_GRAPH, EDGE_DEV, EDGE_IN), sources.reshape(N_GRAPH, EDGE_DEV, HIDDEN_SIZE), edge_alive.reshape(N_GRAPH, EDGE_DEV)))
        incoming = jax.ops.segment_sum(messages.reshape(EDGES, HIDDEN_SIZE), target_node, num_segments=NODES)
        gate_in = low_back(jnp.dot(low(incoming), input_mat, precision=highest)) + input_vec
        gate_hid = low_back(jnp.dot(state_vals, state_mat, precision=highest)) + state_vec
        reset_gate = jax.nn.sigmoid(gate_in[:, :HIDDEN_SIZE] + gate_hid[:, :HIDDEN_SIZE])
        update = jax.nn.sigmoid(gate_in[:, HIDDEN_SIZE:2 * HIDDEN_SIZE] + gate_hid[:, HIDDEN_SIZE:2 * HIDDEN_SIZE])
        candidate = jnp.tanh(gate_in[:, 2 * HIDDEN_SIZE:] + reset_gate * gate_hid[:, 2 * HIDDEN_SIZE:])
        return node_alive * ((1.0 - update) * candidate + update * state_vals)
    inputs = [value.astype(jnp.float32) for value in (states, edge_features, edge_weight_in, edge_bias_in, edge_weight_out, edge_bias_out, input_weights, state_weights, input_bias, state_bias)]
    new_states, pullback = jax.vjp(forward, *inputs)
    grads = pullback(grad_output)
    return (new_states, grads[0], grads[1], grads[2], grads[3], grads[4], grads[5], grads[6], grads[7], grads[8], grads[9])
```

```python
import functools

import jax
import jax.numpy as jnp
import numpy as np
from jax import lax
from jax.experimental import pallas as pl
from jax.experimental.pallas import tpu as pltpu
from jax.sharding import PartitionSpec as P

F32 = jnp.float32
LOW = jnp.bfloat16
WINDOW = 256
GROUP = 16
VMEM = pl.BlockSpec(memory_space=pltpu.VMEM)
SMEM = pl.BlockSpec(memory_space=pltpu.SMEM)


def contract(left, right, left_dim, right_dim):
    return lax.dot_general(
        left, right, (((left_dim,), (right_dim,)), ((), ())), preferred_element_type=F32
    )


def iota(shape, dim):
    return lax.broadcasted_iota(jnp.int32, shape, dim)


def one_hot(mask):
    return jnp.where(mask, 1.0, 0.0).astype(LOW)


def call(kernel, out_shape, in_specs, scratch=(), flops=0, limit=56):
    single = not isinstance(out_shape, (tuple, list))
    return pl.pallas_call(
        kernel,
        out_shape=out_shape,
        in_specs=in_specs,
        out_specs=VMEM if single else [VMEM] * len(out_shape),
        scratch_shapes=scratch,
        compiler_params=pltpu.CompilerParams(vmem_limit_bytes=limit * 2**20),
        cost_estimate=pl.CostEstimate(flops=flops, bytes_accessed=2**20, transcendentals=0),
    )


def pick_kernel(index, states, out):
    rows = states.shape[0]
    for start in range(0, out.shape[0], 256):
        chosen = index[start : start + 256, :] == iota((256, rows), 1)
        out[start : start + 256, :] = jnp.dot(
            one_hot(chosen), states[...], preferred_element_type=F32
        ).astype(LOW)


def silu_parts(preact):
    gate = jax.nn.sigmoid(preact)
    return preact * gate, gate * (1.0 + preact * (1.0 - gate))


def first_kernel(order, features, weight, bias_row, bias_col, hidden, hidden_t, preact_t, feat_t, rows):
    edges = features.shape[0]
    width = features.shape[1]

    def move(i, _):
        for step in range(16):
            at = i * 16 + step
            rows[pl.ds(at, 1), :] = features[pl.ds(order[at], 1), :]
        return 0

    lax.fori_loop(0, edges // 16, move, 0)
    eye = one_hot(iota((width, width), 0) == iota((width, width), 1))
    for start in range(0, edges, 512):
        part = rows[start : start + 512, :].astype(LOW)
        feat_t[:, start : start + 512] = contract(eye, part, 1, 1).astype(LOW)
        preact = jnp.dot(part, weight[...], preferred_element_type=F32) + bias_row[...]
        hidden[start : start + 512, :] = silu_parts(preact)[0].astype(LOW)
        turned = contract(weight[...], part, 0, 1) + bias_col[...]
        preact_t[:, start : start + 512] = turned
        hidden_t[:, start : start + 512] = silu_parts(turned)[0].astype(LOW)
    tail = hidden.shape[0] - edges
    hidden[edges:, :] = jnp.zeros((tail, hidden.shape[1]), LOW)
    hidden_t[:, edges:] = jnp.zeros((hidden_t.shape[0], tail), LOW)


def windows(starts, group):
    first, last = starts[group], starts[group + 1]
    base = (first // 128) * 128
    count = jnp.where(last > first, (last - base + (WINDOW - 1)) // WINDOW, 0)
    return base, count


def node_kernel(
    starts, table, node_count, target, slots, received, hidden, weight, bias_matrix, states,
    input_weights, state_weights, input_bias, state_bias, grad_output,
    new_states, direct, grad_low, source_t, keep_0, send_0, keep_1, send_1,
    product, total, picked, source_f, extras, sums, node_sums,
):
    edges = slots.shape[0]
    table_rows = received.shape[0]
    nodes, width = states.shape
    groups = nodes // GROUP
    pieces = table.shape[1]
    per_piece = width // pieces
    for start in range(0, edges, 256):
        chosen = slots[start : start + 256, :] == iota((256, table_rows), 1)
        got = jnp.dot(one_hot(chosen), received[...], preferred_element_type=F32)
        picked[start : start + 256, :] = got.astype(LOW)
        turned = got.T
        source_f[:, start : start + 256] = turned
        source_t[:, start : start + 256] = turned.astype(LOW)
    tail = picked.shape[0] - edges
    picked[edges:, :] = jnp.zeros((tail, width), LOW)
    source_f[:, edges:] = jnp.zeros((width, tail), F32)
    source_t[:, edges:] = jnp.zeros((width, tail), LOW)

    def group_step(group, _):
        base, count = windows(starts, group)
        row = pl.multiple_of(group * GROUP, GROUP)

        def parts(step, emit, emit_sum):
            at = pl.multiple_of(base + WINDOW * step, 128)
            mine = target[:, pl.ds(at, WINDOW)] == iota((GROUP, WINDOW), 0) + group * GROUP
            right = hidden[pl.ds(at, WINDOW), :]
            emit_sum(jnp.dot(one_hot(mine), picked[pl.ds(at, WINDOW), :], preferred_element_type=F32))
            for chunk in range(width // 16):
                left = jnp.concatenate(
                    [
                        jnp.where(
                            mine,
                            jnp.broadcast_to(
                                source_f[pl.ds(chunk * 16 + q, 1), pl.ds(at, WINDOW)], (GROUP, WINDOW)
                            ),
                            0.0,
                        ).astype(LOW)
                        for q in range(16)
                    ],
                    axis=0,
                )
                emit(chunk, jnp.dot(left, right, preferred_element_type=F32))

        @pl.when(count == 1)
        def _():
            def emit(chunk, part):
                product[pl.ds(chunk * 16, 16), pl.ds(row, GROUP), :] = part.reshape(
                    16, GROUP, width
                ).astype(LOW)

            def emit_sum(part):
                sums[pl.ds(row, GROUP), :] = part

            parts(0, emit, emit_sum)

        @pl.when(count != 1)
        def _():
            total[...] = jnp.zeros_like(total)
            sums[pl.ds(row, GROUP), :] = jnp.zeros((GROUP, width), F32)

            def emit(chunk, part):
                total[pl.ds(chunk * 256, 256), :] += part

            def emit_sum(part):
                sums[pl.ds(row, GROUP), :] += part

            def body(step, _):
                parts(step, emit, emit_sum)
                return 0

            lax.fori_loop(0, count, body, 0)
            product[:, pl.ds(row, GROUP), :] = total[...].reshape(width, GROUP, width).astype(LOW)

        return 0

    lax.fori_loop(0, groups, group_step, 0)
    sums_low = sums[...].astype(LOW)
    node_sums[...] = jnp.dot(sums_low, bias_matrix[...], preferred_element_type=F32)

    def multiply(pair, _):
        lanes = pl.multiple_of(pair * 8 * width, 8 * width)
        left = jnp.concatenate([product[pair * 8 + q] for q in range(8)], axis=1)
        right = jnp.concatenate(
            [weight[:, pl.ds(lanes + q * width, width)] for q in range(8)], axis=0
        )
        node_sums[...] += jnp.dot(left, right, preferred_element_type=F32)
        return 0

    lax.fori_loop(0, width // 8, multiply, 0)
    incoming = node_sums[...].astype(LOW)
    alive = jnp.where(iota((nodes, 1), 0) < node_count[0], 1.0, 0.0)
    gate_in = jnp.dot(incoming, input_weights[...], preferred_element_type=F32) + input_bias[...]
    gate_hid = jnp.dot(states[...], state_weights[...], preferred_element_type=F32) + state_bias[...]
    reset = jax.nn.sigmoid(gate_in[:, :width] + gate_hid[:, :width])
    update = jax.nn.sigmoid(gate_in[:, width : 2 * width] + gate_hid[:, width : 2 * width])
    hid_n = gate_hid[:, 2 * width :]
    candidate = jnp.tanh(gate_in[:, 2 * width :] + reset * hid_n)
    values = states[...].astype(F32)
    new_states[...] = alive * ((1.0 - update) * candidate + update * values)
    upstream = grad_output[...] * alive
    grad_cand = upstream * (1.0 - update) * (1.0 - candidate * candidate)
    grad_update = upstream * (values - candidate) * update * (1.0 - update)
    grad_reset = grad_cand * hid_n * reset * (1.0 - reset)
    grad_gate_in = jnp.concatenate([grad_reset, grad_update, grad_cand], axis=1)
    grad_gate_hid = jnp.concatenate([grad_reset, grad_update, grad_cand * reset], axis=1)
    low_in = grad_gate_in.astype(LOW)
    low_hid = grad_gate_hid.astype(LOW)
    low = contract(low_in, input_weights[...], 1, 1).astype(LOW)
    grad_low[...] = low
    direct[...] = upstream * update + contract(low_hid, state_weights[...], 1, 1)
    extras[0:width, :] = contract(sums_low, low, 0, 0)
    grad_in_w = contract(incoming, low_in, 0, 0)
    grad_st_w = contract(states[...], low_hid, 0, 0)
    in_b = jnp.sum(grad_gate_in, axis=0, keepdims=True)
    st_b = jnp.sum(grad_gate_hid, axis=0, keepdims=True)
    for block in range(3):
        lanes = slice(block * width, (block + 1) * width)
        extras[(1 + block) * width : (2 + block) * width, :] = grad_in_w[:, lanes]
        extras[(4 + block) * width : (5 + block) * width, :] = grad_st_w[:, lanes]
    extras[7 * width :, :] = jnp.zeros((extras.shape[0] - 7 * width, width), F32)
    for block in range(3):
        lanes = slice(block * width, (block + 1) * width)
        extras[7 * width + block : 7 * width + block + 1, :] = in_b[:, lanes]
        extras[7 * width + 3 + block : 7 * width + 4 + block, :] = st_b[:, lanes]

    turned = low.astype(F32).T.astype(LOW)
    half = width // 2
    piece_0 = per_piece * half
    piece_1 = keep_1.shape[0] * 2 // pieces
    extra = piece_1 - piece_0
    for side, (out_0, out_1) in enumerate(((keep_0, keep_1), (send_0, send_1))):

        def piece_step(place, _):
            piece = table[0, side * (pieces // 2) + place]
            other = table[1, side * (pieces // 2) + place]
            row_0 = pl.multiple_of(place * piece_0, 16)
            row_1 = pl.multiple_of(other * piece_1, 16)
            for q in range(per_piece):
                tile = jnp.dot(turned, product[piece * per_piece + q], preferred_element_type=F32)
                tile = tile.T.astype(LOW)
                out_0[pl.ds(row_0 + q * half, half), :] = tile[:half, :]
                out_1[pl.ds(row_1 + q * half, half), :] = tile[half:, :]
            out_1[pl.ds(row_1 + piece_0, extra), :] = extras[
                pl.ds(pl.multiple_of(piece * extra, 8), extra), :
            ].astype(LOW)
            return 0

        lax.fori_loop(0, pieces // 2, piece_step, 0)


def edge_sums(starts, target, spread, right, out):
    width = spread.shape[0]
    groups = spread.shape[1] // GROUP
    out[...] = jnp.zeros_like(out)

    def group_step(group, _):
        base, count = windows(starts, group)
        row = pl.multiple_of(group * GROUP, GROUP)

        def body(step, _):
            at = pl.multiple_of(base + WINDOW * step, 128)
            mine = target[:, pl.ds(at, WINDOW)] == iota((GROUP, WINDOW), 0) + group * GROUP
            window = right[:, pl.ds(at, WINDOW)]
            for chunk in range(width // 16):
                left = spread[pl.ds(chunk * 16, 16), pl.ds(row, GROUP), :].reshape(16 * GROUP, width)
                part = jnp.dot(left, window, preferred_element_type=F32).reshape(16, GROUP, WINDOW)
                part = jnp.sum(jnp.where(mine[None], part, 0.0), axis=1)
                out[pl.ds(chunk * 16, 16), pl.ds(at, WINDOW)] += part
            return 0

        lax.fori_loop(0, count, body, 0)
        return 0

    lax.fori_loop(0, groups, group_step, 0)


def source_kernel(starts, target, slots, grad_low, weight, bias_matrix, hidden_t, out, spread, sums, rows):
    width = grad_low.shape[1]
    groups = grad_low.shape[0] // GROUP
    edges = slots.shape[1]

    def expand(pair, _):
        lanes = pl.multiple_of(pair * 2 * width, 2 * width)
        right = jnp.concatenate(
            [weight[:, pl.ds(lanes, width)], weight[:, pl.ds(lanes + width, width)]], axis=0
        )
        both = contract(grad_low[...], right, 1, 1).astype(LOW)
        spread[pair * 2] = both[:, :width]
        spread[pair * 2 + 1] = both[:, width:]
        return 0

    lax.fori_loop(0, width // 2, expand, 0)
    edge_sums(starts, target, spread, hidden_t, sums)
    by_bias = contract(grad_low[...], bias_matrix[...], 1, 1).astype(LOW)
    spread[0] = by_bias

    def group_step(group, _):
        base, count = windows(starts, group)
        row = pl.multiple_of(group * GROUP, GROUP)

        def body(step, _):
            at = pl.multiple_of(base + WINDOW * step, 128)
            mine = target[:, pl.ds(at, WINDOW)] == iota((GROUP, WINDOW), 0) + group * GROUP
            sums[:, pl.ds(at, WINDOW)] += contract(
                spread[0, pl.ds(row, GROUP), :], one_hot(mine), 0, 0
            )
            return 0

        lax.fori_loop(0, count, body, 0)
        return 0

    lax.fori_loop(0, groups, group_step, 0)
    for start in range(0, edges, 256):
        rows[start : start + 256, :] = sums[:, start : start + 256].T.astype(LOW)
    for start in range(0, out.shape[0], 256):
        chosen = slots[...] == iota((256, edges), 0) + start
        out[start : start + 256, :] = jnp.dot(
            one_hot(chosen), rows[...], preferred_element_type=F32
        ).astype(LOW)


def hidden_kernel(
    order, starts, target, grad_low, weight, source_t, preact_t, feat_t, weight_in,
    grad_features, late, spread, sums, rows,
):
    width = grad_low.shape[1]
    narrow, edges = feat_t.shape

    def expand(pair, _):
        at = pl.multiple_of(pair * 2 * width, 2 * width)
        both = contract(grad_low[...], weight[pl.ds(at, 2 * width), :], 1, 1).astype(LOW)
        spread[pair * 2] = both[:, :width]
        spread[pair * 2 + 1] = both[:, width:]
        return 0

    lax.fori_loop(0, width // 2, expand, 0)
    edge_sums(starts, target, spread, source_t, sums)
    padded = jnp.concatenate(
        [weight_in[...], jnp.zeros((width - narrow, width), LOW)], axis=0
    )
    weight_sum = jnp.zeros((narrow, width), F32)
    bias_sum = jnp.zeros((width, 1), F32)
    for start in range(0, edges, 512):
        lanes = slice(start, start + 512)
        grad_preact = sums[:, lanes] * silu_parts(preact_t[:, lanes])[1]
        low = grad_preact.astype(LOW)
        weight_sum = weight_sum + contract(feat_t[:, lanes], low, 1, 1)
        bias_sum = bias_sum + jnp.sum(grad_preact, axis=1, keepdims=True)
        rows[lanes, :] = jnp.dot(padded, low, preferred_element_type=F32).T
    late[...] = jnp.zeros_like(late)
    late[0:narrow, :] = weight_sum
    late[narrow : narrow + 1, :] = jnp.broadcast_to(bias_sum, (width, width)).T[0:1, :]

    def move(i, _):
        for step in range(16):
            at = i * 16 + step
            grad_features[pl.ds(order[at], 1), :] = rows[pl.ds(at, 1), :][:, :narrow]
        return 0

    lax.fori_loop(0, edges // 16, move, 0)


def collect_kernel(index, returned, direct, out):
    rows = index.shape[1]
    for start in range(0, out.shape[0], 256):
        chosen = index[...] == iota((256, rows), 0) + start
        out[start : start + 256, :] = direct[start : start + 256, :] + jnp.dot(
            one_hot(chosen), returned[...], preferred_element_type=F32
        )


def bit_orders(bits):
    rest = list(range(1, bits))
    if bits < 3:
        return ([0] + rest, [0] + rest)
    return ([0] + rest, [0, rest[1], rest[0]] + rest[2:])


def place_tables(devices):
    bits = devices.bit_length() - 1
    tables = []
    for order in bit_orders(bits):
        place = np.arange(devices)
        position = np.zeros(devices, np.int32)
        for level, bit in enumerate(order):
            position |= (((place >> (bits - 1 - level)) & 1) << bit).astype(np.int32)
        tables.append(position)
    return tables


def swap(value, bit, devices):
    pairs = [(i, i ^ (1 << bit)) for i in range(devices)]
    return lax.ppermute(value, "graph", pairs)


def add_low(left, right):
    return (left.astype(F32) + right.astype(F32)).astype(LOW)


def sum_pieces(keep, send, devices):
    bits = devices.bit_length() - 1
    orders = bit_orders(bits)
    parts = range(len(keep))
    got = [swap(value, 0, devices) for value in send]
    keep = list(keep)
    for level in range(1, bits):
        for part in parts:
            half = keep[part].shape[0] // 2
            out = add_low(keep[part][half:], got[part][half:])
            keep[part] = add_low(keep[part][:half], got[part][:half])
            got[part] = swap(out, orders[part][level], devices)
    held = [add_low(keep[part], got[part]) for part in parts]
    for level in range(bits - 1, 0, -1):
        for part in parts:
            other = swap(held[part], orders[part][level], devices)
            held[part] = jnp.concatenate([held[part], other], axis=0)
    return held, [swap(value, 0, devices) for value in held]


def assemble_kernel(table, own_0, own_1, far_0, far_1, out, extra_out):
    pieces = table.shape[1]
    width = out.shape[0]
    per_piece = width // pieces
    half = width // 2
    here = out.shape[1] // (per_piece * width)
    piece_0 = own_0.shape[0] * 2 // pieces
    piece_1 = own_1.shape[0] * 2 // pieces
    extra = piece_1 - piece_0
    for q in range(here):
        piece = pl.program_id(0) * here + q
        for part, (own, far, size) in enumerate(((own_0, far_0, piece_0), (own_1, far_1, piece_1))):
            place = table[part, piece]

            def write(ref, place):
                row = pl.multiple_of(place * size, 16)
                for i in range(per_piece):
                    lane = (q * per_piece + i) * width
                    out[part * half : (part + 1) * half, lane : lane + width] = ref[
                        pl.ds(row + i * half, half), :
                    ].astype(F32)
                if part == 1:
                    extra_out[q * extra : (q + 1) * extra, :] = ref[
                        pl.ds(row + per_piece * half, extra), :
                    ].astype(F32)

            @pl.when(place < pieces // 2)
            def _():
                write(own, place)

            @pl.when(place >= pieces // 2)
            def _():
                write(far, place - pieces // 2)


def on_device(
    states,
    node_count,
    edge_features,
    edge_count,
    target_rows,
    source_slots,
    send_rows,
    send_count,
    edge_weight_in,
    edge_bias_in,
    edge_weight_out,
    edge_bias_out,
    input_weights,
    state_weights,
    input_bias,
    state_bias,
    grad_output,
):
    nodes, width = states.shape
    edges, narrow = edge_features.shape
    devices = lax.axis_size("graph")
    me = lax.axis_index("graph").astype(jnp.int32)
    received_rows = send_rows.shape[1]
    per_peer = received_rows // devices
    groups = nodes // GROUP
    padded = edges + WINDOW
    shape = jax.ShapeDtypeStruct
    bias_matrix = edge_bias_out.reshape(width, width)

    within = jnp.arange(received_rows, dtype=jnp.int32) % per_peer
    index = jnp.where(within < jnp.repeat(send_count[0], per_peer), send_rows[0], -1)
    outgoing = call(pick_kernel, shape((received_rows, width), LOW), [VMEM] * 2)(
        index[:, None], states
    )
    received = lax.all_to_all(
        outgoing.reshape(devices, per_peer, width), "graph", split_axis=0, concat_axis=0, tiled=True
    ).reshape(received_rows, width)

    alive = jnp.arange(edges, dtype=jnp.int32) < edge_count[0]
    key, slots, order = lax.sort(
        (jnp.where(alive, target_rows, nodes), source_slots, jnp.arange(edges, dtype=jnp.int32)),
        num_keys=1,
        is_stable=False,
    )
    starts = jnp.sum(
        (key[None, :] < (jnp.arange(groups + 1, dtype=jnp.int32) * GROUP)[:, None]).astype(jnp.int32),
        axis=1,
    )
    target = jnp.concatenate([key, jnp.full((WINDOW,), nodes, jnp.int32)])[None, :]
    hidden, hidden_t, preact_t, feat_t = call(
        first_kernel,
        (
            shape((padded, width), LOW),
            shape((width, padded), LOW),
            shape((width, edges), F32),
            shape((narrow, edges), LOW),
        ),
        [SMEM] + [VMEM] * 4,
        [pltpu.VMEM((edges, narrow), F32)],
    )(order, edge_features.astype(F32), edge_weight_in, edge_bias_in[None, :], edge_bias_in[:, None])

    tables = place_tables(devices)
    inverse = [np.argsort(t).astype(np.int32) for t in tables]
    half = devices // 2
    out_table = jnp.stack(
        [jnp.asarray(tables[0]) ^ me, jnp.asarray(inverse[1][tables[0]] % half)]
    )
    extra = max(16, -(-(7 * width + 6) // (devices * 16)) * 16)
    piece_0 = (width // devices) * (width // 2)
    piece_1 = piece_0 + extra
    new_states, direct, grad_low, source_t, keep_0, send_0, keep_1, send_1 = call(
        node_kernel,
        (
            shape((nodes, width), F32),
            shape((nodes, width), F32),
            shape((nodes, width), LOW),
            shape((width, padded), LOW),
            shape((half * piece_0, width), LOW),
            shape((half * piece_0, width), LOW),
            shape((half * piece_1, width), LOW),
            shape((half * piece_1, width), LOW),
        ),
        [SMEM] * 3 + [VMEM] * 12,
        [
            pltpu.VMEM((width, nodes, width), LOW),
            pltpu.VMEM((width * GROUP, width), F32),
            pltpu.VMEM((padded, width), LOW),
            pltpu.VMEM((width, padded), F32),
            pltpu.VMEM((devices * extra, width), F32),
            pltpu.VMEM((nodes, width), F32),
            pltpu.VMEM((nodes, width), F32),
        ],
    )(
        starts, out_table, node_count, target, slots[:, None], received, hidden, edge_weight_out,
        bias_matrix, states, input_weights, state_weights, input_bias[None, :], state_bias[None, :],
        grad_output,
    )

    grad_slots = call(
        source_kernel,
        shape((received_rows, width), LOW),
        [SMEM] + [VMEM] * 6,
        [
            pltpu.VMEM((width, nodes, width), LOW),
            pltpu.VMEM((width, padded), F32),
            pltpu.VMEM((edges, width), LOW),
        ],
    )(starts, target, slots[None, :], grad_low, edge_weight_out, bias_matrix, hidden_t)
    returned = lax.all_to_all(
        grad_slots.reshape(devices, per_peer, width), "graph", split_axis=0, concat_axis=0, tiled=True
    ).reshape(received_rows, width)
    grad_states = call(collect_kernel, shape((nodes, width), F32), [VMEM] * 3)(
        index[None, :], returned, direct
    )

    late_rows = -(-(narrow + 1) // 8) * 8
    grad_edge_features, late = call(
        hidden_kernel,
        (shape((edges, narrow), F32), shape((late_rows, width), F32)),
        [SMEM] * 2 + [VMEM] * 7,
        [
            pltpu.VMEM((width, nodes, width), LOW),
            pltpu.VMEM((width, padded), F32),
            pltpu.VMEM((edges, width), F32),
        ],
    )(
        order, starts, target, grad_low, edge_weight_out.reshape(width * width, width), source_t,
        preact_t, feat_t, edge_weight_in,
    )
    for bit in range(devices.bit_length() - 1):
        late = late + swap(late, bit, devices)

    own, far = sum_pieces((keep_0, keep_1), (send_0, send_1), devices)
    in_table = jnp.stack([jnp.asarray(t)[jnp.arange(devices, dtype=jnp.int32) ^ me] for t in inverse])
    here = min(4, devices)
    whole, extras = pl.pallas_call(
        assemble_kernel,
        grid=(devices // here,),
        out_shape=(shape((width, width * width), F32), shape((devices * extra, width), F32)),
        in_specs=[SMEM] + [VMEM] * 4,
        out_specs=(
            pl.BlockSpec((width, here * (width // devices) * width), lambda i: (0, i)),
            pl.BlockSpec((here * extra, width), lambda i: (i, 0)),
        ),
        compiler_params=pltpu.CompilerParams(vmem_limit_bytes=40 * 2**20),
    )(in_table, own[0], own[1], far[0], far[1])

    def columns(first):
        return jnp.concatenate(
            [extras[(first + b) * width : (first + b + 1) * width] for b in range(3)], axis=1
        )

    biases = extras[7 * width : 7 * width + 6]
    return (
        new_states,
        grad_states,
        grad_edge_features,
        late[:narrow],
        late[narrow],
        whole,
        extras[:width].reshape(width * width),
        columns(1),
        columns(4),
        biases[:3].reshape(3 * width),
        biases[3:].reshape(3 * width),
    )


def solution(mesh):
    in_specs = (
        P("graph", None),
        P("graph"),
        P("graph", None),
        P("graph"),
        P("graph"),
        P("graph"),
        P("graph", None),
        P("graph", None),
        P(),
        P(),
        P(),
        P(),
        P(),
        P(),
        P(),
        P(),
        P("graph", None),
    )
    out_specs = (
        P("graph", None),
        P("graph", None),
        P("graph", None),
        P(),
        P(),
        P(),
        P(),
        P(),
        P(),
        P(),
        P(),
    )
    return jax.shard_map(
        on_device, mesh=mesh, in_specs=in_specs, out_specs=out_specs, check_vma=False
    )
```

```python
import jax
import jax.numpy as jnp
import numpy as np
from jax import lax
from jax.experimental import pallas as pl
from jax.experimental.pallas import tpu as pltpu
from jax.sharding import PartitionSpec as P

F32 = jnp.float32
LOW = jnp.bfloat16
WINDOW = 256
GROUP = 16
UNROLL = 4
VMEM = pl.BlockSpec(memory_space=pltpu.VMEM)
SMEM = pl.BlockSpec(memory_space=pltpu.SMEM)

ANY = pl.BlockSpec(memory_space=pl.ANY)


def contract(left, right, left_dim, right_dim):
    return lax.dot_general(
        left, right, (((left_dim,), (right_dim,)), ((), ())), preferred_element_type=F32
    )


def iota(shape, dim):
    return lax.broadcasted_iota(jnp.int32, shape, dim)


def shift_of(size):
    return size.bit_length() - 1


def one_hot(mask):
    return jnp.where(mask, 1.0, 0.0).astype(LOW)


def call(kernel, out_shape, in_specs, scratch=(), out_specs=None, micros=2, limit=60):
    single = not isinstance(out_shape, (tuple, list))
    if out_specs is None:
        out_specs = VMEM if single else [VMEM] * len(out_shape)
    return pl.pallas_call(
        kernel,
        out_shape=out_shape,
        in_specs=in_specs,
        out_specs=out_specs,
        scratch_shapes=scratch,
        compiler_params=pltpu.CompilerParams(vmem_limit_bytes=limit * 2**20),
        cost_estimate=pl.CostEstimate(
            flops=micros * 10**9, bytes_accessed=2**20, transcendentals=0
        ),
    )


def as_columns(row, start, size):
    return jnp.broadcast_to(row[:, start : start + size], (128, size)).T


def pick_kernel(rows, count, states, out, index):
    nodes = states.shape[0]
    devices = count.shape[1]
    slots = rows.shape[1]
    per_peer = slots // devices
    counts = jnp.broadcast_to(count[...].astype(F32), (8, devices)).astype(LOW)
    owner = one_hot((iota((devices, slots), 1) >> shift_of(per_peer)) == iota((devices, slots), 0))
    live = jnp.dot(counts, owner, preferred_element_type=F32)[0:1, :].astype(jnp.int32)
    index[...] = jnp.where((iota((1, slots), 1) & (per_peer - 1)) < live, rows[...], -1)
    for start in range(0, slots, 256):
        column = as_columns(index, start, 256)
        chosen = jnp.concatenate(
            [one_hot(column == iota((256, 128), 1) + lane) for lane in range(0, nodes, 128)], axis=1
        )
        out[start : start + 256, :] = jnp.dot(
            chosen, states[...], preferred_element_type=F32
        ).astype(LOW)


def silu_parts(preact):
    gate = jax.nn.sigmoid(preact)
    return preact * gate, gate * (1.0 + preact * (1.0 - gate))


def upper_half(target):
    return ((target >> 3) & 1).astype(F32)


def steps_size(groups, edges):
    more = 2 * (edges // 128 + UNROLL)
    return 4 + 2 * groups + 2 * more, more


def plan_steps(starts, node_count, steps, groups, edges):
    alive = (node_count[0] + (GROUP - 1)) // GROUP
    middle = (alive + (2 * UNROLL - 1)) // (2 * UNROLL) * UNROLL
    steps[0] = middle // UNROLL
    steps[3] = 0
    _, size = steps_size(groups, edges)

    def group_step(group, found, table):
        first, last = starts[group], starts[group + 1]
        base = (first // 128) * 128
        steps[4 + 2 * group] = group
        steps[5 + 2 * group] = base
        count = jnp.where(last > first, (last - base + (WINDOW - 1)) // WINDOW, 0)

        def more(step, found):
            steps[table + 2 * found] = group
            steps[table + 1 + 2 * found] = base + WINDOW * step
            return found + 1

        return lax.fori_loop(1, count, more, found)

    for half, (low, high) in enumerate(((0, middle), (middle, groups))):
        table = 4 + 2 * groups + half * size
        found = lax.fori_loop(
            low, high, lambda group, found, table=table: group_step(group, found, table), 0
        )
        steps[1 + half] = (found + (UNROLL - 1)) // UNROLL
        for spare in range(UNROLL):
            steps[table + 2 * (found + spare)] = groups + 1
            steps[table + 1 + 2 * (found + spare)] = 0


def first_kernel(
    starts, node_count, key, slots_in, order_in, features, weight, bias,
    steps, target, slots, order, hidden, hidden_t, preact_t, sorted_features,
):
    edges = order.shape[1]
    nodes = (starts.shape[0] - 1) * GROUP
    bias_row = bias[...].reshape(1, -1)
    target[:, :edges] = key[...].reshape(1, edges)
    target[:, edges:] = jnp.full((1, target.shape[1] - edges), nodes, jnp.int32)
    slots[...] = slots_in[...].reshape(1, edges)
    order[...] = order_in[...].reshape(1, edges)
    narrow = weight.shape[0]
    spread = 128 // narrow
    table_rows = edges // spread
    plan_steps(starts, node_count, steps, starts.shape[0] - 1, edges)
    tiled = jnp.concatenate([weight[...]] * spread, axis=0)
    table = jnp.concatenate(
        [features[:, c * table_rows : (c + 1) * table_rows] for c in range(spread)], axis=0
    )
    table = table.astype(F32).T.astype(LOW)
    lane_part = iota((256, 128), 1) >> shift_of(narrow)
    for start in range(0, edges, 256):
        column = as_columns(order, start, 256)
        chosen = jnp.concatenate(
            [
                one_hot((column & (table_rows - 1)) == iota((256, 128), 1) + lane)
                for lane in range(0, table_rows, 128)
            ],
            axis=1,
        )
        got = jnp.dot(chosen, table, preferred_element_type=F32)
        part = jnp.where((column >> shift_of(table_rows)) == lane_part, got, 0.0).astype(LOW)
        sorted_features[start : start + 256, :] = part
        preact = jnp.dot(part, tiled, preferred_element_type=F32) + bias_row
        value = silu_parts(preact)[0]
        upper = upper_half(as_columns(target, start, 256))
        hidden[start : start + 256, 0:128] = (value * (1.0 - upper)).astype(LOW)
        hidden[start : start + 256, 128:256] = (value * upper).astype(LOW)
        turned = preact.T
        preact_t[:, start : start + 256] = turned
        value = value.T
        upper = upper_half(target[:, start : start + 256])
        hidden_t[0:128, start : start + 256] = (value * (1.0 - upper)).astype(LOW)
        hidden_t[128:256, start : start + 256] = (value * upper).astype(LOW)
    hidden[edges:, :] = jnp.zeros((hidden.shape[0] - edges, 256), LOW)
    hidden_t[:, edges:] = jnp.zeros((256, hidden_t.shape[1] - edges), LOW)


def for_steps(steps, groups, edges, halves, together, body):
    _, size = steps_size(groups, edges)
    each = 2 * together
    repeat = UNROLL // together

    def several(at, further):
        for u in range(together):
            body(steps[at + 2 * u], pl.multiple_of(steps[at + 2 * u + 1], 128), further)

    def first_windows(i, _):
        several(4 + each * (repeat * steps[0] * halves[0] + i), False)
        return 0

    def further_windows(i, _):
        count = repeat * steps[1 + halves[0]]
        at = jnp.where(i < count, each * i, size + each * (i - count))
        several(4 + 2 * groups + halves[0] * size + at, True)
        return 0

    lax.fori_loop(0, repeat * len(halves) * steps[0], first_windows, 0)
    lax.fori_loop(0, repeat * sum(steps[1 + half] for half in halves), further_windows, 0)


def node_kernel(
    steps, table, node_count, target, slots, received, hidden, weight, bias_matrix, states,
    input_weights, state_weights, input_bias, state_bias, grad_output,
    new_states, direct, grad_low, by_bias, source_t, keep_0, send_0, keep_1, send_1,
    product, picked, source_f, extras, sums, node_sums,
):
    edges = slots.shape[1]
    lookup = 512
    ways = received.shape[0] // lookup
    nodes, width = states.shape
    groups = nodes // GROUP
    pieces = table.shape[1]
    per_piece = width // pieces
    several = jnp.concatenate([received[w * lookup : (w + 1) * lookup, :] for w in range(ways)], axis=1)
    for start in range(0, edges, 256):
        column = as_columns(slots, start, 256)
        chosen = jnp.concatenate(
            [
                one_hot((column & (lookup - 1)) == iota((256, 128), 1) + lane)
                for lane in range(0, lookup, 128)
            ],
            axis=1,
        )
        got = jnp.dot(chosen, several, preferred_element_type=F32)
        way = column >> shift_of(lookup)
        value = got[:, :width]
        for w in range(1, ways):
            value = jnp.where(way == w, got[:, w * width : (w + 1) * width], value)
        picked[start : start + 256, :] = value.astype(LOW)
        turned = value.T
        source_f[:, start : start + 256] = turned
        upper = upper_half(target[:, start : start + 256])
        source_t[0:width, start : start + 256] = (turned * (1.0 - upper)).astype(LOW)
        source_t[width:, start : start + 256] = (turned * upper).astype(LOW)
    tail = picked.shape[0] - edges
    picked[edges:, :] = jnp.zeros((tail, width), LOW)
    source_f[:, edges:] = jnp.zeros((width, tail), F32)
    source_t[:, edges:] = jnp.zeros((2 * width, tail), LOW)

    def window_step(group, at, further):
        row = pl.multiple_of(jnp.minimum(group, groups - 1) * GROUP, GROUP)
        there = target[:, pl.ds(at, WINDOW)]
        mine = (there >> 4) == group
        pairs = mine & ((there & 7) == iota((8, WINDOW), 0))
        right = hidden[pl.ds(at, WINDOW), :]
        all_rows = one_hot(mine & ((there & 15) == iota((GROUP, WINDOW), 0)))
        part = jnp.dot(all_rows, picked[pl.ds(at, WINDOW), :], preferred_element_type=F32)
        if further:
            part = part + sums[pl.ds(row, GROUP), :]
        sums[pl.ds(row, GROUP), :] = part
        chunk = 32
        for first in range(0, width, chunk):
            left = jnp.concatenate(
                [
                    jnp.where(
                        pairs,
                        jnp.broadcast_to(source_f[pl.ds(first + q, 1), pl.ds(at, WINDOW)], (8, WINDOW)),
                        0.0,
                    )
                    for q in range(chunk)
                ],
                axis=0,
            ).astype(LOW)
            part = jnp.dot(left, right, preferred_element_type=F32).reshape(chunk, 8, 2 * width)
            part = jnp.concatenate([part[:, :, :width], part[:, :, width:]], axis=1)
            if further:
                part = part + product[first : first + chunk, pl.ds(row, GROUP), :].astype(F32)
            product[first : first + chunk, pl.ds(row, GROUP), :] = part.astype(LOW)

    for_steps(steps, groups, edges, (0, 1), UNROLL, window_step)

    def clear(group, _):
        row = pl.multiple_of(group * GROUP, GROUP)
        product[:, pl.ds(row, GROUP), :] = jnp.zeros((width, GROUP, width), LOW)
        sums[pl.ds(row, GROUP), :] = jnp.zeros((GROUP, width), F32)
        return 0

    lax.fori_loop(2 * steps[0] * UNROLL, groups, clear, 0)
    sums_low = sums[...].astype(LOW)
    node_sums[...] = jnp.dot(sums_low, bias_matrix[...], preferred_element_type=F32)

    def multiply(block, _):
        several = 32
        lanes = pl.multiple_of(block * several * width, several * width)
        left = jnp.concatenate([product[block * several + q] for q in range(several)], axis=1)
        right = jnp.concatenate(
            [weight[:, pl.ds(lanes + q * width, width)] for q in range(several)], axis=0
        )
        node_sums[...] += jnp.dot(left, right, preferred_element_type=F32)
        return 0

    lax.fori_loop(0, width // 32, multiply, 0)
    incoming = node_sums[...].astype(LOW)
    alive = jnp.where(iota((nodes, 1), 0) < node_count[0], 1.0, 0.0)
    gate_in = jnp.dot(incoming, input_weights[...], preferred_element_type=F32)
    gate_in = gate_in + input_bias[...].reshape(1, -1)
    gate_hid = jnp.dot(states[...], state_weights[...], preferred_element_type=F32)
    gate_hid = gate_hid + state_bias[...].reshape(1, -1)
    reset = jax.nn.sigmoid(gate_in[:, :width] + gate_hid[:, :width])
    update = jax.nn.sigmoid(gate_in[:, width : 2 * width] + gate_hid[:, width : 2 * width])
    hid_n = gate_hid[:, 2 * width :]
    candidate = jnp.tanh(gate_in[:, 2 * width :] + reset * hid_n)
    values = states[...].astype(F32)
    new_states[...] = alive * ((1.0 - update) * candidate + update * values)
    upstream = grad_output[...] * alive
    grad_cand = upstream * (1.0 - update) * (1.0 - candidate * candidate)
    grad_update = upstream * (values - candidate) * update * (1.0 - update)
    grad_reset = grad_cand * hid_n * reset * (1.0 - reset)
    grad_gate_in = jnp.concatenate([grad_reset, grad_update, grad_cand], axis=1)
    grad_gate_hid = jnp.concatenate([grad_reset, grad_update, grad_cand * reset], axis=1)
    low_in = grad_gate_in.astype(LOW)
    low_hid = grad_gate_hid.astype(LOW)
    low = contract(low_in, input_weights[...], 1, 1).astype(LOW)
    grad_low[...] = low
    by_bias[...] = contract(low, bias_matrix[...], 1, 1).astype(LOW)
    direct[...] = upstream * update + contract(low_hid, state_weights[...], 1, 1)
    extras[0:width, :] = contract(sums_low, low, 0, 0)
    grad_in_w = contract(incoming, low_in, 0, 0)
    grad_st_w = contract(states[...], low_hid, 0, 0)
    in_b = jnp.sum(grad_gate_in, axis=0, keepdims=True)
    st_b = jnp.sum(grad_gate_hid, axis=0, keepdims=True)
    for block in range(3):
        lanes = slice(block * width, (block + 1) * width)
        extras[(1 + block) * width : (2 + block) * width, :] = grad_in_w[:, lanes]
        extras[(4 + block) * width : (5 + block) * width, :] = grad_st_w[:, lanes]
    extras[7 * width :, :] = jnp.zeros((extras.shape[0] - 7 * width, width), F32)
    for block in range(3):
        lanes = slice(block * width, (block + 1) * width)
        extras[7 * width + block : 7 * width + block + 1, :] = in_b[:, lanes]
        extras[7 * width + 3 + block : 7 * width + 4 + block, :] = st_b[:, lanes]

    half = width // 2
    piece_0 = per_piece * half
    piece_1 = keep_1.shape[0] * 2 // pieces
    extra = piece_1 - piece_0
    at_once = max(1, 32 // per_piece)
    for side, (out_0, out_1) in enumerate(((keep_0, keep_1), (send_0, send_1))):

        def piece_step(step, _):
            for u in range(at_once):
                place = step * at_once + u
                piece = jnp.bitwise_xor(table[0, side * (pieces // 2) + place], lax.axis_index("graph"))
                other = table[1, side * (pieces // 2) + place]
                row_0 = pl.multiple_of(place * piece_0, 16)
                row_1 = pl.multiple_of(other * piece_1, 16)
                for q in range(per_piece):
                    tile = contract(product[piece * per_piece + q], low, 0, 0).astype(LOW)
                    out_0[pl.ds(row_0 + q * half, half), :] = tile[:half, :]
                    out_1[pl.ds(row_1 + q * half, half), :] = tile[half:, :]
                out_1[pl.ds(row_1 + piece_0, extra), :] = extras[
                    pl.ds(pl.multiple_of(piece * extra, 8), extra), :
                ].astype(LOW)
            return 0

        lax.fori_loop(0, pieces // 2 // at_once, piece_step, 0)


def fetch(copies):
    started = [pltpu.make_async_copy(*copy) for copy in copies]
    for copy in started:
        copy.start()
    return [copy.wait for copy in started]


def edge_sums(half, steps, target, grad_low, weight, by_bias, hidden_t, source_t, sums, scratch):
    source_sums, hidden_sums = sums
    spread, weight_here, hidden_here, source_here, done = scratch
    nodes, width = grad_low.shape
    groups = nodes // GROUP
    edges = target.shape[1] - WINDOW
    ready, hidden_ready, source_ready = fetch(
        (
            (weight, weight_here, done.at[0]),
            (hidden_t, hidden_here, done.at[1]),
            (source_t, source_here, done.at[2]),
        )
    )
    first_row = 0
    if half:
        first_row = pl.multiple_of(steps[0] * (UNROLL * GROUP), UNROLL * GROUP)
    chosen = grad_low[pl.ds(first_row, nodes // 2), :]
    pitch = width + 4
    several = 16
    ready()

    def expand(block, _):
        lanes = pl.multiple_of(block * several * width, several * width)
        right = jnp.concatenate(
            [weight_here[:, pl.ds(lanes + q * width, width)] for q in range(several)], axis=0
        )
        both = contract(chosen, right, 1, 1)
        for q in range(several):
            spread[pl.ds(block * several + q, nodes // 2, stride=pitch), :] = both[
                :, q * width : (q + 1) * width
            ]
        return 0

    lax.fori_loop(0, width // several, expand, 0)
    hidden_ready()
    source_ready()

    def window_step(group, at, further):
        row = jnp.minimum(group, groups - 1) * GROUP
        there = target[:, pl.ds(at, WINDOW)]
        mine = (there >> 4) == group
        hidden = hidden_here[:, pl.ds(at, WINDOW)]
        source = source_here[:, pl.ds(at, WINDOW)]
        found = jnp.where(mine, there & 7, -1)
        nodes_here = one_hot(mine & ((there & 15) == iota((GROUP, WINDOW), 0)))
        rows = by_bias[pl.ds(pl.multiple_of(row, GROUP), GROUP), :]
        row = jnp.minimum(row - first_row, nodes // 2 - GROUP)
        total = source_sums[:, pl.ds(at, WINDOW)] + contract(rows, nodes_here, 0, 0)
        other = hidden_sums[:, pl.ds(at, WINDOW)]
        for v in range(8):
            pair = [spread[pl.ds((row + v + 8 * h) * pitch, width), :].astype(LOW) for h in range(2)]
            part = jnp.dot(jnp.concatenate(pair, axis=1), hidden, preferred_element_type=F32)
            total = total + jnp.where(found == v, part, 0.0)
            part = contract(jnp.concatenate(pair, axis=0), source, 0, 0)
            other = other + jnp.where(found == v, part, 0.0)
        source_sums[:, pl.ds(at, WINDOW)] = total
        hidden_sums[:, pl.ds(at, WINDOW)] = other

    for_steps(steps, groups, edges, (half,), 2, window_step)


def edges_first_kernel(
    steps, target, grad_low, weight, by_bias, hidden_t, source_t, source_sums, hidden_sums, *scratch
):
    source_sums[...] = jnp.zeros_like(source_sums)
    hidden_sums[...] = jnp.zeros_like(hidden_sums)
    sums = (source_sums, hidden_sums)
    edge_sums(0, steps, target, grad_low, weight, by_bias, hidden_t, source_t, sums, scratch)


def edges_last_kernel(
    steps, target, slots, grad_low, weight, by_bias, hidden_t, source_t, source_in, hidden_in,
    out, hidden_sums, source_sums, *scratch
):
    source_sums[...] = source_in[...]
    hidden_sums[...] = hidden_in[...]
    sums = (source_sums, hidden_sums)
    edge_sums(1, steps, target, grad_low, weight, by_bias, hidden_t, source_t, sums, scratch)
    width = grad_low.shape[1]
    edges = slots.shape[1]
    lookup = 512
    ways = out.shape[0] // lookup
    total = None
    for start in range(0, edges, 1024):
        rights = []
        for at in range(start, start + 1024, 256):
            rows = source_sums[:, at : at + 256].T
            way = as_columns(slots, at, 256) >> shift_of(lookup)
            rights.append(
                jnp.concatenate([jnp.where(way == w, rows, 0.0) for w in range(ways)], axis=1).astype(LOW)
            )
        chosen = one_hot((slots[:, start : start + 1024] & (lookup - 1)) == iota((lookup, 1024), 0))
        part = jnp.dot(chosen, jnp.concatenate(rights, axis=0), preferred_element_type=F32)
        total = part if total is None else total + part
    for w in range(ways):
        out[w * lookup : (w + 1) * lookup, :] = total[:, w * width : (w + 1) * width].astype(LOW)


def features_kernel(
    order, hidden_sums, preact_t, sorted_features, weight_in, grad_features, late
):
    width = hidden_sums.shape[0]
    narrow = weight_in.shape[0]
    edges = order.shape[1]
    copies = width // narrow
    table_rows = edges // copies
    tiled = jnp.concatenate([weight_in[...]] * copies, axis=0)
    weight_sum = jnp.zeros((width, width), F32)
    bias_sum = jnp.zeros((width, 1), F32)
    total = jnp.zeros((table_rows, width), F32)
    for start in range(0, edges, 512):
        lanes = slice(start, start + 512)
        grad_preact = hidden_sums[:, lanes] * silu_parts(preact_t[:, lanes])[1]
        low = grad_preact.astype(LOW)
        weight_sum = weight_sum + jnp.dot(low, sorted_features[lanes, :], preferred_element_type=F32)
        bias_sum = bias_sum + jnp.sum(grad_preact, axis=1, keepdims=True)
        rows = jnp.dot(tiled, low, preferred_element_type=F32)
        owner = (order[:, lanes] >> shift_of(table_rows)) == (iota((width, 512), 0) >> shift_of(narrow))
        rows = jnp.where(owner, rows, 0.0)
        chosen = one_hot((order[:, lanes] & (table_rows - 1)) == iota((table_rows, 512), 0))
        total = total + jnp.dot(chosen, rows.T.astype(LOW), preferred_element_type=F32)
    turned = total.T
    for copy in range(copies):
        grad_features[:, copy * table_rows : (copy + 1) * table_rows] = turned[
            copy * narrow : (copy + 1) * narrow, :
        ]
    late[...] = jnp.zeros_like(late)
    turned = weight_sum.T
    late[0:narrow, :] = sum(turned[c * narrow : (c + 1) * narrow, :] for c in range(copies))
    late[narrow : narrow + 1, :] = jnp.broadcast_to(bias_sum, (width, width)).T[0:1, :]


def collect_kernel(index, returned, direct, out):
    rows = index.shape[1]
    for start in range(0, out.shape[0], 256):
        chosen = index[...] == iota((256, rows), 0) + start
        out[start : start + 256, :] = direct[start : start + 256, :] + jnp.dot(
            one_hot(chosen), returned[...], preferred_element_type=F32
        )


def bit_orders(bits):
    rest = list(range(1, bits))
    if bits < 3:
        return ([0] + rest, [0] + rest)
    return ([0] + rest, [0, rest[1], rest[0]] + rest[2:])


def place_tables(devices):
    bits = devices.bit_length() - 1
    tables = []
    for order in bit_orders(bits):
        place = np.arange(devices)
        position = np.zeros(devices, np.int32)
        for level, bit in enumerate(order):
            position |= (((place >> (bits - 1 - level)) & 1) << bit).astype(np.int32)
        tables.append(position)
    return tables


def swap(value, bit, devices):
    pairs = [(i, i ^ (1 << bit)) for i in range(devices)]
    return lax.ppermute(value, "graph", pairs)


def add_low(left, right):
    return (left.astype(F32) + right.astype(F32)).astype(LOW)


def swap_together(values, bit, devices):
    flat = swap(jnp.concatenate(values, axis=0), bit, devices)
    cuts = np.cumsum([value.shape[0] for value in values])[:-1]
    return jnp.split(flat, cuts, axis=0)


def swap_parts(values, orders, level, devices):
    bits = [order[level] for order in orders]
    if len(set(bits)) == 1 and level > 0:
        return swap_together(values, bits[0], devices)
    return [swap(value, bit, devices) for value, bit in zip(values, bits)]


def sum_pieces(keep, send, devices, works):
    bits = devices.bit_length() - 1
    orders = bit_orders(bits)
    parts = range(len(keep))
    works = list(works)

    def beside(sent, values, got):
        if not works:
            return values, got
        done = [work(sent) for work in works.pop(0)]
        values, got, _ = lax.optimization_barrier((values, got, done))
        return values, got

    keep = list(keep)
    got = swap_parts(send, orders, 0, devices)
    for level in range(1, bits):
        halves = [value.shape[0] // 2 for value in keep]
        send = [add_low(keep[p][halves[p] :], got[p][halves[p] :]) for p in parts]
        keep = [add_low(keep[p][: halves[p]], got[p][: halves[p]]) for p in parts]
        got = swap_parts(send, orders, level, devices)
        keep, got = beside(send, keep, got)
    held = [add_low(keep[p], got[p]) for p in parts]
    for level in range(bits - 1, 0, -1):
        other = swap_parts(held, orders, level, devices)
        held, other = beside(held, held, other)
        held = [jnp.concatenate([held[p], other[p]], axis=0) for p in parts]
    other = swap_parts(held, orders, 0, devices)
    while works:
        held, other = beside(held, held, other)
    return held, other


def assemble_kernel(table, own_0, own_1, far_0, far_1, out, extra_out):
    pieces = table.shape[1]
    width = out.shape[0]
    per_piece = width // pieces
    half = width // 2
    here = out.shape[1] // (per_piece * width)
    piece_0 = own_0.shape[0] * 2 // pieces
    piece_1 = own_1.shape[0] * 2 // pieces
    extra = piece_1 - piece_0
    for q in range(here):
        piece = pl.program_id(0) * here + q
        for part, (own, far, size) in enumerate(((own_0, far_0, piece_0), (own_1, far_1, piece_1))):
            place = table[part, jnp.bitwise_xor(piece, lax.axis_index("graph"))]

            def write(ref, place):
                row = pl.multiple_of(place * size, 16)
                for i in range(per_piece):
                    lane = (q * per_piece + i) * width
                    out[part * half : (part + 1) * half, lane : lane + width] = ref[
                        pl.ds(row + i * half, half), :
                    ].astype(F32)
                if part == 1:
                    extra_out[q * extra : (q + 1) * extra, :] = ref[
                        pl.ds(row + per_piece * half, extra), :
                    ].astype(F32)

            @pl.when(place < pieces // 2)
            def _():
                write(own, place)

            @pl.when(place >= pieces // 2)
            def _():
                write(far, place - pieces // 2)


def on_device(
    states,
    node_count,
    edge_features,
    edge_count,
    target_rows,
    source_slots,
    send_rows,
    send_count,
    edge_weight_in,
    edge_bias_in,
    edge_weight_out,
    edge_bias_out,
    input_weights,
    state_weights,
    input_bias,
    state_bias,
    grad_output,
):
    nodes, width = states.shape
    edges, narrow = edge_features.shape
    devices = lax.axis_size("graph")
    received_rows = send_rows.shape[1]
    per_peer = received_rows // devices
    groups = nodes // GROUP
    padded = edges + WINDOW
    shape = jax.ShapeDtypeStruct
    bias_matrix = edge_bias_out.reshape(width, width)

    outgoing, index = call(
        pick_kernel,
        (shape((received_rows, width), LOW), shape((1, received_rows), jnp.int32)),
        [VMEM] * 3,
    )(send_rows, send_count, states)
    received = lax.all_to_all(
        outgoing.reshape(devices, per_peer, width), "graph", split_axis=0, concat_axis=0, tiled=True
    ).reshape(received_rows, width)

    alive = jnp.arange(edges, dtype=jnp.int32) < edge_count[0]
    key, slots, order = lax.sort(
        (jnp.where(alive, target_rows, nodes), source_slots, jnp.arange(edges, dtype=jnp.int32)),
        num_keys=1,
        is_stable=False,
    )
    starts = jnp.sum(
        (key[None, :] < (jnp.arange(groups + 1, dtype=jnp.int32) * GROUP)[:, None]).astype(jnp.int32),
        axis=1,
    )
    step_count, _ = steps_size(groups, edges)
    steps, target, slots, order, hidden, hidden_t, preact_t, sorted_features = call(
        first_kernel,
        (
            shape((step_count,), jnp.int32),
            shape((1, padded), jnp.int32),
            shape((1, edges), jnp.int32),
            shape((1, edges), jnp.int32),
            shape((padded, 2 * width), LOW),
            shape((2 * width, padded), LOW),
            shape((width, edges), F32),
            shape((edges, width), LOW),
        ),
        [SMEM] * 2 + [VMEM] * 6,
        out_specs=[SMEM] + [VMEM] * 7,
        micros=6,
    )(
        starts, node_count, key, slots, order, edge_features.T,
        edge_weight_in, edge_bias_in,
    )

    tables = place_tables(devices)
    inverse = [np.argsort(t).astype(np.int32) for t in tables]
    half = devices // 2
    out_table = jnp.asarray(np.stack([tables[0], inverse[1][tables[0]] % half]))
    extra = max(16, -(-(7 * width + 6) // (devices * 16)) * 16)
    piece_0 = (width // devices) * (width // 2)
    piece_1 = piece_0 + extra
    new_states, direct, grad_low, by_bias, source_t, keep_0, send_0, keep_1, send_1 = call(
        node_kernel,
        (
            shape((nodes, width), F32),
            shape((nodes, width), F32),
            shape((nodes, width), LOW),
            shape((nodes, width), LOW),
            shape((2 * width, padded), LOW),
            shape((half * piece_0, width), LOW),
            shape((half * piece_0, width), LOW),
            shape((half * piece_1, width), LOW),
            shape((half * piece_1, width), LOW),
        ),
        [SMEM] * 3 + [VMEM] * 12,
        [
            pltpu.VMEM((width, nodes, width), LOW),
            pltpu.VMEM((padded, width), LOW),
            pltpu.VMEM((width, padded), F32),
            pltpu.VMEM((devices * extra, width), F32),
            pltpu.VMEM((nodes, width), F32),
            pltpu.VMEM((nodes, width), F32),
        ],
        micros=28,
        limit=48,
    )(
        steps, out_table, node_count, target, slots, received, hidden, edge_weight_out,
        bias_matrix, states, input_weights, state_weights, input_bias, state_bias, grad_output,
    )

    late_rows = -(-(narrow + 1) // 8) * 8
    scratch = [
        pltpu.VMEM((nodes // 2 * (width + 4) + 16, width), F32),
        pltpu.VMEM((width, width * width), LOW),
        pltpu.VMEM((2 * width, padded), LOW),
        pltpu.VMEM((2 * width, padded), LOW),
        pltpu.SemaphoreType.DMA((3,)),
    ]
    edge_array = shape((width, padded), F32)
    kept = {}

    def tie(value, before):
        return lax.optimization_barrier((value, before))[0]

    def edges_first(before):
        kept["sums"] = call(
            edges_first_kernel,
            (edge_array, edge_array),
            [SMEM] + [VMEM] * 2 + [ANY, VMEM, ANY, ANY],
            scratch,
            micros=12,
            limit=56,
        )(steps, target, tie(grad_low, before), edge_weight_out, by_bias, hidden_t, source_t)
        return kept["sums"]

    def edges_last(before):
        kept["slots"], kept["hidden"] = call(
            edges_last_kernel,
            (shape((received_rows, width), LOW), edge_array),
            [SMEM] + [VMEM] * 3 + [ANY, VMEM, ANY, ANY] + [VMEM] * 2,
            [pltpu.VMEM((width, padded), F32)] + scratch,
            micros=16,
            limit=58,
        )(
            steps, target, slots, tie(grad_low, before), edge_weight_out, by_bias, hidden_t, source_t,
            *kept["sums"],
        )
        return kept["slots"]

    def send_back(before):
        kept["returned"] = lax.all_to_all(
            kept["slots"].reshape(devices, per_peer, width),
            "graph",
            split_axis=0,
            concat_axis=0,
            tiled=True,
        ).reshape(received_rows, width)
        return kept["returned"]

    def features_work(before):
        kept["features"], kept["late"] = call(
            features_kernel,
            (shape((narrow, edges), F32), shape((late_rows, width), F32)),
            [VMEM] * 5,
            micros=6,
            limit=20,
        )(order, tie(kept["hidden"], before), preact_t, sorted_features, edge_weight_in)
        return kept["features"]

    def add_late(bit):
        def work(before):
            late = tie(kept["late"], before)
            kept["late"] = late + swap(late, bit, devices)
            return kept["late"]

        return work

    def collect(before):
        kept["states"] = call(collect_kernel, shape((nodes, width), F32), [VMEM] * 3)(
            index, kept["returned"], tie(direct, before)
        )
        return kept["states"]

    bits = devices.bit_length() - 1
    works = [[edges_first], [edges_last], [features_work]]
    works += [[add_late(bit)] for bit in range(bits)]
    works[min(4, len(works) - 1)].append(send_back)
    works[min(6, len(works) - 1)].append(collect)
    own, far = sum_pieces((keep_0, keep_1), (send_0, send_1), devices, works)
    grad_edge_features, late, grad_states = kept["features"].T, kept["late"], kept["states"]

    in_table = jnp.asarray(np.stack(inverse))
    here = min(4, devices)
    whole, extras = pl.pallas_call(
        assemble_kernel,
        grid=(devices // here,),
        out_shape=(shape((width, width * width), F32), shape((devices * extra, width), F32)),
        in_specs=[SMEM] + [VMEM] * 4,
        out_specs=(
            pl.BlockSpec((width, here * (width // devices) * width), lambda i: (0, i)),
            pl.BlockSpec((here * extra, width), lambda i: (i, 0)),
        ),
        compiler_params=pltpu.CompilerParams(vmem_limit_bytes=40 * 2**20),
    )(in_table, own[0], own[1], far[0], far[1])

    def columns(first):
        return jnp.concatenate(
            [extras[(first + b) * width : (first + b + 1) * width] for b in range(3)], axis=1
        )

    biases = extras[7 * width : 7 * width + 6]
    return (
        new_states,
        grad_states,
        grad_edge_features,
        late[:narrow],
        late[narrow],
        whole,
        extras[:width].reshape(width * width),
        columns(1),
        columns(4),
        biases[:3].reshape(3 * width),
        biases[3:].reshape(3 * width),
    )


def solution(mesh):
    in_specs = (
        P("graph", None),
        P("graph"),
        P("graph", None),
        P("graph"),
        P("graph"),
        P("graph"),
        P("graph", None),
        P("graph", None),
        P(),
        P(),
        P(),
        P(),
        P(),
        P(),
        P(),
        P(),
        P("graph", None),
    )
    out_specs = (
        P("graph", None),
        P("graph", None),
        P("graph", None),
        P(),
        P(),
        P(),
        P(),
        P(),
        P(),
        P(),
        P(),
    )
    return jax.shard_map(
        on_device, mesh=mesh, in_specs=in_specs, out_specs=out_specs, check_vma=False
    )
```

```python
import jax
import jax.numpy as jnp
import numpy as np
from jax import lax
from jax.experimental import pallas as pl
from jax.experimental.pallas import tpu as pltpu
from jax.sharding import PartitionSpec as P

F32 = jnp.float32
LOW = jnp.bfloat16
WINDOW = 256
GROUP = 16
UNROLL = 4
SLOTS = 2048
VMEM = pl.BlockSpec(memory_space=pltpu.VMEM)
SMEM = pl.BlockSpec(memory_space=pltpu.SMEM)

ANY = pl.BlockSpec(memory_space=pl.ANY)


def contract(left, right, left_dim, right_dim):
    return lax.dot_general(
        left, right, (((left_dim,), (right_dim,)), ((), ())), preferred_element_type=F32
    )


def iota(shape, dim):
    return lax.broadcasted_iota(jnp.int32, shape, dim)


def shift_of(size):
    return size.bit_length() - 1


def one_hot(mask):
    return jnp.where(mask, 1.0, 0.0).astype(LOW)


def call(kernel, out_shape, in_specs, scratch=(), out_specs=None, micros=2, limit=60, aliases=None):
    single = not isinstance(out_shape, (tuple, list))
    if out_specs is None:
        out_specs = VMEM if single else [VMEM] * len(out_shape)
    return pl.pallas_call(
        kernel,
        out_shape=out_shape,
        in_specs=in_specs,
        out_specs=out_specs,
        scratch_shapes=scratch,
        input_output_aliases=aliases or {},
        compiler_params=pltpu.CompilerParams(vmem_limit_bytes=limit * 2**20),
        cost_estimate=pl.CostEstimate(
            flops=micros * 10**9, bytes_accessed=2**20, transcendentals=0
        ),
    )


def fetch(copies):
    started = [pltpu.make_async_copy(*copy) for copy in copies]
    for copy in started:
        copy.start()
    return [copy.wait for copy in started]


def as_columns(row, start, size):
    return jnp.broadcast_to(row[:, start : start + size], (128, size)).T


def pick_kernel(rows, count, states, out, index):
    nodes = states.shape[0]
    devices = count.shape[1]
    slots = rows.shape[1]
    per_peer = slots // devices
    counts = jnp.broadcast_to(count[...].astype(F32), (8, devices)).astype(LOW)
    owner = one_hot((iota((devices, slots), 1) >> shift_of(per_peer)) == iota((devices, slots), 0))
    live = jnp.dot(counts, owner, preferred_element_type=F32)[0:1, :].astype(jnp.int32)
    index[...] = jnp.where((iota((1, slots), 1) & (per_peer - 1)) < live, rows[...], -1)
    for start in range(0, slots, 256):
        column = as_columns(index, start, 256)
        chosen = jnp.concatenate(
            [one_hot(column == iota((256, 128), 1) + lane) for lane in range(0, nodes, 128)], axis=1
        )
        out[start : start + 256, :] = jnp.dot(
            chosen, states[...], preferred_element_type=F32
        ).astype(LOW)


def silu_parts(preact):
    gate = jax.nn.sigmoid(preact)
    return preact * gate, gate * (1.0 + preact * (1.0 - gate))


def upper_half(target):
    return ((target >> 3) & 1).astype(F32)


def steps_size(groups, edges):
    return 2 + 2 * (groups + edges // 128 + UNROLL)


def plan_steps(starts, node_count, steps, groups):
    alive = (node_count[0] + (GROUP - 1)) // GROUP

    def base_of(group):
        return (starts[group] // 128) * 128

    def first_step(group, _):
        steps[2 + 2 * group] = group
        steps[3 + 2 * group] = base_of(group)
        return 0

    def further_step(group, at):
        first, last = starts[group], starts[group + 1]
        base = base_of(group)
        count = jnp.where(last > first, (last - base + (WINDOW - 1)) // WINDOW, 0)

        def more(step, at):
            steps[at] = group
            steps[at + 1] = base + WINDOW * step
            return at + 2

        return lax.fori_loop(1, count, more, at)

    lax.fori_loop(0, alive, first_step, 0)
    at = lax.fori_loop(0, alive, further_step, 2 + 2 * alive)
    steps[0] = alive // UNROLL
    steps[1] = (at // 2 - 1 + (UNROLL - 1)) // UNROLL - alive // UNROLL
    for spare in range(UNROLL):
        steps[at + 2 * spare] = groups + 1
        steps[at + 1 + 2 * spare] = 0


def key_bits(nodes, slots, edges):
    low, high = shift_of(edges), shift_of(edges) + shift_of(slots)
    assert high + shift_of(nodes) <= 32
    return low, high, 1 << (31 - high)


def pack_key(target, slot, row, nodes, slots, edges):
    low, high, offset = key_bits(nodes, slots, edges)
    return ((target - offset) << high) | (slot << low) | row


def unpack_key(key, nodes, edges):
    low, high, offset = key_bits(nodes, SLOTS, edges)
    return (key >> high) + offset, (key >> low) & (SLOTS - 1), key & (edges - 1)


def first_kernel(
    starts, node_count, edge_count, packed, features, weight, bias,
    steps, target, slots, order, hidden_out, preact_out, sorted_out, hidden_t, preact_t, sorted_features, left,
):
    edges = order.shape[1]
    nodes = (starts.shape[0] - 1) * GROUP
    key = packed[...].reshape(1, edges)
    here, slot, row = unpack_key(key, nodes, edges)
    target[:, :edges] = jnp.where(iota((1, edges), 1) < edge_count[0], here, nodes)
    target[:, edges:] = jnp.full((1, target.shape[1] - edges), nodes, jnp.int32)
    slots[...] = slot
    order[...] = row
    narrow = weight.shape[0]
    spread = 128 // narrow
    table_rows = edges // spread
    plan_steps(starts, node_count, steps, starts.shape[0] - 1)
    tiled = jnp.concatenate([weight[...]] * spread, axis=0)
    table = jnp.concatenate(
        [features[:, c * table_rows : (c + 1) * table_rows] for c in range(spread)], axis=0
    )
    table = table.astype(F32).T.astype(LOW)
    lane_part = iota((256, 128), 1) >> shift_of(narrow)
    bias_column = as_columns(bias[...].reshape(1, 128), 0, 128)
    bias_columns = jnp.concatenate([bias_column] * 2, axis=1)
    hidden_t[:, edges:] = jnp.zeros((256, hidden_t.shape[1] - edges), LOW)
    waits = []
    for start in range(0, edges, 256):
        column = as_columns(order, start, 256)
        low = column & (table_rows - 1)
        chosen = jnp.concatenate(
            [one_hot(low == iota((256, 128), 1) + lane) for lane in range(0, table_rows, 128)], axis=1
        )
        got = jnp.dot(chosen, table, preferred_element_type=F32)
        part = jnp.where((column >> shift_of(table_rows)) == lane_part, got, 0.0).astype(LOW)
        sorted_features[start : start + 256, :] = part
        preact = contract(tiled, part, 0, 1) + bias_columns
        preact_t[:, start : start + 256] = preact
        value = silu_parts(preact)[0]
        upper = upper_half(target[:, start : start + 256])
        hidden_t[0:128, start : start + 256] = (value * (1.0 - upper)).astype(LOW)
        hidden_t[128:256, start : start + 256] = (value * upper).astype(LOW)
        quarter = edges // 4
        if (start + 256) % quarter == 0:
            part = start // quarter
            lanes = slice(part * quarter, (part + 1) * quarter)
            wide = lanes if part < 3 else slice(part * quarter, hidden_t.shape[1])
            waits += fetch(
                [
                    (hidden_t.at[:, wide], hidden_out.at[:, wide], left.at[part]),
                    (preact_t.at[:, lanes], preact_out.at[:, lanes], left.at[4 + part]),
                    (sorted_features.at[lanes, :], sorted_out.at[lanes, :], left.at[8 + part]),
                ]
            )
    for wait in waits:
        wait()


def for_steps(steps, together, body, apart=False):
    each = 2 * together
    repeat = UNROLL // together

    def run(count, first, further):
        def several(i, _):
            for u in range(together):
                at = first + each * i + 2 * u
                body(steps[at], pl.multiple_of(steps[at + 1], 128), further)
            return 0

        lax.fori_loop(0, repeat * count, several, 0)

    if not apart:
        run(steps[0] + steps[1], 2, None)
        return
    run(steps[0], 2, False)
    run(steps[1], 2 + 2 * UNROLL * steps[0], True)


def node_kernel(
    steps, table, node_count, target, slots, received, hidden_there, weight_there, bias_matrix, states,
    input_weights, state_weights, input_bias, state_bias, grad_output,
    new_states, direct, grad_low, by_bias, source_out, *rest,
):
    pieces_out, rest = rest[:4], rest[4:]
    product, picked, source_f, extras, sums, node_sums, hidden, weight, source_t, *rest = rest
    pieces_here, (arrived, left) = rest[:4], rest[4:]
    keep_0, send_0, keep_1, send_1 = pieces_here
    (hidden_ready,) = fetch([(hidden_there, hidden, arrived.at[0])])
    edges = slots.shape[1]
    lookup = 512
    ways = received.shape[0] // lookup
    nodes, width = states.shape
    groups = nodes // GROUP
    pieces = table.shape[1]
    per_piece = width // pieces
    several = jnp.concatenate([received[w * lookup : (w + 1) * lookup, :] for w in range(ways)], axis=1)
    for start in range(0, edges, 256):
        column = as_columns(slots, start, 256)
        chosen = jnp.concatenate(
            [
                one_hot((column & (lookup - 1)) == iota((256, 128), 1) + lane)
                for lane in range(0, lookup, 128)
            ],
            axis=1,
        )
        got = jnp.dot(chosen, several, preferred_element_type=F32)
        way = column >> shift_of(lookup)
        value = got[:, :width]
        for w in range(1, ways):
            value = jnp.where(way == w, got[:, w * width : (w + 1) * width], value)
        picked[start : start + 256, :] = value.astype(LOW)
        turned = value.T
        source_f[:, start : start + 256] = turned
        upper = upper_half(target[:, start : start + 256])
        source_t[0:width, start : start + 256] = (turned * (1.0 - upper)).astype(LOW)
        source_t[width:, start : start + 256] = (turned * upper).astype(LOW)
    tail = picked.shape[0] - edges
    picked[edges:, :] = jnp.zeros((tail, width), LOW)
    source_f[:, edges:] = jnp.zeros((width, tail), F32)
    source_t[:, edges:] = jnp.zeros((2 * width, tail), LOW)
    hidden_ready()
    (weight_ready,) = fetch([(weight_there, weight, arrived.at[1])])
    (source_left,) = fetch([(source_t, source_out, left.at[0])])

    def window_step(group, at, further):
        row = pl.multiple_of(jnp.minimum(group, groups - 1) * GROUP, GROUP)
        there = target[:, pl.ds(at, WINDOW)]
        mine = (there >> 4) == group
        pairs = mine & ((there & 7) == iota((8, WINDOW), 0))
        right = hidden[:, pl.ds(at, WINDOW)]
        all_rows = one_hot(mine & ((there & 15) == iota((GROUP, WINDOW), 0)))
        part = jnp.dot(all_rows, picked[pl.ds(at, WINDOW), :], preferred_element_type=F32)
        if further:
            part = part + sums[pl.ds(row, GROUP), :]
        sums[pl.ds(row, GROUP), :] = part
        chunk = 32
        for first in range(0, width, chunk):
            left = jnp.concatenate(
                [
                    jnp.where(
                        pairs,
                        jnp.broadcast_to(source_f[pl.ds(first + q, 1), pl.ds(at, WINDOW)], (8, WINDOW)),
                        0.0,
                    )
                    for q in range(chunk)
                ],
                axis=0,
            ).astype(LOW)
            part = contract(left, right, 1, 1).reshape(chunk, 8, 2 * width)
            part = jnp.concatenate([part[:, :, :width], part[:, :, width:]], axis=1)
            if further:
                part = part + product[first : first + chunk, pl.ds(row, GROUP), :].astype(F32)
            product[first : first + chunk, pl.ds(row, GROUP), :] = part.astype(LOW)

    def clear(group, _):
        row = pl.multiple_of(group * GROUP, GROUP)
        product[:, pl.ds(row, GROUP), :] = jnp.zeros((width, GROUP, width), LOW)
        sums[pl.ds(row, GROUP), :] = jnp.zeros((GROUP, width), F32)
        return 0

    lax.fori_loop(steps[0] * UNROLL, groups, clear, 0)
    for_steps(steps, UNROLL, window_step, apart=True)

    sums_low = sums[...].astype(LOW)
    node_sums[...] = jnp.dot(sums_low, bias_matrix[...], preferred_element_type=F32)

    def multiply(block, _):
        several = 32
        lanes = pl.multiple_of(block * several * width, several * width)
        left = jnp.concatenate([product[block * several + q] for q in range(several)], axis=1)
        right = jnp.concatenate(
            [weight[:, pl.ds(lanes + q * width, width)] for q in range(several)], axis=0
        )
        node_sums[...] += jnp.dot(left, right, preferred_element_type=F32)
        return 0

    weight_ready()
    lax.fori_loop(0, width // 32, multiply, 0)
    incoming = node_sums[...].astype(LOW)
    alive = jnp.where(iota((nodes, 1), 0) < node_count[0], 1.0, 0.0)
    gate_in = jnp.dot(incoming, input_weights[...], preferred_element_type=F32)
    gate_in = gate_in + input_bias[...].reshape(1, -1)
    gate_hid = jnp.dot(states[...], state_weights[...], preferred_element_type=F32)
    gate_hid = gate_hid + state_bias[...].reshape(1, -1)
    reset = jax.nn.sigmoid(gate_in[:, :width] + gate_hid[:, :width])
    update = jax.nn.sigmoid(gate_in[:, width : 2 * width] + gate_hid[:, width : 2 * width])
    hid_n = gate_hid[:, 2 * width :]
    candidate = jnp.tanh(gate_in[:, 2 * width :] + reset * hid_n)
    values = states[...].astype(F32)
    new_states[...] = alive * ((1.0 - update) * candidate + update * values)
    upstream = grad_output[...] * alive
    grad_cand = upstream * (1.0 - update) * (1.0 - candidate * candidate)
    grad_update = upstream * (values - candidate) * update * (1.0 - update)
    grad_reset = grad_cand * hid_n * reset * (1.0 - reset)
    grad_gate_in = jnp.concatenate([grad_reset, grad_update, grad_cand], axis=1)
    grad_gate_hid = jnp.concatenate([grad_reset, grad_update, grad_cand * reset], axis=1)
    low_in = grad_gate_in.astype(LOW)
    low_hid = grad_gate_hid.astype(LOW)
    low = contract(low_in, input_weights[...], 1, 1).astype(LOW)
    grad_low[...] = low
    by_bias[...] = contract(low, bias_matrix[...], 1, 1).astype(LOW)
    direct[...] = upstream * update + contract(low_hid, state_weights[...], 1, 1)
    extras[0:width, :] = contract(sums_low, low, 0, 0)
    grad_in_w = contract(incoming, low_in, 0, 0)
    grad_st_w = contract(states[...], low_hid, 0, 0)
    in_b = jnp.sum(grad_gate_in, axis=0, keepdims=True)
    st_b = jnp.sum(grad_gate_hid, axis=0, keepdims=True)
    for block in range(3):
        lanes = slice(block * width, (block + 1) * width)
        extras[(1 + block) * width : (2 + block) * width, :] = grad_in_w[:, lanes]
        extras[(4 + block) * width : (5 + block) * width, :] = grad_st_w[:, lanes]
    extras[7 * width :, :] = jnp.zeros((extras.shape[0] - 7 * width, width), F32)
    for block in range(3):
        lanes = slice(block * width, (block + 1) * width)
        extras[7 * width + block : 7 * width + block + 1, :] = in_b[:, lanes]
        extras[7 * width + 3 + block : 7 * width + 4 + block, :] = st_b[:, lanes]

    half = width // 2
    piece_0 = per_piece * half
    piece_1 = keep_1.shape[0] * 2 // pieces
    extra = piece_1 - piece_0
    at_once = max(1, 32 // per_piece)
    waits = [source_left]
    for side, (out_0, out_1) in ((1, (send_0, send_1)), (0, (keep_0, keep_1))):

        def piece_step(step, _):
            for u in range(at_once):
                place = step * at_once + u
                piece = jnp.bitwise_xor(table[0, side * (pieces // 2) + place], lax.axis_index("graph"))
                other = table[1, side * (pieces // 2) + place]
                row_0 = pl.multiple_of(place * piece_0, 16)
                row_1 = pl.multiple_of(other * piece_1, 16)
                for q in range(per_piece):
                    tile = contract(product[piece * per_piece + q], low, 0, 0).astype(LOW)
                    out_0[pl.ds(row_0 + q * half, half), :] = tile[:half, :]
                    out_1[pl.ds(row_1 + q * half, half), :] = tile[half:, :]
                out_1[pl.ds(row_1 + piece_0, extra), :] = extras[
                    pl.ds(pl.multiple_of(piece * extra, 8), extra), :
                ].astype(LOW)
            return 0

        lax.fori_loop(0, pieces // 2 // at_once, piece_step, 0)
        waits += fetch(
            [(pieces_here[p], pieces_out[p], left.at[1 + p]) for p in (side, side + 2)]
        )
    for wait in waits:
        wait()


def expand(grad_low, weight, weight_here, done, spread):
    nodes, width = grad_low.shape
    pitch = width + 4
    parts = done.shape[0]
    several = width // parts
    lanes = [slice(part * several * width, (part + 1) * several * width) for part in range(parts)]
    ready = fetch([(weight.at[:, lane], weight_here.at[:, lane], done.at[p]) for p, lane in enumerate(lanes)])
    for part in range(parts):
        ready[part]()
        first = part * several
        right = jnp.concatenate(
            [weight_here[:, (first + q) * width : (first + q + 1) * width] for q in range(several)], axis=0
        )
        both = contract(grad_low[...], right, 1, 1)
        for q in range(several):
            spread[pl.ds(first + q, nodes, stride=pitch), :] = both[:, q * width : (q + 1) * width]


def source_kernel(
    steps, target, grad_low, weight, by_bias, hidden_t, out, spread, weight_here, hidden_here, sums, done, arrived
):
    nodes, width = grad_low.shape
    groups = nodes // GROUP
    pitch = width + 4
    (ready,) = fetch([(hidden_t, hidden_here, arrived)])
    sums[...] = jnp.zeros_like(sums)
    expand(grad_low, weight, weight_here, done, spread)
    ready()

    def window_step(group, at, further):
        row = jnp.minimum(group, groups - 1) * GROUP
        there = target[:, pl.ds(at, WINDOW)]
        mine = (there >> 4) == group
        hidden = hidden_here[:, pl.ds(at, WINDOW)]
        found = jnp.where(mine, there & 7, -1)
        nodes_here = one_hot(mine & ((there & 15) == iota((GROUP, WINDOW), 0)))
        rows = by_bias[pl.ds(pl.multiple_of(row, GROUP), GROUP), :]
        total = sums[:, pl.ds(at, WINDOW)] + contract(rows, nodes_here, 0, 0)
        value = None
        for v in range(8):
            pair = [spread[pl.ds((row + v + 8 * h) * pitch, width), :].astype(LOW) for h in range(2)]
            part = jnp.dot(jnp.concatenate(pair, axis=1), hidden, preferred_element_type=F32)
            value = jnp.where(found == v, part, 0.0 if value is None else value)
        sums[:, pl.ds(at, WINDOW)] = total + value

    for_steps(steps, UNROLL, window_step)
    out[...] = sums[...].astype(LOW)


def scatter_kernel(slots, sums, out):
    width = sums.shape[0]
    edges = slots.shape[1]
    lookup = 512
    ways = out.shape[0] // lookup
    total = None
    for start in range(0, edges, 1024):
        rights = []
        for at in range(start, start + 1024, 256):
            rows = sums[:, at : at + 256].astype(F32).T
            way = as_columns(slots, at, 256) >> shift_of(lookup)
            rights.append(
                jnp.concatenate([jnp.where(way == w, rows, 0.0) for w in range(ways)], axis=1).astype(LOW)
            )
        chosen = one_hot((slots[:, start : start + 1024] & (lookup - 1)) == iota((lookup, 1024), 0))
        part = jnp.dot(chosen, jnp.concatenate(rights, axis=0), preferred_element_type=F32)
        total = part if total is None else total + part
    for w in range(ways):
        out[w * lookup : (w + 1) * lookup, :] = total[:, w * width : (w + 1) * width].astype(LOW)


def hidden_kernel(
    steps, target, grad_low, weight, source_t, sums, spread, weight_here, source_here, done, arrived
):
    nodes, width = grad_low.shape
    groups = nodes // GROUP
    pitch = width + 4
    (ready,) = fetch([(source_t, source_here, arrived)])
    sums[...] = jnp.zeros_like(sums)
    expand(grad_low, weight, weight_here, done, spread)
    ready()

    def window_step(group, at, further):
        row = jnp.minimum(group, groups - 1) * GROUP
        there = target[:, pl.ds(at, WINDOW)]
        source = source_here[:, pl.ds(at, WINDOW)]
        found = jnp.where((there >> 4) == group, there & 7, -1)
        value = None
        for v in range(8):
            pair = [spread[pl.ds((row + v + 8 * h) * pitch, width), :].astype(LOW) for h in range(2)]
            part = contract(jnp.concatenate(pair, axis=0), source, 0, 0)
            value = jnp.where(found == v, part, 0.0 if value is None else value)
        sums[:, pl.ds(at, WINDOW)] += value

    for_steps(steps, UNROLL, window_step)


def features_kernel(
    order, hidden_sums, preact_t, sorted_features, weight_in, grad_features, late
):
    width = hidden_sums.shape[0]
    narrow = weight_in.shape[0]
    edges = order.shape[1]
    copies = width // narrow
    table_rows = edges // copies
    tiled = jnp.concatenate([weight_in[...]] * copies, axis=0)
    weight_sum = jnp.zeros((width, width), F32)
    bias_sum = jnp.zeros((width, 1), F32)
    total = jnp.zeros((table_rows, width), F32)
    for start in range(0, edges, 512):
        lanes = slice(start, start + 512)
        grad_preact = hidden_sums[:, lanes] * silu_parts(preact_t[:, lanes])[1]
        low = grad_preact.astype(LOW)
        weight_sum = weight_sum + jnp.dot(low, sorted_features[lanes, :], preferred_element_type=F32)
        bias_sum = bias_sum + jnp.sum(grad_preact, axis=1, keepdims=True)
        rows = jnp.dot(tiled, low, preferred_element_type=F32)
        owner = (order[:, lanes] >> shift_of(table_rows)) == (iota((width, 512), 0) >> shift_of(narrow))
        rows = jnp.where(owner, rows, 0.0)
        chosen = one_hot((order[:, lanes] & (table_rows - 1)) == iota((table_rows, 512), 0))
        total = total + jnp.dot(chosen, rows.T.astype(LOW), preferred_element_type=F32)
    turned = total.T
    for copy in range(copies):
        grad_features[:, copy * table_rows : (copy + 1) * table_rows] = turned[
            copy * narrow : (copy + 1) * narrow, :
        ]
    late[...] = jnp.zeros_like(late)
    turned = weight_sum.T
    late[0:narrow, :] = sum(turned[c * narrow : (c + 1) * narrow, :] for c in range(copies))
    late[narrow : narrow + 1, :] = jnp.broadcast_to(bias_sum, (width, width)).T[0:1, :]


def collect_kernel(index, returned, direct, out):
    rows = index.shape[1]
    for start in range(0, out.shape[0], 256):
        chosen = index[...] == iota((256, rows), 0) + start
        out[start : start + 256, :] = direct[start : start + 256, :] + jnp.dot(
            one_hot(chosen), returned[...], preferred_element_type=F32
        )


def bit_orders(bits):
    rest = list(range(1, bits))
    if bits < 3:
        return ([0] + rest, [0] + rest)
    return ([0] + rest, [0, rest[1], rest[0]] + rest[2:])


def place_tables(devices):
    bits = devices.bit_length() - 1
    tables = []
    for order in bit_orders(bits):
        place = np.arange(devices)
        position = np.zeros(devices, np.int32)
        for level, bit in enumerate(order):
            position |= (((place >> (bits - 1 - level)) & 1) << bit).astype(np.int32)
        tables.append(position)
    return tables


def swap(value, bit, devices):
    pairs = [(i, i ^ (1 << bit)) for i in range(devices)]
    return lax.ppermute(value, "graph", pairs)


def add_low(left, right):
    return (left.astype(F32) + right.astype(F32)).astype(LOW)


def swap_together(values, bit, devices):
    flat = swap(jnp.concatenate(values, axis=0), bit, devices)
    cuts = np.cumsum([value.shape[0] for value in values])[:-1]
    return jnp.split(flat, cuts, axis=0)


def swap_parts(values, orders, level, devices):
    bits = [order[level] for order in orders]
    if len(set(bits)) == 1 and level > 0:
        return swap_together(values, bits[0], devices)
    return [swap(value, bit, devices) for value, bit in zip(values, bits)]


def sum_pieces(keep, send, devices, works, own_work, middle_work):
    bits = devices.bit_length() - 1
    orders = bit_orders(bits)
    parts = range(len(keep))
    works = list(works)

    def beside(sent, values, got):
        if not works:
            return values, got
        done = [work(sent) for work in works.pop(0)]
        values, got, _ = lax.optimization_barrier((values, got, done))
        return values, got

    keep = list(keep)
    got = swap_parts(send, orders, 0, devices)
    for level in range(1, bits - 1):
        halves = [value.shape[0] // 2 for value in keep]
        send = [add_low(keep[p][halves[p] :], got[p][halves[p] :]) for p in parts]
        keep = [add_low(keep[p][: halves[p]], got[p][: halves[p]]) for p in parts]
        got = swap_parts(send, orders, level, devices)
        keep, got = beside(send, keep, got)
    held = [add_low(keep[p], got[p]) for p in parts]
    got = swap_together(held, orders[0][bits - 1], devices)
    held, got = beside(held, held, got)
    sums = []
    for p in parts:
        half = held[p].shape[0] // 2
        turned = jnp.concatenate([got[p][half:], got[p][:half]], axis=0)
        sums.append(add_low(held[p], turned))
    held = sums
    for level in range(bits - 2, 0, -1):
        other = swap_parts(held, orders, level, devices)
        if level == 1:
            far = swap_parts(held, orders, 0, devices)
            works[:1] = [[lambda before, own=held: own_work(own)] + sum(works[:1], [])]
        held, other = beside(held, held, other)
        if level > 1:
            held = [jnp.concatenate([held[p], other[p]], axis=0) for p in parts]
    last = swap_parts(other, orders, 0, devices)
    works[:1] = [[lambda before: middle_work(far, other)] + sum(works[:1], [])]
    while works:
        other, last = beside(other, other, last)
    return last


def assemble(batches, table, done, blocks, whole, extras):
    places = table.shape[1] // 2
    here = lax.axis_index("graph")
    width = extras.shape[1]
    per_piece = whole.shape[1] // width // (4 * places)
    half = width // 2
    copies = []
    for second, far, values in batches:
        sizes = [value.shape[0] // places for value in values]
        extra = sizes[1] - per_piece * half
        for part, value in enumerate(values):
            for place in range(places):
                piece = jnp.bitwise_xor(table[part, second * places + place], here)
                piece = jnp.bitwise_xor(piece, far)
                slot = len(copies)
                row = place * sizes[part]
                for q in range(per_piece):
                    blocks[slot, :, q * width : (q + 1) * width] = value[
                        row + q * half : row + (q + 1) * half, :
                    ].astype(F32)
                if part == 1:
                    extras[pl.ds(pl.multiple_of(piece * extra, 8), extra), :] = value[
                        row + per_piece * half : row + sizes[part], :
                    ].astype(F32)
                lane = pl.multiple_of(piece * (per_piece * width), per_piece * width)
                copy = pltpu.make_async_copy(
                    blocks.at[slot],
                    whole.at[pl.ds(part * half, half), pl.ds(lane, per_piece * width)],
                    done.at[slot],
                )
                copy.start()
                copies.append(copy)
    for copy in copies:
        copy.wait()


def assemble_own_kernel(table, own_0, own_1, whole, extras, blocks, done):
    extras[...] = jnp.zeros_like(extras)
    assemble([(0, 0, (own_0, own_1))], table, done, blocks, whole, extras)


def assemble_middle_kernel(
    table, far_0, far_1, own_0, own_1, extras_in, whole_in, whole, extras, blocks, done
):
    del whole_in
    extras[...] = extras_in[...]
    batches = [(0, 1, (far_0, far_1)), (1, 0, (own_0, own_1))]
    assemble(batches, table, done, blocks, whole, extras)


def assemble_last_kernel(
    table, far_0, far_1, late, late_far, extras_in, whole_in,
    whole, bias_out, input_weights, state_weights, input_bias, state_bias, weight_in, bias_in,
    extras, blocks, done,
):
    del whole_in
    extras[...] = extras_in[...]
    narrow = weight_in.shape[0]
    weight_in[...] = late[:narrow, :] + late_far[:narrow, :]
    bias_in[...] = late[narrow, :] + late_far[narrow, :]
    assemble([(1, 1, (far_0, far_1))], table, done, blocks, whole, extras)
    width = extras.shape[1]
    bias_out[...] = extras[0:width, :]
    for block in range(3):
        lanes = slice(block * width, (block + 1) * width)
        input_weights[:, lanes] = extras[(1 + block) * width : (2 + block) * width, :]
        state_weights[:, lanes] = extras[(4 + block) * width : (5 + block) * width, :]
        input_bias[lanes] = extras[7 * width + block, :]
        state_bias[lanes] = extras[7 * width + 3 + block, :]


def on_device(
    states,
    node_count,
    edge_features,
    edge_count,
    target_rows,
    source_slots,
    send_rows,
    send_count,
    edge_weight_in,
    edge_bias_in,
    edge_weight_out,
    edge_bias_out,
    input_weights,
    state_weights,
    input_bias,
    state_bias,
    grad_output,
):
    nodes, width = states.shape
    edges, narrow = edge_features.shape
    devices = lax.axis_size("graph")
    received_rows = send_rows.shape[1]
    per_peer = received_rows // devices
    groups = nodes // GROUP
    padded = edges + WINDOW
    shape = jax.ShapeDtypeStruct
    bias_matrix = edge_bias_out.reshape(width, width)

    outgoing, index = call(
        pick_kernel,
        (shape((received_rows, width), LOW), shape((1, received_rows), jnp.int32)),
        [VMEM] * 3,
    )(send_rows, send_count, states)
    received = lax.all_to_all(
        outgoing.reshape(devices, per_peer, width), "graph", split_axis=0, concat_axis=0, tiled=True
    ).reshape(received_rows, width)

    assert received_rows == SLOTS
    rows = jnp.arange(edges, dtype=jnp.int32)
    packed = pack_key(target_rows, source_slots, rows, nodes, received_rows, edges)
    packed = lax.sort(jnp.where(rows < edge_count[0], packed, np.iinfo(np.int32).max), is_stable=False)
    limits = pack_key(jnp.arange(groups, dtype=jnp.int32) * GROUP, 0, 0, nodes, received_rows, edges)
    starts = jnp.sum((packed[None, :] < limits[:, None]).astype(jnp.int32), axis=1)
    starts = jnp.concatenate([starts, edge_count])
    step_count = steps_size(groups, edges)
    steps, target, slots, order, hidden_t, preact_t, sorted_features = call(
        first_kernel,
        (
            shape((step_count,), jnp.int32),
            shape((1, padded), jnp.int32),
            shape((1, edges), jnp.int32),
            shape((1, edges), jnp.int32),
            shape((2 * width, padded), LOW),
            shape((width, edges), F32),
            shape((edges, width), LOW),
        ),
        [SMEM] * 3 + [VMEM] * 4,
        [
            pltpu.VMEM((2 * width, padded), LOW),
            pltpu.VMEM((width, edges), F32),
            pltpu.VMEM((edges, width), LOW),
            pltpu.SemaphoreType.DMA((12,)),
        ],
        out_specs=[SMEM] + [VMEM] * 3 + [ANY] * 3,
        micros=6,
    )(
        starts, node_count, edge_count, packed, edge_features.T, edge_weight_in, edge_bias_in
    )

    tables = place_tables(devices)
    inverse = [np.argsort(t).astype(np.int32) for t in tables]
    half = devices // 2
    out_table = jnp.asarray(np.stack([tables[0], inverse[1][tables[0]] % half]))
    extra = max(16, -(-(7 * width + 6) // (devices * 16)) * 16)
    piece_0 = (width // devices) * (width // 2)
    piece_1 = piece_0 + extra
    new_states, direct, grad_low, by_bias, source_t, keep_0, send_0, keep_1, send_1 = call(
        node_kernel,
        (
            shape((nodes, width), F32),
            shape((nodes, width), F32),
            shape((nodes, width), LOW),
            shape((nodes, width), LOW),
            shape((2 * width, padded), LOW),
            shape((half * piece_0, width), LOW),
            shape((half * piece_0, width), LOW),
            shape((half * piece_1, width), LOW),
            shape((half * piece_1, width), LOW),
        ),
        [SMEM] * 3 + [VMEM] * 3 + [ANY] * 2 + [VMEM] * 7,
        [
            pltpu.VMEM((width, nodes, width), LOW),
            pltpu.VMEM((padded, width), LOW),
            pltpu.VMEM((width, padded), F32),
            pltpu.VMEM((devices * extra, width), F32),
            pltpu.VMEM((nodes, width), F32),
            pltpu.VMEM((nodes, width), F32),
            pltpu.VMEM((2 * width, padded), LOW),
            pltpu.VMEM((width, width * width), LOW),
            pltpu.VMEM((2 * width, padded), LOW),
            pltpu.VMEM((half * piece_0, width), LOW),
            pltpu.VMEM((half * piece_0, width), LOW),
            pltpu.VMEM((half * piece_1, width), LOW),
            pltpu.VMEM((half * piece_1, width), LOW),
            pltpu.SemaphoreType.DMA((2,)),
            pltpu.SemaphoreType.DMA((5,)),
        ],
        out_specs=[VMEM] * 4 + [ANY] * 5,
        micros=24,
    )(
        steps, out_table, node_count, target, slots, received, hidden_t, edge_weight_out,
        bias_matrix, states, input_weights, state_weights, input_bias, state_bias, grad_output,
    )

    late_rows = 32
    scratch = [
        pltpu.VMEM((nodes * (width + 4) + 16, width), F32),
        pltpu.VMEM((width, width * width), LOW),
        pltpu.VMEM((2 * width, padded), LOW),
    ]
    signals = [pltpu.SemaphoreType.DMA((8,)), pltpu.SemaphoreType.DMA]
    edge_array = shape((width, padded), F32)
    kept = {}

    def tie(value, before):
        return lax.optimization_barrier((value, before))[0]

    def source_work(before):
        kept["source"] = call(
            source_kernel,
            shape((width, padded), LOW),
            [SMEM] + [VMEM] * 2 + [ANY, VMEM, ANY],
            scratch + [pltpu.VMEM((width, padded), F32)] + signals,
            micros=15,
        )(steps, target, tie(grad_low, before), edge_weight_out, by_bias, hidden_t)
        return kept["source"]

    def scatter_work(before):
        kept["slots"] = call(
            scatter_kernel, shape((received_rows, width), LOW), [VMEM] * 2, micros=4, limit=24
        )(slots, tie(kept["source"], before))
        return kept["slots"]

    def hidden_work(before):
        kept["hidden"] = call(
            hidden_kernel,
            edge_array,
            [SMEM] + [VMEM] * 2 + [ANY, ANY],
            scratch + signals,
            micros=12,
        )(steps, target, tie(grad_low, before), edge_weight_out, source_t)
        return kept["hidden"]

    def send_back(before):
        before = kept["late"]
        kept["returned"] = lax.all_to_all(
            tie(kept["slots"], before).reshape(devices, per_peer, width),
            "graph",
            split_axis=0,
            concat_axis=0,
            tiled=True,
        ).reshape(received_rows, width)
        return kept["returned"]

    def features_work(before):
        kept["features"], kept["late"] = call(
            features_kernel,
            (shape((narrow, edges), F32), shape((late_rows, width), F32)),
            [VMEM] * 5,
            micros=6,
            limit=20,
        )(order, tie(kept["hidden"], before), preact_t, sorted_features, edge_weight_in)
        return kept["features"]

    def add_late(bit):
        def work(before):
            late = tie(kept["late"], before)
            kept["late"] = late + swap(late, bit, devices)
            return kept["late"]

        return work

    def last_late(bit):
        def work(before):
            kept["late far"] = swap(tie(kept["late"], before), bit, devices)
            return kept["late far"]

        return work

    def add_late_soon(bit):
        def work(before):
            kept["late"] = kept["late"] + swap(kept["late"], bit, devices)
            return kept["late"]

        return work

    def collect(before):
        kept["states"] = call(collect_kernel, shape((nodes, width), F32), [VMEM] * 3)(
            index, kept["returned"], tie(direct, before)
        )
        return kept["states"]

    table = jnp.asarray(np.stack([t[: devices // 2] for t in tables]))
    per_piece = width // devices
    extras_array = shape((devices * extra, width), F32)
    whole_array = shape((width, width * width), F32)

    def blocks(quarters):
        count = quarters * devices // 2
        return [
            pltpu.VMEM((count, width // 2, per_piece * width), F32),
            pltpu.SemaphoreType.DMA((count,)),
        ]

    def assemble_own(own):
        kept["whole"] = call(
            assemble_own_kernel,
            (whole_array, extras_array),
            [SMEM] + [VMEM] * 2,
            blocks(1),
            out_specs=[ANY, VMEM],
            micros=3,
            limit=24,
        )(table, *own)
        return kept["whole"]

    def assemble_middle(far, own):
        whole, extras = kept["whole"]
        kept["whole"] = call(
            assemble_middle_kernel,
            (whole_array, extras_array),
            [SMEM] + [VMEM] * 5 + [ANY],
            blocks(2),
            out_specs=[ANY, VMEM],
            micros=4,
            limit=24,
            aliases={6: 0},
        )(table, *far, *own, extras, whole)
        return kept["whole"]

    last = sum_pieces(
        (keep_0, keep_1),
        (send_0, send_1),
        devices,
        [[source_work], [], [scatter_work], [hidden_work], [features_work], [add_late(0)], [send_back, add_late(4), add_late_soon(3)], [add_late(2), last_late(1), collect]],
        assemble_own,
        assemble_middle,
    )
    whole, extras = kept["whole"]
    whole, grad_bias_out, grad_in_w, grad_st_w, grad_in_b, grad_st_b, grad_w_in, grad_b_in = call(
        assemble_last_kernel,
        (
            whole_array,
            shape((width, width), F32),
            shape((width, 3 * width), F32),
            shape((width, 3 * width), F32),
            shape((3 * width,), F32),
            shape((3 * width,), F32),
            shape((narrow, width), F32),
            shape((width,), F32),
        ),
        [SMEM] + [VMEM] * 5 + [ANY],
        [pltpu.VMEM((devices * extra, width), F32)] + blocks(1),
        out_specs=[ANY] + [VMEM] * 7,
        micros=4,
        limit=24,
        aliases={6: 0},
    )(table, *last, kept["late"], kept["late far"], extras, whole)
    return (
        new_states,
        kept["states"],
        kept["features"].T,
        grad_w_in,
        grad_b_in,
        whole,
        grad_bias_out.reshape(width * width),
        grad_in_w,
        grad_st_w,
        grad_in_b,
        grad_st_b,
    )


def solution(mesh):
    in_specs = (
        P("graph", None),
        P("graph"),
        P("graph", None),
        P("graph"),
        P("graph"),
        P("graph"),
        P("graph", None),
        P("graph", None),
        P(),
        P(),
        P(),
        P(),
        P(),
        P(),
        P(),
        P(),
        P("graph", None),
    )
    out_specs = (
        P("graph", None),
        P("graph", None),
        P("graph", None),
        P(),
        P(),
        P(),
        P(),
        P(),
        P(),
        P(),
        P(),
    )
    return jax.shard_map(
        on_device, mesh=mesh, in_specs=in_specs, out_specs=out_specs, check_vma=False
    )
```

```python
import jax
import jax.numpy as jnp
import numpy as np
from jax import lax
from jax.experimental import pallas as pl
from jax.experimental.pallas import tpu as pltpu
from jax.sharding import PartitionSpec as P

F32 = jnp.float32
LOW = jnp.bfloat16
WINDOW = 256
GROUP = 16
UNROLL = 4
SLOTS = 2048
VMEM = pl.BlockSpec(memory_space=pltpu.VMEM)
SMEM = pl.BlockSpec(memory_space=pltpu.SMEM)

ANY = pl.BlockSpec(memory_space=pl.ANY)


def contract(left, right, left_dim, right_dim):
    return lax.dot_general(
        left, right, (((left_dim,), (right_dim,)), ((), ())), preferred_element_type=F32
    )


def iota(shape, dim):
    return lax.broadcasted_iota(jnp.int32, shape, dim)


def shift_of(size):
    return size.bit_length() - 1


def one_hot(mask):
    return jnp.where(mask, 1.0, 0.0).astype(LOW)


def call(kernel, out_shape, in_specs, scratch=(), out_specs=None, micros=2, limit=60, aliases=None):
    single = not isinstance(out_shape, (tuple, list))
    if out_specs is None:
        out_specs = VMEM if single else [VMEM] * len(out_shape)
    return pl.pallas_call(
        kernel,
        out_shape=out_shape,
        in_specs=in_specs,
        out_specs=out_specs,
        scratch_shapes=scratch,
        input_output_aliases=aliases or {},
        compiler_params=pltpu.CompilerParams(vmem_limit_bytes=limit * 2**20),
        cost_estimate=pl.CostEstimate(
            flops=micros * 10**9, bytes_accessed=2**20, transcendentals=0
        ),
    )


def fetch(copies):
    started = [pltpu.make_async_copy(*copy) for copy in copies]
    for copy in started:
        copy.start()
    return [copy.wait for copy in started]


def as_columns(row, start, size):
    return jnp.broadcast_to(row[:, start : start + size], (128, size)).T


def pick_kernel(rows, count, states, out, index):
    nodes = states.shape[0]
    devices = count.shape[1]
    slots = rows.shape[1]
    per_peer = slots // devices
    counts = jnp.broadcast_to(count[...].astype(F32), (8, devices)).astype(LOW)
    owner = one_hot((iota((devices, slots), 1) >> shift_of(per_peer)) == iota((devices, slots), 0))
    live = jnp.dot(counts, owner, preferred_element_type=F32)[0:1, :].astype(jnp.int32)
    index[...] = jnp.where((iota((1, slots), 1) & (per_peer - 1)) < live, rows[...], -1)
    for start in range(0, slots, 256):
        column = as_columns(index, start, 256)
        chosen = jnp.concatenate(
            [one_hot(column == iota((256, 128), 1) + lane) for lane in range(0, nodes, 128)], axis=1
        )
        out[start : start + 256, :] = jnp.dot(
            chosen, states[...], preferred_element_type=F32
        ).astype(LOW)


def silu_parts(preact):
    gate = jax.nn.sigmoid(preact)
    return preact * gate, gate * (1.0 + preact * (1.0 - gate))


def upper_half(target):
    return ((target >> 3) & 1).astype(F32)


def steps_size(groups, edges):
    return 2 + 2 * (groups + edges // 128 + UNROLL)


def plan_steps(starts, node_count, steps, groups):
    alive = (node_count[0] + (GROUP - 1)) // GROUP

    def base_of(group):
        return (starts[group] // 128) * 128

    def first_step(group, _):
        steps[2 + 2 * group] = group
        steps[3 + 2 * group] = base_of(group)
        return 0

    def further_step(group, at):
        first, last = starts[group], starts[group + 1]
        base = base_of(group)
        count = jnp.where(last > first, (last - base + (WINDOW - 1)) // WINDOW, 0)

        def more(step, at):
            steps[at] = group
            steps[at + 1] = base + WINDOW * step
            return at + 2

        return lax.fori_loop(1, count, more, at)

    lax.fori_loop(0, alive, first_step, 0)
    at = lax.fori_loop(0, alive, further_step, 2 + 2 * alive)
    steps[0] = alive // UNROLL
    steps[1] = (at // 2 - 1 + (UNROLL - 1)) // UNROLL - alive // UNROLL
    for spare in range(UNROLL):
        steps[at + 2 * spare] = groups + 1
        steps[at + 1 + 2 * spare] = 0


def key_bits(nodes, slots, edges):
    low, high = shift_of(edges), shift_of(edges) + shift_of(slots)
    assert high + shift_of(nodes) <= 32
    return low, high, 1 << (31 - high)


def pack_key(target, slot, row, nodes, slots, edges):
    low, high, offset = key_bits(nodes, slots, edges)
    return ((target - offset) << high) | (slot << low) | row


def unpack_key(key, nodes, edges):
    low, high, offset = key_bits(nodes, SLOTS, edges)
    return (key >> high) + offset, (key >> low) & (SLOTS - 1), key & (edges - 1)


def first_kernel(
    starts, node_count, edge_count, packed, features, weight, bias,
    steps, target, slots, order, hidden_out, preact_out, sorted_out, hidden_t, preact_t, sorted_features, left,
):
    edges = order.shape[1]
    nodes = (starts.shape[0] - 1) * GROUP
    key = packed[...].reshape(1, edges)
    here, slot, row = unpack_key(key, nodes, edges)
    target[:, :edges] = jnp.where(iota((1, edges), 1) < edge_count[0], here, nodes)
    target[:, edges:] = jnp.full((1, target.shape[1] - edges), nodes, jnp.int32)
    slots[...] = slot
    order[...] = row
    narrow = weight.shape[0]
    spread = 128 // narrow
    table_rows = edges // spread
    plan_steps(starts, node_count, steps, starts.shape[0] - 1)
    tiled = jnp.concatenate([weight[...]] * spread, axis=0)
    table = jnp.concatenate(
        [features[:, c * table_rows : (c + 1) * table_rows] for c in range(spread)], axis=0
    )
    table = table.astype(F32).T.astype(LOW)
    lane_part = iota((256, 128), 1) >> shift_of(narrow)
    bias_column = as_columns(bias[...].reshape(1, 128), 0, 128)
    bias_columns = jnp.concatenate([bias_column] * 2, axis=1)
    hidden_t[:, edges:] = jnp.zeros((256, hidden_t.shape[1] - edges), LOW)
    waits = []
    for start in range(0, edges, 256):
        column = as_columns(order, start, 256)
        low = column & (table_rows - 1)
        chosen = jnp.concatenate(
            [one_hot(low == iota((256, 128), 1) + lane) for lane in range(0, table_rows, 128)], axis=1
        )
        got = jnp.dot(chosen, table, preferred_element_type=F32)
        part = jnp.where((column >> shift_of(table_rows)) == lane_part, got, 0.0).astype(LOW)
        sorted_features[start : start + 256, :] = part
        preact = contract(tiled, part, 0, 1) + bias_columns
        preact_t[:, start : start + 256] = preact
        value = silu_parts(preact)[0]
        upper = upper_half(target[:, start : start + 256])
        hidden_t[0:128, start : start + 256] = (value * (1.0 - upper)).astype(LOW)
        hidden_t[128:256, start : start + 256] = (value * upper).astype(LOW)
        quarter = edges // 4
        if (start + 256) % quarter == 0:
            part = start // quarter
            lanes = slice(part * quarter, (part + 1) * quarter)
            wide = lanes if part < 3 else slice(part * quarter, hidden_t.shape[1])
            waits += fetch(
                [
                    (hidden_t.at[:, wide], hidden_out.at[:, wide], left.at[part]),
                    (preact_t.at[:, lanes], preact_out.at[:, lanes], left.at[4 + part]),
                    (sorted_features.at[lanes, :], sorted_out.at[lanes, :], left.at[8 + part]),
                ]
            )
    for wait in waits:
        wait()


def for_steps(steps, body, apart=False):
    def run(count, first, further, together=UNROLL):
        def several(i, _):
            for u in range(together):
                at = first + 2 * (together * i + u)
                body(steps[at], pl.multiple_of(steps[at + 1], 128), further)
            return 0

        lax.fori_loop(0, UNROLL // together * count, several, 0)

    if not apart:
        run(steps[0] + steps[1], 2, None)
        return
    run(steps[0], 2, False)
    run(steps[1], 2 + 2 * UNROLL * steps[0], True, UNROLL // 2)


def node_kernel(
    steps, table, node_count, target, slots, received, hidden_there, weight_there, bias_matrix, states,
    input_weights, state_weights, input_bias, state_bias, grad_output,
    new_states, direct, grad_low, by_bias, source_out, *rest,
):
    pieces_out, rest = rest[:4], rest[4:]
    product, picked, source_f, extras, sums, node_sums, hidden, weight, source_t, *rest = rest
    pieces_here, (arrived, left) = rest[:4], rest[4:]
    keep_0, send_0, keep_1, send_1 = pieces_here
    (hidden_ready,) = fetch([(hidden_there, hidden, arrived.at[0])])
    edges = slots.shape[1]
    lookup = 512
    ways = received.shape[0] // lookup
    nodes, width = states.shape
    groups = nodes // GROUP
    pieces = table.shape[1]
    per_piece = width // pieces
    several = jnp.concatenate([received[w * lookup : (w + 1) * lookup, :] for w in range(ways)], axis=1)
    for start in range(0, edges, 256):
        column = as_columns(slots, start, 256)
        chosen = jnp.concatenate(
            [
                one_hot((column & (lookup - 1)) == iota((256, 128), 1) + lane)
                for lane in range(0, lookup, 128)
            ],
            axis=1,
        )
        got = jnp.dot(chosen, several, preferred_element_type=F32)
        way = column >> shift_of(lookup)
        value = got[:, :width]
        for w in range(1, ways):
            value = jnp.where(way == w, got[:, w * width : (w + 1) * width], value)
        picked[start : start + 256, :] = value.astype(LOW)
        turned = value.T
        source_f[:, start : start + 256] = turned
        upper = upper_half(target[:, start : start + 256])
        source_t[0:width, start : start + 256] = (turned * (1.0 - upper)).astype(LOW)
        source_t[width:, start : start + 256] = (turned * upper).astype(LOW)
    tail = picked.shape[0] - edges
    picked[edges:, :] = jnp.zeros((tail, width), LOW)
    source_f[:, edges:] = jnp.zeros((width, tail), F32)
    source_t[:, edges:] = jnp.zeros((2 * width, tail), LOW)
    hidden_ready()
    (weight_ready,) = fetch([(weight_there, weight, arrived.at[1])])
    (source_left,) = fetch([(source_t, source_out, left.at[0])])

    def window_step(group, at, further):
        row = pl.multiple_of(jnp.minimum(group, groups - 1) * GROUP, GROUP)
        there = target[:, pl.ds(at, WINDOW)]
        mine = (there >> 4) == group
        pairs = mine & ((there & 7) == iota((8, WINDOW), 0))
        right = hidden[:, pl.ds(at, WINDOW)]
        all_rows = one_hot(mine & ((there & 15) == iota((GROUP, WINDOW), 0)))
        part = jnp.dot(all_rows, picked[pl.ds(at, WINDOW), :], preferred_element_type=F32)
        if further:
            part = part + sums[pl.ds(row, GROUP), :]
        sums[pl.ds(row, GROUP), :] = part
        chunk = 32
        for first in range(0, width, chunk):
            left = jnp.concatenate(
                [
                    jnp.where(
                        pairs,
                        jnp.broadcast_to(source_f[pl.ds(first + q, 1), pl.ds(at, WINDOW)], (8, WINDOW)),
                        0.0,
                    )
                    for q in range(chunk)
                ],
                axis=0,
            ).astype(LOW)
            part = contract(left, right, 1, 1).reshape(chunk, 8, 2 * width)
            part = jnp.concatenate([part[:, :, :width], part[:, :, width:]], axis=1)
            if further:
                part = part + product[first : first + chunk, pl.ds(row, GROUP), :].astype(F32)
            product[first : first + chunk, pl.ds(row, GROUP), :] = part.astype(LOW)

    def clear(group, _):
        row = pl.multiple_of(group * GROUP, GROUP)
        product[:, pl.ds(row, GROUP), :] = jnp.zeros((width, GROUP, width), LOW)
        sums[pl.ds(row, GROUP), :] = jnp.zeros((GROUP, width), F32)
        return 0

    lax.fori_loop(steps[0] * UNROLL, groups, clear, 0)
    for_steps(steps, window_step, apart=True)

    sums_low = sums[...].astype(LOW)
    node_sums[...] = jnp.dot(sums_low, bias_matrix[...], preferred_element_type=F32)

    def multiply(block, _):
        several = 32
        lanes = pl.multiple_of(block * several * width, several * width)
        left = jnp.concatenate([product[block * several + q] for q in range(several)], axis=1)
        right = jnp.concatenate(
            [weight[:, pl.ds(lanes + q * width, width)] for q in range(several)], axis=0
        )
        node_sums[...] += jnp.dot(left, right, preferred_element_type=F32)
        return 0

    weight_ready()
    lax.fori_loop(0, width // 32, multiply, 0)
    incoming = node_sums[...].astype(LOW)
    alive = jnp.where(iota((nodes, 1), 0) < node_count[0], 1.0, 0.0)
    gate_in = jnp.dot(incoming, input_weights[...], preferred_element_type=F32)
    gate_in = gate_in + input_bias[...].reshape(1, -1)
    gate_hid = jnp.dot(states[...], state_weights[...], preferred_element_type=F32)
    gate_hid = gate_hid + state_bias[...].reshape(1, -1)
    reset = jax.nn.sigmoid(gate_in[:, :width] + gate_hid[:, :width])
    update = jax.nn.sigmoid(gate_in[:, width : 2 * width] + gate_hid[:, width : 2 * width])
    hid_n = gate_hid[:, 2 * width :]
    candidate = jnp.tanh(gate_in[:, 2 * width :] + reset * hid_n)
    values = states[...].astype(F32)
    new_states[...] = alive * ((1.0 - update) * candidate + update * values)
    upstream = grad_output[...] * alive
    grad_cand = upstream * (1.0 - update) * (1.0 - candidate * candidate)
    grad_update = upstream * (values - candidate) * update * (1.0 - update)
    grad_reset = grad_cand * hid_n * reset * (1.0 - reset)
    grad_gate_in = jnp.concatenate([grad_reset, grad_update, grad_cand], axis=1)
    grad_gate_hid = jnp.concatenate([grad_reset, grad_update, grad_cand * reset], axis=1)
    low_in = grad_gate_in.astype(LOW)
    low_hid = grad_gate_hid.astype(LOW)
    low = contract(low_in, input_weights[...], 1, 1).astype(LOW)
    grad_low[...] = low
    by_bias[...] = contract(low, bias_matrix[...], 1, 1).astype(LOW)
    direct[...] = upstream * update + contract(low_hid, state_weights[...], 1, 1)
    extras[0:width, :] = contract(sums_low, low, 0, 0)
    grad_in_w = contract(incoming, low_in, 0, 0)
    grad_st_w = contract(states[...], low_hid, 0, 0)
    in_b = jnp.sum(grad_gate_in, axis=0, keepdims=True)
    st_b = jnp.sum(grad_gate_hid, axis=0, keepdims=True)
    for block in range(3):
        lanes = slice(block * width, (block + 1) * width)
        extras[(1 + block) * width : (2 + block) * width, :] = grad_in_w[:, lanes]
        extras[(4 + block) * width : (5 + block) * width, :] = grad_st_w[:, lanes]
    extras[7 * width :, :] = jnp.zeros((extras.shape[0] - 7 * width, width), F32)
    for block in range(3):
        lanes = slice(block * width, (block + 1) * width)
        extras[7 * width + block : 7 * width + block + 1, :] = in_b[:, lanes]
        extras[7 * width + 3 + block : 7 * width + 4 + block, :] = st_b[:, lanes]

    half = width // 2
    piece_0 = per_piece * half
    piece_1 = keep_1.shape[0] * 2 // pieces
    extra = piece_1 - piece_0
    at_once = max(1, 32 // per_piece)
    waits = [source_left]
    for side, (out_0, out_1) in ((1, (send_0, send_1)), (0, (keep_0, keep_1))):

        def piece_step(step, _):
            for u in range(at_once):
                place = step * at_once + u
                piece = jnp.bitwise_xor(table[0, side * (pieces // 2) + place], lax.axis_index("graph"))
                other = table[1, side * (pieces // 2) + place]
                row_0 = pl.multiple_of(place * piece_0, 16)
                row_1 = pl.multiple_of(other * piece_1, 16)
                for q in range(per_piece):
                    tile = contract(product[piece * per_piece + q], low, 0, 0).astype(LOW)
                    out_0[pl.ds(row_0 + q * half, half), :] = tile[:half, :]
                    out_1[pl.ds(row_1 + q * half, half), :] = tile[half:, :]
                out_1[pl.ds(row_1 + piece_0, extra), :] = extras[
                    pl.ds(pl.multiple_of(piece * extra, 8), extra), :
                ].astype(LOW)
            return 0

        lax.fori_loop(0, pieces // 2 // at_once, piece_step, 0)
        waits += fetch(
            [(pieces_here[p], pieces_out[p], left.at[1 + p]) for p in (side, side + 2)]
        )
    for wait in waits:
        wait()


def expand(grad_low, weight, weight_here, done, spread):
    nodes, width = grad_low.shape
    pitch = width + 4
    parts = done.shape[0]
    several = width // parts

    def arrival(part):
        lanes = pl.ds(pl.multiple_of(part * several * width, several * width), several * width)
        return pltpu.make_async_copy(weight.at[:, lanes], weight_here.at[:, lanes], done.at[part])

    for part in range(parts):
        arrival(part).start()

    def block_step(part, _):
        arrival(part).wait()
        first = part * several
        right = jnp.concatenate(
            [
                weight_here[:, pl.ds(pl.multiple_of((first + q) * width, width), width)]
                for q in range(several)
            ],
            axis=0,
        )
        both = contract(grad_low[...], right, 1, 1)
        for q in range(several):
            spread[pl.ds(first + q, nodes, stride=pitch), :] = both[:, q * width : (q + 1) * width]
        return 0

    lax.fori_loop(0, parts, block_step, 0)


def source_kernel(
    steps, target, grad_low, weight, by_bias, hidden_t, out, spread, weight_here, hidden_here, sums, done, arrived
):
    nodes, width = grad_low.shape
    groups = nodes // GROUP
    pitch = width + 4
    (ready,) = fetch([(hidden_t, hidden_here, arrived)])
    sums[...] = jnp.zeros_like(sums)
    expand(grad_low, weight, weight_here, done, spread)
    ready()

    def window_step(group, at, further):
        row = jnp.minimum(group, groups - 1) * GROUP
        there = target[:, pl.ds(at, WINDOW)]
        mine = (there >> 4) == group
        hidden = hidden_here[:, pl.ds(at, WINDOW)]
        found = jnp.where(mine, there & 7, -1)
        nodes_here = one_hot(mine & ((there & 15) == iota((GROUP, WINDOW), 0)))
        rows = by_bias[pl.ds(pl.multiple_of(row, GROUP), GROUP), :]
        total = sums[:, pl.ds(at, WINDOW)] + contract(rows, nodes_here, 0, 0)
        value = None
        for v in range(8):
            pair = [spread[pl.ds((row + v + 8 * h) * pitch, width), :].astype(LOW) for h in range(2)]
            part = jnp.dot(jnp.concatenate(pair, axis=1), hidden, preferred_element_type=F32)
            value = jnp.where(found == v, part, 0.0 if value is None else value)
        sums[:, pl.ds(at, WINDOW)] = total + value

    for_steps(steps, window_step)
    out[...] = sums[...].astype(LOW)


def scatter_kernel(slots, sums, out):
    width = sums.shape[0]
    edges = slots.shape[1]
    lookup = 512
    ways = out.shape[0] // lookup
    total = None
    for start in range(0, edges, 1024):
        rights = []
        for at in range(start, start + 1024, 256):
            rows = sums[:, at : at + 256].astype(F32).T
            way = as_columns(slots, at, 256) >> shift_of(lookup)
            rights.append(
                jnp.concatenate([jnp.where(way == w, rows, 0.0) for w in range(ways)], axis=1).astype(LOW)
            )
        chosen = one_hot((slots[:, start : start + 1024] & (lookup - 1)) == iota((lookup, 1024), 0))
        part = jnp.dot(chosen, jnp.concatenate(rights, axis=0), preferred_element_type=F32)
        total = part if total is None else total + part
    for w in range(ways):
        out[w * lookup : (w + 1) * lookup, :] = total[:, w * width : (w + 1) * width].astype(LOW)


def hidden_kernel(
    steps, target, grad_low, weight, source_t, sums, spread, weight_here, source_here, done, arrived
):
    nodes, width = grad_low.shape
    groups = nodes // GROUP
    pitch = width + 4
    (ready,) = fetch([(source_t, source_here, arrived)])
    sums[...] = jnp.zeros_like(sums)
    expand(grad_low, weight, weight_here, done, spread)
    ready()

    def window_step(group, at, further):
        row = jnp.minimum(group, groups - 1) * GROUP
        there = target[:, pl.ds(at, WINDOW)]
        source = source_here[:, pl.ds(at, WINDOW)]
        found = jnp.where((there >> 4) == group, there & 7, -1)
        value = None
        for v in range(8):
            pair = [spread[pl.ds((row + v + 8 * h) * pitch, width), :].astype(LOW) for h in range(2)]
            part = contract(jnp.concatenate(pair, axis=0), source, 0, 0)
            value = jnp.where(found == v, part, 0.0 if value is None else value)
        sums[:, pl.ds(at, WINDOW)] += value

    for_steps(steps, window_step)


def features_kernel(
    order, hidden_sums, preact_t, sorted_features, weight_in, grad_features, late
):
    width = hidden_sums.shape[0]
    narrow = weight_in.shape[0]
    edges = order.shape[1]
    copies = width // narrow
    table_rows = edges // copies
    tiled = jnp.concatenate([weight_in[...]] * copies, axis=0)
    weight_sum = jnp.zeros((width, width), F32)
    bias_sum = jnp.zeros((width, 1), F32)
    total = jnp.zeros((table_rows, width), F32)
    for start in range(0, edges, 512):
        lanes = slice(start, start + 512)
        grad_preact = hidden_sums[:, lanes] * silu_parts(preact_t[:, lanes])[1]
        low = grad_preact.astype(LOW)
        weight_sum = weight_sum + jnp.dot(low, sorted_features[lanes, :], preferred_element_type=F32)
        bias_sum = bias_sum + jnp.sum(grad_preact, axis=1, keepdims=True)
        rows = jnp.dot(tiled, low, preferred_element_type=F32)
        owner = (order[:, lanes] >> shift_of(table_rows)) == (iota((width, 512), 0) >> shift_of(narrow))
        rows = jnp.where(owner, rows, 0.0)
        chosen = one_hot((order[:, lanes] & (table_rows - 1)) == iota((table_rows, 512), 0))
        total = total + jnp.dot(chosen, rows.T.astype(LOW), preferred_element_type=F32)
    turned = total.T
    for copy in range(copies):
        grad_features[:, copy * table_rows : (copy + 1) * table_rows] = turned[
            copy * narrow : (copy + 1) * narrow, :
        ]
    late[...] = jnp.zeros_like(late)
    turned = weight_sum.T
    late[0:narrow, :] = sum(turned[c * narrow : (c + 1) * narrow, :] for c in range(copies))
    late[narrow : narrow + 1, :] = jnp.broadcast_to(bias_sum, (width, width)).T[0:1, :]


def collect_kernel(index, returned, direct, out):
    rows = index.shape[1]
    for start in range(0, out.shape[0], 256):
        chosen = index[...] == iota((256, rows), 0) + start
        out[start : start + 256, :] = direct[start : start + 256, :] + jnp.dot(
            one_hot(chosen), returned[...], preferred_element_type=F32
        )


def bit_orders(bits):
    rest = list(range(1, bits))
    if bits < 3:
        return ([0] + rest, [0] + rest)
    return ([0] + rest, [0, rest[1], rest[0]] + rest[2:])


def place_tables(devices):
    bits = devices.bit_length() - 1
    tables = []
    for order in bit_orders(bits):
        place = np.arange(devices)
        position = np.zeros(devices, np.int32)
        for level, bit in enumerate(order):
            position |= (((place >> (bits - 1 - level)) & 1) << bit).astype(np.int32)
        tables.append(position)
    return tables


def swap(value, bit, devices):
    pairs = [(i, i ^ (1 << bit)) for i in range(devices)]
    return lax.ppermute(value, "graph", pairs)


def add_low(left, right):
    return (left.astype(F32) + right.astype(F32)).astype(LOW)


def swap_together(values, bit, devices):
    flat = swap(jnp.concatenate(values, axis=0), bit, devices)
    cuts = np.cumsum([value.shape[0] for value in values])[:-1]
    return jnp.split(flat, cuts, axis=0)


def swap_parts(values, orders, level, devices):
    bits = [order[level] for order in orders]
    if len(set(bits)) == 1 and level > 0:
        return swap_together(values, bits[0], devices)
    return [swap(value, bit, devices) for value, bit in zip(values, bits)]


def sum_pieces(keep, send, devices, works, own_work, middle_work):
    bits = devices.bit_length() - 1
    orders = bit_orders(bits)
    parts = range(len(keep))
    works = list(works)

    def beside(sent, values, got):
        if not works:
            return values, got
        done = [work(sent) for work in works.pop(0)]
        values, got, _ = lax.optimization_barrier((values, got, done))
        return values, got

    keep = list(keep)
    got = swap_parts(send, orders, 0, devices)
    for level in range(1, bits - 1):
        halves = [value.shape[0] // 2 for value in keep]
        send = [add_low(keep[p][halves[p] :], got[p][halves[p] :]) for p in parts]
        keep = [add_low(keep[p][: halves[p]], got[p][: halves[p]]) for p in parts]
        got = swap_parts(send, orders, level, devices)
        keep, got = beside(send, keep, got)
    held = [add_low(keep[p], got[p]) for p in parts]
    got = swap_together(held, orders[0][bits - 1], devices)
    held, got = beside(held, held, got)
    sums = []
    for p in parts:
        half = held[p].shape[0] // 2
        turned = jnp.concatenate([got[p][half:], got[p][:half]], axis=0)
        sums.append(add_low(held[p], turned))
    held = sums
    for level in range(bits - 2, 0, -1):
        other = swap_parts(held, orders, level, devices)
        if level == 1:
            far = swap_parts(held, orders, 0, devices)
            works[:1] = [[lambda before, own=held: own_work(own)] + sum(works[:1], [])]
        held, other = beside(held, held, other)
        if level > 1:
            held = [jnp.concatenate([held[p], other[p]], axis=0) for p in parts]
    last = swap_parts(other, orders, 0, devices)
    works[:1] = [[lambda before: middle_work(far, other)] + sum(works[:1], [])]
    while works:
        other, last = beside(other, other, last)
    return last


def assemble(batches, table, done, blocks, whole, extras):
    places = table.shape[1] // 2
    here = lax.axis_index("graph")
    width = extras.shape[1]
    per_piece = whole.shape[1] // width // (4 * places)
    half = width // 2
    copies = []
    for second, far, values in batches:
        sizes = [value.shape[0] // places for value in values]
        extra = sizes[1] - per_piece * half
        for part, value in enumerate(values):
            for place in range(places):
                piece = jnp.bitwise_xor(table[part, second * places + place], here)
                piece = jnp.bitwise_xor(piece, far)
                slot = len(copies)
                row = place * sizes[part]
                for q in range(per_piece):
                    blocks[slot, :, q * width : (q + 1) * width] = value[
                        row + q * half : row + (q + 1) * half, :
                    ].astype(F32)
                if part == 1:
                    extras[pl.ds(pl.multiple_of(piece * extra, 8), extra), :] = value[
                        row + per_piece * half : row + sizes[part], :
                    ].astype(F32)
                lane = pl.multiple_of(piece * (per_piece * width), per_piece * width)
                copy = pltpu.make_async_copy(
                    blocks.at[slot],
                    whole.at[pl.ds(part * half, half), pl.ds(lane, per_piece * width)],
                    done.at[slot],
                )
                copy.start()
                copies.append(copy)
    for copy in copies:
        copy.wait()


def assemble_own_kernel(table, own_0, own_1, whole, extras, blocks, done):
    extras[...] = jnp.zeros_like(extras)
    assemble([(0, 0, (own_0, own_1))], table, done, blocks, whole, extras)


def assemble_middle_kernel(
    table, far_0, far_1, own_0, own_1, extras_in, whole_in, whole, extras, blocks, done
):
    del whole_in
    extras[...] = extras_in[...]
    batches = [(0, 1, (far_0, far_1)), (1, 0, (own_0, own_1))]
    assemble(batches, table, done, blocks, whole, extras)


def assemble_last_kernel(
    table, far_0, far_1, late, late_far, extras_in, whole_in,
    whole, bias_out, input_weights, state_weights, input_bias, state_bias, weight_in, bias_in,
    extras, blocks, done,
):
    del whole_in
    extras[...] = extras_in[...]
    narrow = weight_in.shape[0]
    weight_in[...] = late[:narrow, :] + late_far[:narrow, :]
    bias_in[...] = late[narrow, :] + late_far[narrow, :]
    assemble([(1, 1, (far_0, far_1))], table, done, blocks, whole, extras)
    width = extras.shape[1]
    bias_out[...] = extras[0:width, :]
    for block in range(3):
        lanes = slice(block * width, (block + 1) * width)
        input_weights[:, lanes] = extras[(1 + block) * width : (2 + block) * width, :]
        state_weights[:, lanes] = extras[(4 + block) * width : (5 + block) * width, :]
        input_bias[lanes] = extras[7 * width + block, :]
        state_bias[lanes] = extras[7 * width + 3 + block, :]


def on_device(
    states,
    node_count,
    edge_features,
    edge_count,
    target_rows,
    source_slots,
    send_rows,
    send_count,
    edge_weight_in,
    edge_bias_in,
    edge_weight_out,
    edge_bias_out,
    input_weights,
    state_weights,
    input_bias,
    state_bias,
    grad_output,
):
    nodes, width = states.shape
    edges, narrow = edge_features.shape
    devices = lax.axis_size("graph")
    received_rows = send_rows.shape[1]
    per_peer = received_rows // devices
    groups = nodes // GROUP
    padded = edges + WINDOW
    shape = jax.ShapeDtypeStruct
    bias_matrix = edge_bias_out.reshape(width, width)

    outgoing, index = call(
        pick_kernel,
        (shape((received_rows, width), LOW), shape((1, received_rows), jnp.int32)),
        [VMEM] * 3,
    )(send_rows, send_count, states)
    received = lax.all_to_all(
        outgoing.reshape(devices, per_peer, width), "graph", split_axis=0, concat_axis=0, tiled=True
    ).reshape(received_rows, width)

    assert received_rows == SLOTS
    rows = jnp.arange(edges, dtype=jnp.int32)
    packed = pack_key(target_rows, source_slots, rows, nodes, received_rows, edges)
    packed = lax.sort(jnp.where(rows < edge_count[0], packed, np.iinfo(np.int32).max), is_stable=False)
    limits = pack_key(jnp.arange(groups, dtype=jnp.int32) * GROUP, 0, 0, nodes, received_rows, edges)
    starts = jnp.sum((packed[None, :] < limits[:, None]).astype(jnp.int32), axis=1)
    starts = jnp.concatenate([starts, edge_count])
    step_count = steps_size(groups, edges)
    steps, target, slots, order, hidden_t, preact_t, sorted_features = call(
        first_kernel,
        (
            shape((step_count,), jnp.int32),
            shape((1, padded), jnp.int32),
            shape((1, edges), jnp.int32),
            shape((1, edges), jnp.int32),
            shape((2 * width, padded), LOW),
            shape((width, edges), F32),
            shape((edges, width), LOW),
        ),
        [SMEM] * 3 + [VMEM] * 4,
        [
            pltpu.VMEM((2 * width, padded), LOW),
            pltpu.VMEM((width, edges), F32),
            pltpu.VMEM((edges, width), LOW),
            pltpu.SemaphoreType.DMA((12,)),
        ],
        out_specs=[SMEM] + [VMEM] * 3 + [ANY] * 3,
        micros=6,
    )(
        starts, node_count, edge_count, packed, edge_features.T, edge_weight_in, edge_bias_in
    )

    tables = place_tables(devices)
    inverse = [np.argsort(t).astype(np.int32) for t in tables]
    half = devices // 2
    out_table = jnp.asarray(np.stack([tables[0], inverse[1][tables[0]] % half]))
    extra = max(16, -(-(7 * width + 6) // (devices * 16)) * 16)
    piece_0 = (width // devices) * (width // 2)
    piece_1 = piece_0 + extra
    new_states, direct, grad_low, by_bias, source_t, keep_0, send_0, keep_1, send_1 = call(
        node_kernel,
        (
            shape((nodes, width), F32),
            shape((nodes, width), F32),
            shape((nodes, width), LOW),
            shape((nodes, width), LOW),
            shape((2 * width, padded), LOW),
            shape((half * piece_0, width), LOW),
            shape((half * piece_0, width), LOW),
            shape((half * piece_1, width), LOW),
            shape((half * piece_1, width), LOW),
        ),
        [SMEM] * 3 + [VMEM] * 3 + [ANY] * 2 + [VMEM] * 7,
        [
            pltpu.VMEM((width, nodes, width), LOW),
            pltpu.VMEM((padded, width), LOW),
            pltpu.VMEM((width, padded), F32),
            pltpu.VMEM((devices * extra, width), F32),
            pltpu.VMEM((nodes, width), F32),
            pltpu.VMEM((nodes, width), F32),
            pltpu.VMEM((2 * width, padded), LOW),
            pltpu.VMEM((width, width * width), LOW),
            pltpu.VMEM((2 * width, padded), LOW),
            pltpu.VMEM((half * piece_0, width), LOW),
            pltpu.VMEM((half * piece_0, width), LOW),
            pltpu.VMEM((half * piece_1, width), LOW),
            pltpu.VMEM((half * piece_1, width), LOW),
            pltpu.SemaphoreType.DMA((2,)),
            pltpu.SemaphoreType.DMA((5,)),
        ],
        out_specs=[VMEM] * 4 + [ANY] * 5,
        micros=24,
    )(
        steps, out_table, node_count, target, slots, received, hidden_t, edge_weight_out,
        bias_matrix, states, input_weights, state_weights, input_bias, state_bias, grad_output,
    )

    late_rows = 32
    scratch = [
        pltpu.VMEM((nodes * (width + 4) + 16, width), F32),
        pltpu.VMEM((width, width * width), LOW),
        pltpu.VMEM((2 * width, padded), LOW),
    ]
    signals = [pltpu.SemaphoreType.DMA((8,)), pltpu.SemaphoreType.DMA]
    edge_array = shape((width, padded), F32)
    kept = {}

    def tie(value, before):
        return lax.optimization_barrier((value, before))[0]

    def source_work(before):
        kept["source"] = call(
            source_kernel,
            shape((width, padded), LOW),
            [SMEM] + [VMEM] * 2 + [ANY, VMEM, ANY],
            scratch + [pltpu.VMEM((width, padded), F32)] + signals,
            micros=15,
        )(steps, target, tie(grad_low, before), edge_weight_out, by_bias, hidden_t)
        return kept["source"]

    def scatter_work(before):
        kept["slots"] = call(
            scatter_kernel, shape((received_rows, width), LOW), [VMEM] * 2, micros=4, limit=24
        )(slots, tie(kept["source"], before))
        return kept["slots"]

    def hidden_work(before):
        kept["hidden"] = call(
            hidden_kernel,
            edge_array,
            [SMEM] + [VMEM] * 2 + [ANY, ANY],
            scratch + signals,
            micros=12,
        )(steps, target, tie(grad_low, before), edge_weight_out, source_t)
        return kept["hidden"]

    def send_back(before):
        before = kept["late"]
        kept["returned"] = lax.all_to_all(
            tie(kept["slots"], before).reshape(devices, per_peer, width),
            "graph",
            split_axis=0,
            concat_axis=0,
            tiled=True,
        ).reshape(received_rows, width)
        return kept["returned"]

    def features_work(before):
        kept["features"], kept["late"] = call(
            features_kernel,
            (shape((narrow, edges), F32), shape((late_rows, width), F32)),
            [VMEM] * 5,
            micros=6,
            limit=20,
        )(order, tie(kept["hidden"], before), preact_t, sorted_features, edge_weight_in)
        return kept["features"]

    def add_late(bit):
        def work(before):
            late = tie(kept["late"], before)
            kept["late"] = late + swap(late, bit, devices)
            return kept["late"]

        return work

    def last_late(bit):
        def work(before):
            kept["late far"] = swap(tie(kept["late"], before), bit, devices)
            return kept["late far"]

        return work

    def add_late_soon(bit):
        def work(before):
            kept["late"] = kept["late"] + swap(kept["late"], bit, devices)
            return kept["late"]

        return work

    def collect(before):
        kept["states"] = call(collect_kernel, shape((nodes, width), F32), [VMEM] * 3)(
            index, kept["returned"], tie(direct, before)
        )
        return kept["states"]

    table = jnp.asarray(np.stack([t[: devices // 2] for t in tables]))
    per_piece = width // devices
    extras_array = shape((devices * extra, width), F32)
    whole_array = shape((width, width * width), F32)

    def blocks(quarters):
        count = quarters * devices // 2
        return [
            pltpu.VMEM((count, width // 2, per_piece * width), F32),
            pltpu.SemaphoreType.DMA((count,)),
        ]

    def assemble_own(own):
        kept["whole"] = call(
            assemble_own_kernel,
            (whole_array, extras_array),
            [SMEM] + [VMEM] * 2,
            blocks(1),
            out_specs=[ANY, VMEM],
            micros=3,
            limit=24,
        )(table, *own)
        return kept["whole"]

    def assemble_middle(far, own):
        whole, extras = kept["whole"]
        kept["whole"] = call(
            assemble_middle_kernel,
            (whole_array, extras_array),
            [SMEM] + [VMEM] * 5 + [ANY],
            blocks(2),
            out_specs=[ANY, VMEM],
            micros=4,
            limit=24,
            aliases={6: 0},
        )(table, *far, *own, extras, whole)
        return kept["whole"]

    last = sum_pieces(
        (keep_0, keep_1),
        (send_0, send_1),
        devices,
        [[source_work], [], [scatter_work], [hidden_work], [features_work], [add_late(0)], [send_back, add_late(4), add_late_soon(3)], [add_late(2), last_late(1), collect]],
        assemble_own,
        assemble_middle,
    )
    whole, extras = kept["whole"]
    whole, grad_bias_out, grad_in_w, grad_st_w, grad_in_b, grad_st_b, grad_w_in, grad_b_in = call(
        assemble_last_kernel,
        (
            whole_array,
            shape((width, width), F32),
            shape((width, 3 * width), F32),
            shape((width, 3 * width), F32),
            shape((3 * width,), F32),
            shape((3 * width,), F32),
            shape((narrow, width), F32),
            shape((width,), F32),
        ),
        [SMEM] + [VMEM] * 5 + [ANY],
        [pltpu.VMEM((devices * extra, width), F32)] + blocks(1),
        out_specs=[ANY] + [VMEM] * 7,
        micros=4,
        limit=24,
        aliases={6: 0},
    )(table, *last, kept["late"], kept["late far"], extras, whole)
    return (
        new_states,
        kept["states"],
        kept["features"].T,
        grad_w_in,
        grad_b_in,
        whole,
        grad_bias_out.reshape(width * width),
        grad_in_w,
        grad_st_w,
        grad_in_b,
        grad_st_b,
    )


def solution(mesh):
    in_specs = (
        P("graph", None),
        P("graph"),
        P("graph", None),
        P("graph"),
        P("graph"),
        P("graph"),
        P("graph", None),
        P("graph", None),
        P(),
        P(),
        P(),
        P(),
        P(),
        P(),
        P(),
        P(),
        P("graph", None),
    )
    out_specs = (
        P("graph", None),
        P("graph", None),
        P("graph", None),
        P(),
        P(),
        P(),
        P(),
        P(),
        P(),
        P(),
        P(),
    )
    return jax.shard_map(
        on_device, mesh=mesh, in_specs=in_specs, out_specs=out_specs, check_vma=False
    )
```

```python
import jax
import jax.numpy as jnp
import numpy as np
from jax import lax
from jax.experimental import pallas as pl
from jax.experimental.pallas import tpu as pltpu
from jax.sharding import PartitionSpec as P

F32 = jnp.float32
LOW = jnp.bfloat16
WINDOW = 256
GROUP = 16
UNROLL = 4
SLOTS = 2048
VMEM = pl.BlockSpec(memory_space=pltpu.VMEM)
SMEM = pl.BlockSpec(memory_space=pltpu.SMEM)

ANY = pl.BlockSpec(memory_space=pl.ANY)


def contract(left, right, left_dim, right_dim):
    return lax.dot_general(
        left, right, (((left_dim,), (right_dim,)), ((), ())), preferred_element_type=F32
    )


def iota(shape, dim):
    return lax.broadcasted_iota(jnp.int32, shape, dim)


def shift_of(size):
    return size.bit_length() - 1


def one_hot(mask):
    return jnp.where(mask, 1.0, 0.0).astype(LOW)


def call(kernel, out_shape, in_specs, scratch=(), out_specs=None, micros=2, limit=60, aliases=None):
    single = not isinstance(out_shape, (tuple, list))
    if out_specs is None:
        out_specs = VMEM if single else [VMEM] * len(out_shape)
    return pl.pallas_call(
        kernel,
        out_shape=out_shape,
        in_specs=in_specs,
        out_specs=out_specs,
        scratch_shapes=scratch,
        input_output_aliases=aliases or {},
        compiler_params=pltpu.CompilerParams(vmem_limit_bytes=limit * 2**20),
        cost_estimate=pl.CostEstimate(
            flops=micros * 10**9, bytes_accessed=2**20, transcendentals=0
        ),
    )


def fetch(copies):
    started = [pltpu.make_async_copy(*copy) for copy in copies]
    for copy in started:
        copy.start()
    return [copy.wait for copy in started]


def as_columns(row, start, size):
    return jnp.broadcast_to(row[:, start : start + size], (128, size)).T


def pick_kernel(rows, count, states, out, index):
    nodes = states.shape[0]
    devices = count.shape[1]
    slots = rows.shape[1]
    per_peer = slots // devices
    counts = jnp.broadcast_to(count[...].astype(F32), (8, devices)).astype(LOW)
    owner = one_hot((iota((devices, slots), 1) >> shift_of(per_peer)) == iota((devices, slots), 0))
    live = jnp.dot(counts, owner, preferred_element_type=F32)[0:1, :].astype(jnp.int32)
    index[...] = jnp.where((iota((1, slots), 1) & (per_peer - 1)) < live, rows[...], -1)
    for start in range(0, slots, 256):
        column = as_columns(index, start, 256)
        chosen = jnp.concatenate(
            [one_hot(column == iota((256, 128), 1) + lane) for lane in range(0, nodes, 128)], axis=1
        )
        out[start : start + 256, :] = jnp.dot(
            chosen, states[...], preferred_element_type=F32
        ).astype(LOW)


def silu_parts(preact):
    gate = jax.nn.sigmoid(preact)
    return preact * gate, gate * (1.0 + preact * (1.0 - gate))


def upper_half(target):
    return ((target >> 3) & 1).astype(F32)


def steps_size(groups, edges):
    return 2 + 2 * (groups + edges // 128 + UNROLL)


def plan_steps(starts, node_count, steps, groups):
    alive = (node_count[0] + (GROUP - 1)) // GROUP

    def base_of(group):
        return (starts[group] // 128) * 128

    def first_step(group, _):
        steps[2 + 2 * group] = group
        steps[3 + 2 * group] = base_of(group)
        return 0

    def further_step(group, at):
        first, last = starts[group], starts[group + 1]
        base = base_of(group)
        count = jnp.where(last > first, (last - base + (WINDOW - 1)) // WINDOW, 0)

        def more(step, at):
            steps[at] = group
            steps[at + 1] = base + WINDOW * step
            return at + 2

        return lax.fori_loop(1, count, more, at)

    lax.fori_loop(0, alive, first_step, 0)
    at = lax.fori_loop(0, alive, further_step, 2 + 2 * alive)
    steps[0] = alive // UNROLL
    steps[1] = (at // 2 - 1 + (UNROLL - 1)) // UNROLL - alive // UNROLL
    for spare in range(UNROLL):
        steps[at + 2 * spare] = groups + 1
        steps[at + 1 + 2 * spare] = 0


def key_bits(nodes, slots, edges):
    low, high = shift_of(edges), shift_of(edges) + shift_of(slots)
    assert high + shift_of(nodes) <= 32
    return low, high, 1 << (31 - high)


def pack_key(target, slot, row, nodes, slots, edges):
    low, high, offset = key_bits(nodes, slots, edges)
    return ((target - offset) << high) | (slot << low) | row


def unpack_key(key, nodes, edges):
    low, high, offset = key_bits(nodes, SLOTS, edges)
    return (key >> high) + offset, (key >> low) & (SLOTS - 1), key & (edges - 1)


def first_kernel(
    starts, node_count, edge_count, packed, features, weight, bias,
    steps, target, slots, order, hidden_out, preact_out, sorted_out, hidden_t, preact_t, sorted_features, left,
):
    edges = order.shape[1]
    nodes = (starts.shape[0] - 1) * GROUP
    key = packed[...].reshape(1, edges)
    here, slot, row = unpack_key(key, nodes, edges)
    target[:, :edges] = jnp.where(iota((1, edges), 1) < edge_count[0], here, nodes)
    target[:, edges:] = jnp.full((1, target.shape[1] - edges), nodes, jnp.int32)
    slots[...] = slot
    order[...] = row
    narrow = weight.shape[0]
    spread = 128 // narrow
    table_rows = edges // spread
    plan_steps(starts, node_count, steps, starts.shape[0] - 1)
    tiled = jnp.concatenate([weight[...]] * spread, axis=0)
    table = jnp.concatenate(
        [features[:, c * table_rows : (c + 1) * table_rows] for c in range(spread)], axis=0
    )
    table = table.astype(F32).T.astype(LOW)
    lane_part = iota((256, 128), 1) >> shift_of(narrow)
    bias_column = as_columns(bias[...].reshape(1, 128), 0, 128)
    bias_columns = jnp.concatenate([bias_column] * 2, axis=1)
    hidden_t[:, edges:] = jnp.zeros((256, hidden_t.shape[1] - edges), LOW)
    waits = []
    for start in range(0, edges, 256):
        column = as_columns(order, start, 256)
        low = column & (table_rows - 1)
        chosen = jnp.concatenate(
            [one_hot(low == iota((256, 128), 1) + lane) for lane in range(0, table_rows, 128)], axis=1
        )
        got = jnp.dot(chosen, table, preferred_element_type=F32)
        part = jnp.where((column >> shift_of(table_rows)) == lane_part, got, 0.0).astype(LOW)
        sorted_features[start : start + 256, :] = part
        preact = contract(tiled, part, 0, 1) + bias_columns
        preact_t[:, start : start + 256] = preact
        value = silu_parts(preact)[0]
        upper = upper_half(target[:, start : start + 256])
        hidden_t[0:128, start : start + 256] = (value * (1.0 - upper)).astype(LOW)
        hidden_t[128:256, start : start + 256] = (value * upper).astype(LOW)
        quarter = edges // 4
        if (start + 256) % quarter == 0:
            part = start // quarter
            lanes = slice(part * quarter, (part + 1) * quarter)
            wide = lanes if part < 3 else slice(part * quarter, hidden_t.shape[1])
            waits += fetch(
                [
                    (hidden_t.at[:, wide], hidden_out.at[:, wide], left.at[part]),
                    (preact_t.at[:, lanes], preact_out.at[:, lanes], left.at[4 + part]),
                    (sorted_features.at[lanes, :], sorted_out.at[lanes, :], left.at[8 + part]),
                ]
            )
    for wait in waits:
        wait()


def for_steps(steps, body, apart=False):
    def run(count, first, further, together=UNROLL):
        def several(i, _):
            for u in range(together):
                at = first + 2 * (together * i + u)
                body(steps[at], pl.multiple_of(steps[at + 1], 128), further)
            return 0

        lax.fori_loop(0, max(1, UNROLL // together) * count, several, 0)

    if not apart:
        count = steps[0] + steps[1]
        run(count // 2, 2, None, 2 * UNROLL)
        run(count % 2, 2 + 4 * UNROLL * (count // 2), None)
        return
    run(steps[0], 2, False)
    run(steps[1], 2 + 2 * UNROLL * steps[0], True, UNROLL // 2)


def node_kernel(
    steps, table, node_count, target, slots, received, hidden_there, weight_there, bias_matrix, states,
    input_weights, state_weights, input_bias, state_bias, grad_output,
    new_states, direct, grad_low, by_bias, source_out, *rest,
):
    pieces_out, rest = rest[:4], rest[4:]
    product, picked, source_f, extras, sums, node_sums, hidden, weight, source_t, *rest = rest
    pieces_here, (arrived, left) = rest[:4], rest[4:]
    keep_0, send_0, keep_1, send_1 = pieces_here
    (hidden_ready,) = fetch([(hidden_there, hidden, arrived.at[0])])
    edges = slots.shape[1]
    lookup = 512
    ways = received.shape[0] // lookup
    nodes, width = states.shape
    groups = nodes // GROUP
    pieces = table.shape[1]
    per_piece = width // pieces
    several = jnp.concatenate([received[w * lookup : (w + 1) * lookup, :] for w in range(ways)], axis=1)
    for start in range(0, edges, 256):
        column = as_columns(slots, start, 256)
        chosen = jnp.concatenate(
            [
                one_hot((column & (lookup - 1)) == iota((256, 128), 1) + lane)
                for lane in range(0, lookup, 128)
            ],
            axis=1,
        )
        got = jnp.dot(chosen, several, preferred_element_type=F32)
        way = column >> shift_of(lookup)
        value = got[:, :width]
        for w in range(1, ways):
            value = jnp.where(way == w, got[:, w * width : (w + 1) * width], value)
        picked[start : start + 256, :] = value.astype(LOW)
        turned = value.T
        source_f[:, start : start + 256] = turned
        upper = upper_half(target[:, start : start + 256])
        source_t[0:width, start : start + 256] = (turned * (1.0 - upper)).astype(LOW)
        source_t[width:, start : start + 256] = (turned * upper).astype(LOW)
    tail = picked.shape[0] - edges
    picked[edges:, :] = jnp.zeros((tail, width), LOW)
    source_f[:, edges:] = jnp.zeros((width, tail), F32)
    source_t[:, edges:] = jnp.zeros((2 * width, tail), LOW)
    hidden_ready()
    (weight_ready,) = fetch([(weight_there, weight, arrived.at[1])])
    (source_left,) = fetch([(source_t, source_out, left.at[0])])

    def window_step(group, at, further):
        row = pl.multiple_of(jnp.minimum(group, groups - 1) * GROUP, GROUP)
        there = target[:, pl.ds(at, WINDOW)]
        mine = (there >> 4) == group
        pairs = mine & ((there & 7) == iota((8, WINDOW), 0))
        right = hidden[:, pl.ds(at, WINDOW)]
        all_rows = one_hot(mine & ((there & 15) == iota((GROUP, WINDOW), 0)))
        part = jnp.dot(all_rows, picked[pl.ds(at, WINDOW), :], preferred_element_type=F32)
        if further:
            part = part + sums[pl.ds(row, GROUP), :]
        sums[pl.ds(row, GROUP), :] = part
        chunk = 32
        for first in range(0, width, chunk):
            left = jnp.concatenate(
                [
                    jnp.where(
                        pairs,
                        jnp.broadcast_to(source_f[pl.ds(first + q, 1), pl.ds(at, WINDOW)], (8, WINDOW)),
                        0.0,
                    )
                    for q in range(chunk)
                ],
                axis=0,
            ).astype(LOW)
            part = contract(left, right, 1, 1).reshape(chunk, 8, 2 * width)
            part = jnp.concatenate([part[:, :, :width], part[:, :, width:]], axis=1)
            if further:
                part = part + product[first : first + chunk, pl.ds(row, GROUP), :].astype(F32)
            product[first : first + chunk, pl.ds(row, GROUP), :] = part.astype(LOW)

    def clear(group, _):
        row = pl.multiple_of(group * GROUP, GROUP)
        product[:, pl.ds(row, GROUP), :] = jnp.zeros((width, GROUP, width), LOW)
        sums[pl.ds(row, GROUP), :] = jnp.zeros((GROUP, width), F32)
        return 0

    lax.fori_loop(steps[0] * UNROLL, groups, clear, 0)
    for_steps(steps, window_step, apart=True)

    sums_low = sums[...].astype(LOW)
    node_sums[...] = jnp.dot(sums_low, bias_matrix[...], preferred_element_type=F32)

    def multiply(block, _):
        several = 32
        lanes = pl.multiple_of(block * several * width, several * width)
        left = jnp.concatenate([product[block * several + q] for q in range(several)], axis=1)
        right = jnp.concatenate(
            [weight[:, pl.ds(lanes + q * width, width)] for q in range(several)], axis=0
        )
        node_sums[...] += jnp.dot(left, right, preferred_element_type=F32)
        return 0

    weight_ready()
    lax.fori_loop(0, width // 32, multiply, 0)
    incoming = node_sums[...].astype(LOW)
    alive = jnp.where(iota((nodes, 1), 0) < node_count[0], 1.0, 0.0)
    gate_in = jnp.dot(incoming, input_weights[...], preferred_element_type=F32)
    gate_in = gate_in + input_bias[...].reshape(1, -1)
    gate_hid = jnp.dot(states[...], state_weights[...], preferred_element_type=F32)
    gate_hid = gate_hid + state_bias[...].reshape(1, -1)
    reset = jax.nn.sigmoid(gate_in[:, :width] + gate_hid[:, :width])
    update = jax.nn.sigmoid(gate_in[:, width : 2 * width] + gate_hid[:, width : 2 * width])
    hid_n = gate_hid[:, 2 * width :]
    candidate = jnp.tanh(gate_in[:, 2 * width :] + reset * hid_n)
    values = states[...].astype(F32)
    new_states[...] = alive * ((1.0 - update) * candidate + update * values)
    upstream = grad_output[...] * alive
    grad_cand = upstream * (1.0 - update) * (1.0 - candidate * candidate)
    grad_update = upstream * (values - candidate) * update * (1.0 - update)
    grad_reset = grad_cand * hid_n * reset * (1.0 - reset)
    grad_gate_in = jnp.concatenate([grad_reset, grad_update, grad_cand], axis=1)
    grad_gate_hid = jnp.concatenate([grad_reset, grad_update, grad_cand * reset], axis=1)
    low_in = grad_gate_in.astype(LOW)
    low_hid = grad_gate_hid.astype(LOW)
    low = contract(low_in, input_weights[...], 1, 1).astype(LOW)
    grad_low[...] = low
    by_bias[...] = contract(low, bias_matrix[...], 1, 1).astype(LOW)
    direct[...] = upstream * update + contract(low_hid, state_weights[...], 1, 1)
    extras[0:width, :] = contract(sums_low, low, 0, 0)
    grad_in_w = contract(incoming, low_in, 0, 0)
    grad_st_w = contract(states[...], low_hid, 0, 0)
    in_b = jnp.sum(grad_gate_in, axis=0, keepdims=True)
    st_b = jnp.sum(grad_gate_hid, axis=0, keepdims=True)
    for block in range(3):
        lanes = slice(block * width, (block + 1) * width)
        extras[(1 + block) * width : (2 + block) * width, :] = grad_in_w[:, lanes]
        extras[(4 + block) * width : (5 + block) * width, :] = grad_st_w[:, lanes]
    extras[7 * width :, :] = jnp.zeros((extras.shape[0] - 7 * width, width), F32)
    for block in range(3):
        lanes = slice(block * width, (block + 1) * width)
        extras[7 * width + block : 7 * width + block + 1, :] = in_b[:, lanes]
        extras[7 * width + 3 + block : 7 * width + 4 + block, :] = st_b[:, lanes]

    half = width // 2
    piece_0 = per_piece * half
    piece_1 = keep_1.shape[0] * 2 // pieces
    extra = piece_1 - piece_0
    at_once = max(1, 32 // per_piece)
    waits = [source_left]
    for side, (out_0, out_1) in ((1, (send_0, send_1)), (0, (keep_0, keep_1))):

        def piece_step(step, _):
            for u in range(at_once):
                place = step * at_once + u
                piece = jnp.bitwise_xor(table[0, side * (pieces // 2) + place], lax.axis_index("graph"))
                other = table[1, side * (pieces // 2) + place]
                row_0 = pl.multiple_of(place * piece_0, 16)
                row_1 = pl.multiple_of(other * piece_1, 16)
                for q in range(per_piece):
                    tile = contract(product[piece * per_piece + q], low, 0, 0).astype(LOW)
                    out_0[pl.ds(row_0 + q * half, half), :] = tile[:half, :]
                    out_1[pl.ds(row_1 + q * half, half), :] = tile[half:, :]
                out_1[pl.ds(row_1 + piece_0, extra), :] = extras[
                    pl.ds(pl.multiple_of(piece * extra, 8), extra), :
                ].astype(LOW)
            return 0

        lax.fori_loop(0, pieces // 2 // at_once, piece_step, 0)
        waits += fetch(
            [(pieces_here[p], pieces_out[p], left.at[1 + p]) for p in (side, side + 2)]
        )
    for wait in waits:
        wait()


def expand(grad_low, weight, weight_here, done, spread):
    nodes, width = grad_low.shape
    pitch = width + 4
    parts = done.shape[0]
    several = width // parts

    def arrival(part):
        lanes = pl.ds(pl.multiple_of(part * several * width, several * width), several * width)
        return pltpu.make_async_copy(weight.at[:, lanes], weight_here.at[:, lanes], done.at[part])

    for part in range(parts):
        arrival(part).start()

    def block_step(pair, _):
        for part in (2 * pair, 2 * pair + 1):
            arrival(part).wait()
            first = part * several
            right = jnp.concatenate(
                [
                    weight_here[:, pl.ds(pl.multiple_of((first + q) * width, width), width)]
                    for q in range(several)
                ],
                axis=0,
            )
            both = contract(grad_low[...], right, 1, 1)
            for q in range(several):
                spread[pl.ds(first + q, nodes, stride=pitch), :] = both[:, q * width : (q + 1) * width]
        return 0

    lax.fori_loop(0, parts // 2, block_step, 0)


def source_kernel(
    steps, target, grad_low, weight, by_bias, hidden_t, out, spread, weight_here, hidden_here, sums, done, arrived
):
    nodes, width = grad_low.shape
    groups = nodes // GROUP
    pitch = width + 4
    (ready,) = fetch([(hidden_t, hidden_here, arrived)])
    sums[...] = jnp.zeros_like(sums)
    expand(grad_low, weight, weight_here, done, spread)
    ready()

    def window_step(group, at, further):
        row = jnp.minimum(group, groups - 1) * GROUP
        there = target[:, pl.ds(at, WINDOW)]
        mine = (there >> 4) == group
        hidden = hidden_here[:, pl.ds(at, WINDOW)]
        found = jnp.where(mine, there & 7, -1)
        nodes_here = one_hot(mine & ((there & 15) == iota((GROUP, WINDOW), 0)))
        rows = by_bias[pl.ds(pl.multiple_of(row, GROUP), GROUP), :]
        total = sums[:, pl.ds(at, WINDOW)] + contract(rows, nodes_here, 0, 0)
        value = None
        for v in range(8):
            pair = [spread[pl.ds((row + v + 8 * h) * pitch, width), :].astype(LOW) for h in range(2)]
            part = jnp.dot(jnp.concatenate(pair, axis=1), hidden, preferred_element_type=F32)
            value = jnp.where(found == v, part, 0.0 if value is None else value)
        sums[:, pl.ds(at, WINDOW)] = total + value

    for_steps(steps, window_step)
    out[...] = sums[...].astype(LOW)


def scatter_kernel(slots, sums, out):
    width = sums.shape[0]
    edges = slots.shape[1]
    lookup = 512
    ways = out.shape[0] // lookup
    total = None
    for start in range(0, edges, 1024):
        rights = []
        for at in range(start, start + 1024, 256):
            rows = sums[:, at : at + 256].astype(F32).T
            way = as_columns(slots, at, 256) >> shift_of(lookup)
            rights.append(
                jnp.concatenate([jnp.where(way == w, rows, 0.0) for w in range(ways)], axis=1).astype(LOW)
            )
        chosen = one_hot((slots[:, start : start + 1024] & (lookup - 1)) == iota((lookup, 1024), 0))
        part = jnp.dot(chosen, jnp.concatenate(rights, axis=0), preferred_element_type=F32)
        total = part if total is None else total + part
    for w in range(ways):
        out[w * lookup : (w + 1) * lookup, :] = total[:, w * width : (w + 1) * width].astype(LOW)


def hidden_kernel(
    steps, target, grad_low, weight, source_t, sums, spread, weight_here, source_here, done, arrived
):
    nodes, width = grad_low.shape
    groups = nodes // GROUP
    pitch = width + 4
    (ready,) = fetch([(source_t, source_here, arrived)])
    sums[...] = jnp.zeros_like(sums)
    expand(grad_low, weight, weight_here, done, spread)
    ready()

    def window_step(group, at, further):
        row = jnp.minimum(group, groups - 1) * GROUP
        there = target[:, pl.ds(at, WINDOW)]
        source = source_here[:, pl.ds(at, WINDOW)]
        found = jnp.where((there >> 4) == group, there & 7, -1)
        value = None
        for v in range(8):
            pair = [spread[pl.ds((row + v + 8 * h) * pitch, width), :].astype(LOW) for h in range(2)]
            part = contract(jnp.concatenate(pair, axis=0), source, 0, 0)
            value = jnp.where(found == v, part, 0.0 if value is None else value)
        sums[:, pl.ds(at, WINDOW)] += value

    for_steps(steps, window_step)


def features_kernel(
    order, hidden_sums, preact_t, sorted_features, weight_in, grad_features, late
):
    width = hidden_sums.shape[0]
    narrow = weight_in.shape[0]
    edges = order.shape[1]
    copies = width // narrow
    table_rows = edges // copies
    tiled = jnp.concatenate([weight_in[...]] * copies, axis=0)
    weight_sum = jnp.zeros((width, width), F32)
    bias_sum = jnp.zeros((width, 1), F32)
    total = jnp.zeros((table_rows, width), F32)
    for start in range(0, edges, 512):
        lanes = slice(start, start + 512)
        grad_preact = hidden_sums[:, lanes] * silu_parts(preact_t[:, lanes])[1]
        low = grad_preact.astype(LOW)
        weight_sum = weight_sum + jnp.dot(low, sorted_features[lanes, :], preferred_element_type=F32)
        bias_sum = bias_sum + jnp.sum(grad_preact, axis=1, keepdims=True)
        rows = jnp.dot(tiled, low, preferred_element_type=F32)
        owner = (order[:, lanes] >> shift_of(table_rows)) == (iota((width, 512), 0) >> shift_of(narrow))
        rows = jnp.where(owner, rows, 0.0)
        chosen = one_hot((order[:, lanes] & (table_rows - 1)) == iota((table_rows, 512), 0))
        total = total + jnp.dot(chosen, rows.T.astype(LOW), preferred_element_type=F32)
    turned = total.T
    for copy in range(copies):
        grad_features[:, copy * table_rows : (copy + 1) * table_rows] = turned[
            copy * narrow : (copy + 1) * narrow, :
        ]
    late[...] = jnp.zeros_like(late)
    turned = weight_sum.T
    late[0:narrow, :] = sum(turned[c * narrow : (c + 1) * narrow, :] for c in range(copies))
    late[narrow : narrow + 1, :] = jnp.broadcast_to(bias_sum, (width, width)).T[0:1, :]


def collect(index, returned, direct, out):
    rows = index.shape[1]
    for start in range(0, out.shape[0], 256):
        chosen = index[...] == iota((256, rows), 0) + start
        out[start : start + 256, :] = direct[start : start + 256, :] + jnp.dot(
            one_hot(chosen), returned[...], preferred_element_type=F32
        )


def bit_orders(bits):
    rest = list(range(1, bits))
    if bits < 3:
        return ([0] + rest, [0] + rest)
    return ([0] + rest, [0, rest[1], rest[0]] + rest[2:])


def place_tables(devices):
    bits = devices.bit_length() - 1
    tables = []
    for order in bit_orders(bits):
        place = np.arange(devices)
        position = np.zeros(devices, np.int32)
        for level, bit in enumerate(order):
            position |= (((place >> (bits - 1 - level)) & 1) << bit).astype(np.int32)
        tables.append(position)
    return tables


def swap(value, bit, devices):
    pairs = [(i, i ^ (1 << bit)) for i in range(devices)]
    return lax.ppermute(value, "graph", pairs)


def add_low(left, right):
    return (left.astype(F32) + right.astype(F32)).astype(LOW)


def swap_together(values, bit, devices):
    flat = swap(jnp.concatenate(values, axis=0), bit, devices)
    cuts = np.cumsum([value.shape[0] for value in values])[:-1]
    return jnp.split(flat, cuts, axis=0)


def swap_parts(values, orders, level, devices):
    bits = [order[level] for order in orders]
    if len(set(bits)) == 1 and level > 0:
        return swap_together(values, bits[0], devices)
    return [swap(value, bit, devices) for value, bit in zip(values, bits)]


def sum_pieces(keep, send, devices, works, own_work, middle_work):
    bits = devices.bit_length() - 1
    orders = bit_orders(bits)
    parts = range(len(keep))
    works = list(works)

    def beside(sent, values, got):
        if not works:
            return values, got
        done = [work(sent) for work in works.pop(0)]
        values, got, _ = lax.optimization_barrier((values, got, done))
        return values, got

    keep = list(keep)
    got = swap_parts(send, orders, 0, devices)
    for level in range(1, bits - 1):
        halves = [value.shape[0] // 2 for value in keep]
        send = [add_low(keep[p][halves[p] :], got[p][halves[p] :]) for p in parts]
        keep = [add_low(keep[p][: halves[p]], got[p][: halves[p]]) for p in parts]
        got = swap_parts(send, orders, level, devices)
        keep, got = beside(send, keep, got)
    held = [add_low(keep[p], got[p]) for p in parts]
    got = swap_together(held, orders[0][bits - 1], devices)
    held, got = beside(held, held, got)
    sums = []
    for p in parts:
        half = held[p].shape[0] // 2
        turned = jnp.concatenate([got[p][half:], got[p][:half]], axis=0)
        sums.append(add_low(held[p], turned))
    held = sums
    for level in range(bits - 2, 0, -1):
        other = swap_parts(held, orders, level, devices)
        if level == 1:
            far = swap_parts(held, orders, 0, devices)
            own = own_work(held)
            later = sum(works[:1], [])
            works[:1] = [[lambda before: own] + [lambda before, work=work: work(own) for work in later]]
        held, other = beside(held, held, other)
        if level > 1:
            held = [jnp.concatenate([held[p], other[p]], axis=0) for p in parts]
    last = swap_parts(other, orders, 0, devices)
    works[:1] = [[lambda before: middle_work(far, other)] + sum(works[:1], [])]
    while works:
        other, last = beside(other, other, last)
    return last


def piece_of(table, second, far, part, place):
    places = table.shape[1] // 2
    piece = jnp.bitwise_xor(table[part, second * places + place], lax.axis_index("graph"))
    return jnp.bitwise_xor(piece, far)


def assemble(batches, table, done, blocks, whole, extras, beside=None):
    places = table.shape[1] // 2
    width = extras.shape[1]
    per_piece = whole.shape[1] // width // (4 * places)
    half = width // 2
    copies = []
    for batch, (second, far, values) in enumerate(batches):
        sizes = [value.shape[0] // places for value in values]
        extra = sizes[1] - per_piece * half
        for part, value in enumerate(values):
            for place in range(places):
                slot = len(copies)
                row = place * sizes[part]
                for q in range(per_piece):
                    blocks[slot, :, q * width : (q + 1) * width] = value[
                        row + q * half : row + (q + 1) * half, :
                    ].astype(F32)
                if part == 1:
                    goal = (batch * places + place) * extra
                    extras[goal : goal + extra, :] = value[row + per_piece * half : row + sizes[part], :]
                piece = piece_of(table, second, far, part, place)
                lane = pl.multiple_of(piece * (per_piece * width), per_piece * width)
                copy = pltpu.make_async_copy(
                    blocks.at[slot],
                    whole.at[pl.ds(part * half, half), pl.ds(lane, per_piece * width)],
                    done.at[slot],
                )
                copy.start()
                copies.append(copy)
    if beside is not None:
        beside()
    for copy in copies:
        copy.wait()


def assemble_own_kernel(table, own_0, own_1, whole, extras, blocks, done):
    assemble([(0, 0, (own_0, own_1))], table, done, blocks, whole, extras)


def assemble_middle_kernel(table, far_0, far_1, own_0, own_1, whole_in, whole, extras, blocks, done):
    del whole_in
    batches = [(0, 1, (far_0, far_1)), (1, 0, (own_0, own_1))]
    assemble(batches, table, done, blocks, whole, extras)


def assemble_last_kernel(
    table, far_0, far_1, late, late_far, index, returned, direct, extras_own, extras_middle, whole_in,
    whole, bias_out, input_weights, state_weights, input_bias, state_bias, weight_in, bias_in, grad_states,
    extras_last, extras, blocks, done,
):
    del whole_in

    def beside():
        narrow = weight_in.shape[0]
        weight_in[...] = late[:narrow, :] + late_far[:narrow, :]
        bias_in[...] = late[narrow, :] + late_far[narrow, :]
        collect(index, returned, direct, grad_states)
        places = table.shape[1] // 2
        extra = extras_own.shape[0] // places
        for value, halves in (
            (extras_own, ((0, 0),)),
            (extras_middle, ((0, 1), (1, 0))),
            (extras_last, ((1, 1),)),
        ):
            for batch, (second, far) in enumerate(halves):
                for place in range(places):
                    row = (batch * places + place) * extra
                    piece = piece_of(table, second, far, 1, place)
                    extras[pl.ds(pl.multiple_of(piece * extra, 8), extra), :] = value[
                        row : row + extra, :
                    ].astype(F32)
        width = extras.shape[1]
        bias_out[...] = extras[0:width, :]
        for block in range(3):
            lanes = slice(block * width, (block + 1) * width)
            input_weights[:, lanes] = extras[(1 + block) * width : (2 + block) * width, :]
            state_weights[:, lanes] = extras[(4 + block) * width : (5 + block) * width, :]
            input_bias[lanes] = extras[7 * width + block, :]
            state_bias[lanes] = extras[7 * width + 3 + block, :]

    assemble([(1, 1, (far_0, far_1))], table, done, blocks, whole, extras_last, beside)


def on_device(
    states,
    node_count,
    edge_features,
    edge_count,
    target_rows,
    source_slots,
    send_rows,
    send_count,
    edge_weight_in,
    edge_bias_in,
    edge_weight_out,
    edge_bias_out,
    input_weights,
    state_weights,
    input_bias,
    state_bias,
    grad_output,
):
    nodes, width = states.shape
    edges, narrow = edge_features.shape
    devices = lax.axis_size("graph")
    received_rows = send_rows.shape[1]
    per_peer = received_rows // devices
    groups = nodes // GROUP
    padded = edges + WINDOW
    shape = jax.ShapeDtypeStruct
    bias_matrix = edge_bias_out.reshape(width, width)

    outgoing, index = call(
        pick_kernel,
        (shape((received_rows, width), LOW), shape((1, received_rows), jnp.int32)),
        [VMEM] * 3,
    )(send_rows, send_count, states)
    received = lax.all_to_all(
        outgoing.reshape(devices, per_peer, width), "graph", split_axis=0, concat_axis=0, tiled=True
    ).reshape(received_rows, width)

    assert received_rows == SLOTS
    rows = jnp.arange(edges, dtype=jnp.int32)
    packed = pack_key(target_rows, source_slots, rows, nodes, received_rows, edges)
    packed = lax.sort(jnp.where(rows < edge_count[0], packed, np.iinfo(np.int32).max), is_stable=False)
    limits = pack_key(jnp.arange(groups, dtype=jnp.int32) * GROUP, 0, 0, nodes, received_rows, edges)
    starts = jnp.sum((packed[None, :] < limits[:, None]).astype(jnp.int32), axis=1)
    starts = jnp.concatenate([starts, edge_count])
    step_count = steps_size(groups, edges)
    steps, target, slots, order, hidden_t, preact_t, sorted_features = call(
        first_kernel,
        (
            shape((step_count,), jnp.int32),
            shape((1, padded), jnp.int32),
            shape((1, edges), jnp.int32),
            shape((1, edges), jnp.int32),
            shape((2 * width, padded), LOW),
            shape((width, edges), F32),
            shape((edges, width), LOW),
        ),
        [SMEM] * 3 + [VMEM] * 4,
        [
            pltpu.VMEM((2 * width, padded), LOW),
            pltpu.VMEM((width, edges), F32),
            pltpu.VMEM((edges, width), LOW),
            pltpu.SemaphoreType.DMA((12,)),
        ],
        out_specs=[SMEM] + [VMEM] * 3 + [ANY] * 3,
        micros=6,
    )(
        starts, node_count, edge_count, packed, edge_features.T, edge_weight_in, edge_bias_in
    )

    tables = place_tables(devices)
    inverse = [np.argsort(t).astype(np.int32) for t in tables]
    half = devices // 2
    out_table = jnp.asarray(np.stack([tables[0], inverse[1][tables[0]] % half]))
    extra = max(16, -(-(7 * width + 6) // (devices * 16)) * 16)
    piece_0 = (width // devices) * (width // 2)
    piece_1 = piece_0 + extra
    new_states, direct, grad_low, by_bias, source_t, keep_0, send_0, keep_1, send_1 = call(
        node_kernel,
        (
            shape((nodes, width), F32),
            shape((nodes, width), F32),
            shape((nodes, width), LOW),
            shape((nodes, width), LOW),
            shape((2 * width, padded), LOW),
            shape((half * piece_0, width), LOW),
            shape((half * piece_0, width), LOW),
            shape((half * piece_1, width), LOW),
            shape((half * piece_1, width), LOW),
        ),
        [SMEM] * 3 + [VMEM] * 3 + [ANY] * 2 + [VMEM] * 7,
        [
            pltpu.VMEM((width, nodes, width), LOW),
            pltpu.VMEM((padded, width), LOW),
            pltpu.VMEM((width, padded), F32),
            pltpu.VMEM((devices * extra, width), F32),
            pltpu.VMEM((nodes, width), F32),
            pltpu.VMEM((nodes, width), F32),
            pltpu.VMEM((2 * width, padded), LOW),
            pltpu.VMEM((width, width * width), LOW),
            pltpu.VMEM((2 * width, padded), LOW),
            pltpu.VMEM((half * piece_0, width), LOW),
            pltpu.VMEM((half * piece_0, width), LOW),
            pltpu.VMEM((half * piece_1, width), LOW),
            pltpu.VMEM((half * piece_1, width), LOW),
            pltpu.SemaphoreType.DMA((2,)),
            pltpu.SemaphoreType.DMA((5,)),
        ],
        out_specs=[VMEM] * 4 + [ANY] * 5,
        micros=24,
    )(
        steps, out_table, node_count, target, slots, received, hidden_t, edge_weight_out,
        bias_matrix, states, input_weights, state_weights, input_bias, state_bias, grad_output,
    )

    late_rows = 32
    scratch = [
        pltpu.VMEM((nodes * (width + 4) + 16, width), F32),
        pltpu.VMEM((width, width * width), LOW),
        pltpu.VMEM((2 * width, padded), LOW),
    ]
    signals = [pltpu.SemaphoreType.DMA((8,)), pltpu.SemaphoreType.DMA]
    edge_array = shape((width, padded), F32)
    kept = {}

    def tie(value, before):
        return lax.optimization_barrier((value, before))[0]

    def source_work(before):
        kept["source"] = call(
            source_kernel,
            shape((width, padded), LOW),
            [SMEM] + [VMEM] * 2 + [ANY, VMEM, ANY],
            scratch + [pltpu.VMEM((width, padded), F32)] + signals,
            micros=15,
        )(steps, target, tie(grad_low, before), edge_weight_out, by_bias, hidden_t)
        return kept["source"]

    def scatter_work(before):
        kept["slots"] = call(
            scatter_kernel, shape((received_rows, width), LOW), [VMEM] * 2, micros=4, limit=24
        )(slots, tie(kept["source"], before))
        return kept["slots"]

    def hidden_work(before):
        kept["hidden"] = call(
            hidden_kernel,
            edge_array,
            [SMEM] + [VMEM] * 2 + [ANY, ANY],
            scratch + signals,
            micros=12,
        )(steps, target, tie(grad_low, before), edge_weight_out, source_t)
        return kept["hidden"]

    def send_back(before):
        slots = tie(kept["slots"], before)
        kept["returned"] = lax.all_to_all(
            slots.reshape(devices, per_peer, width), "graph", split_axis=0, concat_axis=0, tiled=True
        ).reshape(received_rows, width)
        return slots

    def arrive(before):
        return kept["returned"]

    def features_work(before):
        kept["features"], kept["late"] = call(
            features_kernel,
            (shape((narrow, edges), F32), shape((late_rows, width), F32)),
            [VMEM] * 5,
            micros=6,
            limit=20,
        )(order, tie(kept["hidden"], before), preact_t, sorted_features, edge_weight_in)
        return kept["features"]

    def add_late(bit):
        def work(before):
            late = tie(kept["late"], before)
            kept["late"] = late + swap(late, bit, devices)
            return kept["late"]

        return work

    def last_late(bit):
        def work(before):
            kept["late far"] = swap(tie(kept["late"], before), bit, devices)
            return kept["late far"]

        return work

    def add_late_soon(bit):
        def work(before):
            kept["late"] = kept["late"] + swap(kept["late"], bit, devices)
            return kept["late"]

        return work

    table = jnp.asarray(np.stack([t[: devices // 2] for t in tables]))
    per_piece = width // devices
    places = devices // 4
    whole_array = shape((width, width * width), F32)

    def blocks(quarters):
        count = quarters * devices // 2
        return [
            pltpu.VMEM((count, width // 2, per_piece * width), F32),
            pltpu.SemaphoreType.DMA((count,)),
        ]

    def assemble_own(own):
        kept["whole"] = call(
            assemble_own_kernel,
            (whole_array, shape((places * extra, width), LOW)),
            [SMEM] + [VMEM] * 2,
            blocks(1),
            out_specs=[ANY, VMEM],
            micros=3,
            limit=24,
        )(table, *own)
        return kept["whole"]

    def assemble_middle(far, own):
        whole, kept["extras"] = kept["whole"]
        kept["whole"] = call(
            assemble_middle_kernel,
            (whole_array, shape((2 * places * extra, width), LOW)),
            [SMEM] + [VMEM] * 4 + [ANY],
            blocks(2),
            out_specs=[ANY, VMEM],
            micros=4,
            limit=24,
            aliases={5: 0},
        )(table, *far, *own, whole)
        return kept["whole"]

    last = sum_pieces(
        (keep_0, keep_1),
        (send_0, send_1),
        devices,
        [[source_work], [], [scatter_work], [hidden_work], [features_work], [send_back, add_late(0)], [arrive, add_late(4), add_late_soon(3), add_late_soon(2)], [last_late(1)]],
        assemble_own,
        assemble_middle,
    )
    whole, extras = kept["whole"]
    whole, grad_bias_out, grad_in_w, grad_st_w, grad_in_b, grad_st_b, grad_w_in, grad_b_in, grad_states = call(
        assemble_last_kernel,
        (
            whole_array,
            shape((width, width), F32),
            shape((width, 3 * width), F32),
            shape((width, 3 * width), F32),
            shape((3 * width,), F32),
            shape((3 * width,), F32),
            shape((narrow, width), F32),
            shape((width,), F32),
            shape((nodes, width), F32),
        ),
        [SMEM] + [VMEM] * 9 + [ANY],
        [pltpu.VMEM((places * extra, width), LOW), pltpu.VMEM((devices * extra, width), F32)] + blocks(1),
        out_specs=[ANY] + [VMEM] * 8,
        micros=4,
        limit=24,
        aliases={10: 0},
    )(
        table, *last, kept["late"], kept["late far"], index, kept["returned"], direct, kept["extras"],
        extras, whole,
    )
    return (
        new_states,
        grad_states,
        kept["features"].T,
        grad_w_in,
        grad_b_in,
        whole,
        grad_bias_out.reshape(width * width),
        grad_in_w,
        grad_st_w,
        grad_in_b,
        grad_st_b,
    )


def solution(mesh):
    in_specs = (
        P("graph", None),
        P("graph"),
        P("graph", None),
        P("graph"),
        P("graph"),
        P("graph"),
        P("graph", None),
        P("graph", None),
        P(),
        P(),
        P(),
        P(),
        P(),
        P(),
        P(),
        P(),
        P("graph", None),
    )
    out_specs = (
        P("graph", None),
        P("graph", None),
        P("graph", None),
        P(),
        P(),
        P(),
        P(),
        P(),
        P(),
        P(),
        P(),
    )
    return jax.shard_map(
        on_device, mesh=mesh, in_specs=in_specs, out_specs=out_specs, check_vma=False
    )
```

```python
import jax
import jax.numpy as jnp
import numpy as np
from jax import lax
from jax.experimental import pallas as pl
from jax.experimental.pallas import tpu as pltpu
from jax.sharding import PartitionSpec as P

F32 = jnp.float32
LOW = jnp.bfloat16
WINDOW = 256
GROUP = 16
UNROLL = 4
SLOTS = 2048
VMEM = pl.BlockSpec(memory_space=pltpu.VMEM)
SMEM = pl.BlockSpec(memory_space=pltpu.SMEM)

ANY = pl.BlockSpec(memory_space=pl.ANY)


def contract(left, right, left_dim, right_dim):
    return lax.dot_general(
        left, right, (((left_dim,), (right_dim,)), ((), ())), preferred_element_type=F32
    )


def iota(shape, dim):
    return lax.broadcasted_iota(jnp.int32, shape, dim)


def shift_of(size):
    return size.bit_length() - 1


def one_hot(mask):
    return jnp.where(mask, 1.0, 0.0).astype(LOW)


def call(kernel, out_shape, in_specs, scratch=(), out_specs=None, micros=2, limit=60, aliases=None):
    single = not isinstance(out_shape, (tuple, list))
    if out_specs is None:
        out_specs = VMEM if single else [VMEM] * len(out_shape)
    return pl.pallas_call(
        kernel,
        out_shape=out_shape,
        in_specs=in_specs,
        out_specs=out_specs,
        scratch_shapes=scratch,
        input_output_aliases=aliases or {},
        compiler_params=pltpu.CompilerParams(vmem_limit_bytes=limit * 2**20),
        cost_estimate=pl.CostEstimate(
            flops=micros * 10**9, bytes_accessed=2**20, transcendentals=0
        ),
    )


def fetch(copies):
    started = [pltpu.make_async_copy(*copy) for copy in copies]
    for copy in started:
        copy.start()
    return [copy.wait for copy in started]


def as_columns(row, start, size):
    return jnp.broadcast_to(row[:, start : start + size], (128, size)).T


def pick_kernel(rows, count, states, out, index):
    nodes = states.shape[0]
    devices = count.shape[1]
    slots = rows.shape[1]
    per_peer = slots // devices
    counts = jnp.broadcast_to(count[...].astype(F32), (8, devices)).astype(LOW)
    owner = one_hot((iota((devices, slots), 1) >> shift_of(per_peer)) == iota((devices, slots), 0))
    live = jnp.dot(counts, owner, preferred_element_type=F32)[0:1, :].astype(jnp.int32)
    index[...] = jnp.where((iota((1, slots), 1) & (per_peer - 1)) < live, rows[...], -1)
    for start in range(0, slots, 256):
        column = as_columns(index, start, 256)
        chosen = jnp.concatenate(
            [one_hot(column == iota((256, 128), 1) + lane) for lane in range(0, nodes, 128)], axis=1
        )
        out[start : start + 256, :] = jnp.dot(
            chosen, states[...], preferred_element_type=F32
        ).astype(LOW)


def silu_parts(preact):
    gate = jax.nn.sigmoid(preact)
    return preact * gate, gate * (1.0 + preact * (1.0 - gate))


def upper_half(target):
    return ((target >> 3) & 1).astype(F32)


def steps_size(groups, edges):
    return 2 + 2 * (groups + edges // 128 + UNROLL)


def plan_steps(starts, node_count, steps, groups):
    alive = (node_count[0] + (GROUP - 1)) // GROUP

    def base_of(group):
        return (starts[group] // 128) * 128

    def first_step(group, _):
        steps[2 + 2 * group] = group
        steps[3 + 2 * group] = base_of(group)
        return 0

    def further_step(group, at):
        first, last = starts[group], starts[group + 1]
        base = base_of(group)
        count = jnp.where(last > first, (last - base + (WINDOW - 1)) // WINDOW, 0)

        def more(step, at):
            steps[at] = group
            steps[at + 1] = base + WINDOW * step
            return at + 2

        return lax.fori_loop(1, count, more, at)

    lax.fori_loop(0, alive, first_step, 0)
    at = lax.fori_loop(0, alive, further_step, 2 + 2 * alive)
    steps[0] = alive // UNROLL
    steps[1] = (at // 2 - 1 + (UNROLL - 1)) // UNROLL - alive // UNROLL
    for spare in range(UNROLL):
        steps[at + 2 * spare] = groups + 1
        steps[at + 1 + 2 * spare] = 0


def key_bits(nodes, slots, edges):
    low, high = shift_of(edges), shift_of(edges) + shift_of(slots)
    assert high + shift_of(nodes) <= 32
    return low, high, 1 << (31 - high)


def pack_key(target, slot, row, nodes, slots, edges):
    low, high, offset = key_bits(nodes, slots, edges)
    return ((target - offset) << high) | (slot << low) | row


def unpack_key(key, nodes, edges):
    low, high, offset = key_bits(nodes, SLOTS, edges)
    return (key >> high) + offset, (key >> low) & (SLOTS - 1), key & (edges - 1)


def first_kernel(
    starts, node_count, edge_count, packed, features, weight, bias,
    steps, target, slots, order, hidden_out, preact_out, sorted_out, hidden_t, preact_t, sorted_features, left,
):
    edges = order.shape[1]
    nodes = (starts.shape[0] - 1) * GROUP
    key = packed[...].reshape(1, edges)
    here, slot, row = unpack_key(key, nodes, edges)
    target[:, :edges] = jnp.where(iota((1, edges), 1) < edge_count[0], here, nodes)
    target[:, edges:] = jnp.full((1, target.shape[1] - edges), nodes, jnp.int32)
    slots[...] = slot
    order[...] = row
    narrow = weight.shape[0]
    spread = 128 // narrow
    table_rows = edges // spread
    plan_steps(starts, node_count, steps, starts.shape[0] - 1)
    tiled = jnp.concatenate([weight[...]] * spread, axis=0)
    table = jnp.concatenate(
        [features[:, c * table_rows : (c + 1) * table_rows] for c in range(spread)], axis=0
    )
    table = table.astype(F32).T.astype(LOW)
    lane_part = iota((256, 128), 1) >> shift_of(narrow)
    bias_column = as_columns(bias[...].reshape(1, 128), 0, 128)
    bias_columns = jnp.concatenate([bias_column] * 2, axis=1)
    hidden_t[:, edges:] = jnp.zeros((256, hidden_t.shape[1] - edges), LOW)
    waits = []
    for start in range(0, edges, 256):
        column = as_columns(order, start, 256)
        low = column & (table_rows - 1)
        chosen = jnp.concatenate(
            [one_hot(low == iota((256, 128), 1) + lane) for lane in range(0, table_rows, 128)], axis=1
        )
        got = jnp.dot(chosen, table, preferred_element_type=F32)
        part = jnp.where((column >> shift_of(table_rows)) == lane_part, got, 0.0).astype(LOW)
        sorted_features[start : start + 256, :] = part
        preact = contract(tiled, part, 0, 1) + bias_columns
        preact_t[:, start : start + 256] = preact
        value = silu_parts(preact)[0]
        upper = upper_half(target[:, start : start + 256])
        hidden_t[0:128, start : start + 256] = (value * (1.0 - upper)).astype(LOW)
        hidden_t[128:256, start : start + 256] = (value * upper).astype(LOW)
        quarter = edges // 4
        if (start + 256) % quarter == 0:
            part = start // quarter
            lanes = slice(part * quarter, (part + 1) * quarter)
            wide = lanes if part < 3 else slice(part * quarter, hidden_t.shape[1])
            waits += fetch(
                [
                    (hidden_t.at[:, wide], hidden_out.at[:, wide], left.at[part]),
                    (preact_t.at[:, lanes], preact_out.at[:, lanes], left.at[4 + part]),
                    (sorted_features.at[lanes, :], sorted_out.at[lanes, :], left.at[8 + part]),
                ]
            )
    for wait in waits:
        wait()


def for_steps(steps, body, apart=False):
    def run(count, first, further, together=UNROLL):
        def several(i, _):
            for u in range(together):
                at = first + 2 * (together * i + u)
                body(steps[at], pl.multiple_of(steps[at + 1], 128), further)
            return 0

        lax.fori_loop(0, max(1, UNROLL // together) * count, several, 0)

    if not apart:
        count = steps[0] + steps[1]
        run(count // 2, 2, None, 2 * UNROLL)
        run(count % 2, 2 + 4 * UNROLL * (count // 2), None)
        return
    run(steps[0], 2, False)
    run(steps[1], 2 + 2 * UNROLL * steps[0], True, UNROLL // 2)


def node_kernel(
    steps, table, node_count, target, slots, received, hidden_there, weight_there, bias_matrix, states,
    input_weights, state_weights, input_bias, state_bias, grad_output,
    new_states, direct, grad_low, by_bias, source_out, *rest,
):
    pieces_out, rest = rest[:4], rest[4:]
    product, picked, source_f, extras, sums, node_sums, hidden, weight, source_t, *rest = rest
    pieces_here, (arrived, left) = rest[:4], rest[4:]
    keep_0, send_0, keep_1, send_1 = pieces_here
    (hidden_ready,) = fetch([(hidden_there, hidden, arrived.at[0])])
    edges = slots.shape[1]
    lookup = 512
    ways = received.shape[0] // lookup
    nodes, width = states.shape
    groups = nodes // GROUP
    pieces = table.shape[1]
    per_piece = width // pieces
    several = jnp.concatenate([received[w * lookup : (w + 1) * lookup, :] for w in range(ways)], axis=1)
    for start in range(0, edges, 256):
        column = as_columns(slots, start, 256)
        chosen = jnp.concatenate(
            [
                one_hot((column & (lookup - 1)) == iota((256, 128), 1) + lane)
                for lane in range(0, lookup, 128)
            ],
            axis=1,
        )
        got = jnp.dot(chosen, several, preferred_element_type=F32)
        way = column >> shift_of(lookup)
        value = got[:, :width]
        for w in range(1, ways):
            value = jnp.where(way == w, got[:, w * width : (w + 1) * width], value)
        picked[start : start + 256, :] = value.astype(LOW)
        turned = value.T
        source_f[:, start : start + 256] = turned
        upper = upper_half(target[:, start : start + 256])
        source_t[0:width, start : start + 256] = (turned * (1.0 - upper)).astype(LOW)
        source_t[width:, start : start + 256] = (turned * upper).astype(LOW)
    tail = picked.shape[0] - edges
    picked[edges:, :] = jnp.zeros((tail, width), LOW)
    source_f[:, edges:] = jnp.zeros((width, tail), F32)
    source_t[:, edges:] = jnp.zeros((2 * width, tail), LOW)
    hidden_ready()
    (weight_ready,) = fetch([(weight_there, weight, arrived.at[1])])
    (source_left,) = fetch([(source_t, source_out, left.at[0])])

    def window_step(group, at, further):
        row = pl.multiple_of(jnp.minimum(group, groups - 1) * GROUP, GROUP)
        there = target[:, pl.ds(at, WINDOW)]
        mine = (there >> 4) == group
        pairs = mine & ((there & 7) == iota((8, WINDOW), 0))
        right = hidden[:, pl.ds(at, WINDOW)]
        all_rows = one_hot(mine & ((there & 15) == iota((GROUP, WINDOW), 0)))
        part = jnp.dot(all_rows, picked[pl.ds(at, WINDOW), :], preferred_element_type=F32)
        if further:
            part = part + sums[pl.ds(row, GROUP), :]
        sums[pl.ds(row, GROUP), :] = part
        chunk = 32
        for first in range(0, width, chunk):
            left = jnp.concatenate(
                [
                    jnp.where(
                        pairs,
                        jnp.broadcast_to(source_f[pl.ds(first + q, 1), pl.ds(at, WINDOW)], (8, WINDOW)),
                        0.0,
                    )
                    for q in range(chunk)
                ],
                axis=0,
            ).astype(LOW)
            part = contract(left, right, 1, 1).reshape(chunk, 8, 2 * width)
            part = jnp.concatenate([part[:, :, :width], part[:, :, width:]], axis=1)
            if further:
                part = part + product[first : first + chunk, pl.ds(row, GROUP), :].astype(F32)
            product[first : first + chunk, pl.ds(row, GROUP), :] = part.astype(LOW)

    def clear(group, _):
        row = pl.multiple_of(group * GROUP, GROUP)
        product[:, pl.ds(row, GROUP), :] = jnp.zeros((width, GROUP, width), LOW)
        sums[pl.ds(row, GROUP), :] = jnp.zeros((GROUP, width), F32)
        return 0

    lax.fori_loop(steps[0] * UNROLL, groups, clear, 0)
    for_steps(steps, window_step, apart=True)

    sums_low = sums[...].astype(LOW)
    node_sums[...] = jnp.dot(sums_low, bias_matrix[...], preferred_element_type=F32)

    def multiply(block, _):
        several = 32
        lanes = pl.multiple_of(block * several * width, several * width)
        left = jnp.concatenate([product[block * several + q] for q in range(several)], axis=1)
        right = jnp.concatenate(
            [weight[:, pl.ds(lanes + q * width, width)] for q in range(several)], axis=0
        )
        node_sums[...] += jnp.dot(left, right, preferred_element_type=F32)
        return 0

    weight_ready()
    lax.fori_loop(0, width // 32, multiply, 0)
    incoming = node_sums[...].astype(LOW)
    alive = jnp.where(iota((nodes, 1), 0) < node_count[0], 1.0, 0.0)
    gate_in = jnp.dot(incoming, input_weights[...], preferred_element_type=F32)
    gate_in = gate_in + input_bias[...].reshape(1, -1)
    gate_hid = jnp.dot(states[...], state_weights[...], preferred_element_type=F32)
    gate_hid = gate_hid + state_bias[...].reshape(1, -1)
    reset = jax.nn.sigmoid(gate_in[:, :width] + gate_hid[:, :width])
    update = jax.nn.sigmoid(gate_in[:, width : 2 * width] + gate_hid[:, width : 2 * width])
    hid_n = gate_hid[:, 2 * width :]
    candidate = jnp.tanh(gate_in[:, 2 * width :] + reset * hid_n)
    values = states[...].astype(F32)
    new_states[...] = alive * ((1.0 - update) * candidate + update * values)
    upstream = grad_output[...] * alive
    grad_cand = upstream * (1.0 - update) * (1.0 - candidate * candidate)
    grad_update = upstream * (values - candidate) * update * (1.0 - update)
    grad_reset = grad_cand * hid_n * reset * (1.0 - reset)
    grad_gate_in = jnp.concatenate([grad_reset, grad_update, grad_cand], axis=1)
    grad_gate_hid = jnp.concatenate([grad_reset, grad_update, grad_cand * reset], axis=1)
    low_in = grad_gate_in.astype(LOW)
    low_hid = grad_gate_hid.astype(LOW)
    low = contract(low_in, input_weights[...], 1, 1).astype(LOW)
    grad_low[...] = low
    by_bias[...] = contract(low, bias_matrix[...], 1, 1).astype(LOW)
    direct[...] = upstream * update + contract(low_hid, state_weights[...], 1, 1)
    extras[0:width, :] = contract(sums_low, low, 0, 0)
    grad_in_w = contract(incoming, low_in, 0, 0)
    grad_st_w = contract(states[...], low_hid, 0, 0)
    in_b = jnp.sum(grad_gate_in, axis=0, keepdims=True)
    st_b = jnp.sum(grad_gate_hid, axis=0, keepdims=True)
    for block in range(3):
        lanes = slice(block * width, (block + 1) * width)
        extras[(1 + block) * width : (2 + block) * width, :] = grad_in_w[:, lanes]
        extras[(4 + block) * width : (5 + block) * width, :] = grad_st_w[:, lanes]
    extras[7 * width :, :] = jnp.zeros((extras.shape[0] - 7 * width, width), F32)
    for block in range(3):
        lanes = slice(block * width, (block + 1) * width)
        extras[7 * width + block : 7 * width + block + 1, :] = in_b[:, lanes]
        extras[7 * width + 3 + block : 7 * width + 4 + block, :] = st_b[:, lanes]

    half = width // 2
    piece_0 = per_piece * half
    piece_1 = keep_1.shape[0] * 2 // pieces
    extra = piece_1 - piece_0
    at_once = max(1, 32 // per_piece)
    waits = [source_left]
    for side, (out_0, out_1) in ((1, (send_0, send_1)), (0, (keep_0, keep_1))):

        def piece_step(step, _):
            for u in range(at_once):
                place = step * at_once + u
                piece = jnp.bitwise_xor(table[0, side * (pieces // 2) + place], lax.axis_index("graph"))
                other = table[1, side * (pieces // 2) + place]
                row_0 = pl.multiple_of(place * piece_0, 16)
                row_1 = pl.multiple_of(other * piece_1, 16)
                for q in range(per_piece):
                    tile = contract(product[piece * per_piece + q], low, 0, 0).astype(LOW)
                    out_0[pl.ds(row_0 + q * half, half), :] = tile[:half, :]
                    out_1[pl.ds(row_1 + q * half, half), :] = tile[half:, :]
                out_1[pl.ds(row_1 + piece_0, extra), :] = extras[
                    pl.ds(pl.multiple_of(piece * extra, 8), extra), :
                ].astype(LOW)
            return 0

        lax.fori_loop(0, pieces // 2 // at_once, piece_step, 0)
        waits += fetch(
            [(pieces_here[p], pieces_out[p], left.at[1 + p]) for p in (side, side + 2)]
        )
    for wait in waits:
        wait()


def expand(grad_low, weight, weight_here, done, spread):
    nodes, width = grad_low.shape
    pitch = width + 4
    parts = done.shape[0]
    several = width // parts

    def arrival(part):
        lanes = pl.ds(pl.multiple_of(part * several * width, several * width), several * width)
        return pltpu.make_async_copy(weight.at[:, lanes], weight_here.at[:, lanes], done.at[part])

    for part in range(parts):
        arrival(part).start()

    def block_step(pair, _):
        for part in (2 * pair, 2 * pair + 1):
            arrival(part).wait()
            first = part * several
            right = jnp.concatenate(
                [
                    weight_here[:, pl.ds(pl.multiple_of((first + q) * width, width), width)]
                    for q in range(several)
                ],
                axis=0,
            )
            both = contract(grad_low[...], right, 1, 1)
            for q in range(several):
                spread[pl.ds(first + q, nodes, stride=pitch), :] = both[:, q * width : (q + 1) * width]
        return 0

    lax.fori_loop(0, parts // 2, block_step, 0)


def source_kernel(
    steps, target, grad_low, weight, by_bias, hidden_t, out, spread, weight_here, hidden_here, sums, done, arrived
):
    nodes, width = grad_low.shape
    groups = nodes // GROUP
    pitch = width + 4
    (ready,) = fetch([(hidden_t, hidden_here, arrived)])
    sums[...] = jnp.zeros_like(sums)
    expand(grad_low, weight, weight_here, done, spread)
    ready()

    def window_step(group, at, further):
        row = jnp.minimum(group, groups - 1) * GROUP
        there = target[:, pl.ds(at, WINDOW)]
        mine = (there >> 4) == group
        hidden = hidden_here[:, pl.ds(at, WINDOW)]
        found = jnp.where(mine, there & 7, -1)
        nodes_here = one_hot(mine & ((there & 15) == iota((GROUP, WINDOW), 0)))
        rows = by_bias[pl.ds(pl.multiple_of(row, GROUP), GROUP), :]
        total = sums[:, pl.ds(at, WINDOW)] + contract(rows, nodes_here, 0, 0)
        value = None
        for v in range(8):
            pair = [spread[pl.ds((row + v + 8 * h) * pitch, width), :].astype(LOW) for h in range(2)]
            part = jnp.dot(jnp.concatenate(pair, axis=1), hidden, preferred_element_type=F32)
            value = jnp.where(found == v, part, 0.0 if value is None else value)
        sums[:, pl.ds(at, WINDOW)] = total + value

    for_steps(steps, window_step)
    out[...] = sums[...].astype(LOW)


def scatter_kernel(slots, sums, out):
    width = sums.shape[0]
    edges = slots.shape[1]
    lookup = 512
    ways = out.shape[0] // lookup
    total = None
    for start in range(0, edges, 1024):
        rights = []
        for at in range(start, start + 1024, 256):
            rows = sums[:, at : at + 256].astype(F32).T
            way = as_columns(slots, at, 256) >> shift_of(lookup)
            rights.append(
                jnp.concatenate([jnp.where(way == w, rows, 0.0) for w in range(ways)], axis=1).astype(LOW)
            )
        chosen = one_hot((slots[:, start : start + 1024] & (lookup - 1)) == iota((lookup, 1024), 0))
        part = jnp.dot(chosen, jnp.concatenate(rights, axis=0), preferred_element_type=F32)
        total = part if total is None else total + part
    for w in range(ways):
        out[w * lookup : (w + 1) * lookup, :] = total[:, w * width : (w + 1) * width].astype(LOW)


def hidden_kernel(
    steps, target, grad_low, weight, source_t, sums, spread, weight_here, source_here, done, arrived
):
    nodes, width = grad_low.shape
    groups = nodes // GROUP
    pitch = width + 4
    (ready,) = fetch([(source_t, source_here, arrived)])
    sums[...] = jnp.zeros_like(sums)
    expand(grad_low, weight, weight_here, done, spread)
    ready()

    def window_step(group, at, further):
        row = jnp.minimum(group, groups - 1) * GROUP
        there = target[:, pl.ds(at, WINDOW)]
        source = source_here[:, pl.ds(at, WINDOW)]
        found = jnp.where((there >> 4) == group, there & 7, -1)
        value = None
        for v in range(8):
            pair = [spread[pl.ds((row + v + 8 * h) * pitch, width), :].astype(LOW) for h in range(2)]
            part = contract(jnp.concatenate(pair, axis=0), source, 0, 0)
            value = jnp.where(found == v, part, 0.0 if value is None else value)
        sums[:, pl.ds(at, WINDOW)] += value

    for_steps(steps, window_step)


def features_kernel(
    order, hidden_sums, preact_t, sorted_features, weight_in, grad_features, late
):
    width = hidden_sums.shape[0]
    narrow = weight_in.shape[0]
    edges = order.shape[1]
    copies = width // narrow
    table_rows = edges // copies
    tiled = jnp.concatenate([weight_in[...]] * copies, axis=0)
    weight_sum = jnp.zeros((width, width), F32)
    bias_sum = jnp.zeros((width, 1), F32)
    total = jnp.zeros((table_rows, width), F32)
    for start in range(0, edges, 512):
        lanes = slice(start, start + 512)
        grad_preact = hidden_sums[:, lanes] * silu_parts(preact_t[:, lanes])[1]
        low = grad_preact.astype(LOW)
        weight_sum = weight_sum + jnp.dot(low, sorted_features[lanes, :], preferred_element_type=F32)
        bias_sum = bias_sum + jnp.sum(grad_preact, axis=1, keepdims=True)
        rows = jnp.dot(tiled, low, preferred_element_type=F32)
        owner = (order[:, lanes] >> shift_of(table_rows)) == (iota((width, 512), 0) >> shift_of(narrow))
        rows = jnp.where(owner, rows, 0.0)
        chosen = one_hot((order[:, lanes] & (table_rows - 1)) == iota((table_rows, 512), 0))
        total = total + jnp.dot(chosen, rows.T.astype(LOW), preferred_element_type=F32)
    turned = total.T
    for copy in range(copies):
        grad_features[:, copy * table_rows : (copy + 1) * table_rows] = turned[
            copy * narrow : (copy + 1) * narrow, :
        ]
    late[...] = jnp.zeros_like(late)
    turned = weight_sum.T
    late[0:narrow, :] = sum(turned[c * narrow : (c + 1) * narrow, :] for c in range(copies))
    late[narrow : narrow + 1, :] = jnp.broadcast_to(bias_sum, (width, width)).T[0:1, :]


def collect(index, returned, direct, out):
    rows = index.shape[1]
    for start in range(0, out.shape[0], 256):
        chosen = index[...] == iota((256, rows), 0) + start
        out[start : start + 256, :] = direct[start : start + 256, :] + jnp.dot(
            one_hot(chosen), returned[...], preferred_element_type=F32
        )


def bit_orders(bits):
    rest = list(range(1, bits))
    if bits < 3:
        return ([0] + rest, [0] + rest)
    if bits < 5:
        return ([0] + rest, [0, rest[1], rest[0]] + rest[2:])
    return ([0, rest[0], rest[2], rest[1]] + rest[3:], [0, rest[1], rest[0]] + rest[2:])


def place_tables(devices):
    bits = devices.bit_length() - 1
    tables = []
    for order in bit_orders(bits):
        place = np.arange(devices)
        position = np.zeros(devices, np.int32)
        for level, bit in enumerate(order):
            position |= (((place >> (bits - 1 - level)) & 1) << bit).astype(np.int32)
        tables.append(position)
    return tables


def swap(value, bit, devices):
    pairs = [(i, i ^ (1 << bit)) for i in range(devices)]
    return lax.ppermute(value, "graph", pairs)


def add_low(left, right):
    return (left.astype(F32) + right.astype(F32)).astype(LOW)


def swap_together(values, bit, devices):
    flat = swap(jnp.concatenate(values, axis=0), bit, devices)
    cuts = np.cumsum([value.shape[0] for value in values])[:-1]
    return jnp.split(flat, cuts, axis=0)


def swap_parts(values, orders, level, devices):
    bits = [order[level] for order in orders]
    if len(set(bits)) == 1 and level > 0:
        return swap_together(values, bits[0], devices)
    return [swap(value, bit, devices) for value, bit in zip(values, bits)]


def sum_pieces(keep, send, devices, works, own_work, middle_work):
    bits = devices.bit_length() - 1
    orders = bit_orders(bits)
    parts = range(len(keep))
    works = list(works)

    def beside(sent, values, got):
        if not works:
            return values, got
        done = [work(sent) for work in works.pop(0)]
        values, got, _ = lax.optimization_barrier((values, got, done))
        return values, got

    keep = list(keep)
    got = swap_parts(send, orders, 0, devices)
    for level in range(1, bits - 1):
        halves = [value.shape[0] // 2 for value in keep]
        send = [add_low(keep[p][halves[p] :], got[p][halves[p] :]) for p in parts]
        keep = [add_low(keep[p][: halves[p]], got[p][: halves[p]]) for p in parts]
        got = swap_parts(send, orders, level, devices)
        keep, got = beside(send, keep, got)
    held = [add_low(keep[p], got[p]) for p in parts]
    got = swap_together(held, orders[0][bits - 1], devices)
    held, got = beside(held, held, got)
    sums = []
    for p in parts:
        half = held[p].shape[0] // 2
        turned = jnp.concatenate([got[p][half:], got[p][:half]], axis=0)
        sums.append(add_low(held[p], turned))
    held = sums
    for level in range(bits - 2, 0, -1):
        other = swap_parts(held, orders, level, devices)
        if level == 1:
            far = swap_parts(held, orders, 0, devices)
            own = own_work(held)
            later = sum(works[:1], [])
            works[:1] = [[lambda before: own] + [lambda before, work=work: work(own) for work in later]]
        held, other = beside(held, held, other)
        if level > 1:
            held = [jnp.concatenate([held[p], other[p]], axis=0) for p in parts]
    last = swap_parts(other, orders, 0, devices)
    works[:1] = [[lambda before: middle_work(far, other)] + sum(works[:1], [])]
    while works:
        other, last = beside(other, other, last)
    return last


def piece_of(table, second, far, part, place):
    places = table.shape[1] // 2
    piece = jnp.bitwise_xor(table[part, second * places + place], lax.axis_index("graph"))
    return jnp.bitwise_xor(piece, far)


def assemble(batches, table, done, blocks, whole, extras, beside=None):
    places = table.shape[1] // 2
    width = extras.shape[1]
    per_piece = whole.shape[1] // width // (4 * places)
    half = width // 2
    copies = []
    for batch, (second, far, values) in enumerate(batches):
        sizes = [value.shape[0] // places for value in values]
        extra = sizes[1] - per_piece * half
        for part, value in enumerate(values):
            for place in range(places):
                slot = len(copies)
                row = place * sizes[part]
                for q in range(per_piece):
                    blocks[slot, :, q * width : (q + 1) * width] = value[
                        row + q * half : row + (q + 1) * half, :
                    ].astype(F32)
                if part == 1:
                    goal = (batch * places + place) * extra
                    extras[goal : goal + extra, :] = value[row + per_piece * half : row + sizes[part], :]
                piece = piece_of(table, second, far, part, place)
                lane = pl.multiple_of(piece * (per_piece * width), per_piece * width)
                copy = pltpu.make_async_copy(
                    blocks.at[slot],
                    whole.at[pl.ds(part * half, half), pl.ds(lane, per_piece * width)],
                    done.at[slot],
                )
                copy.start()
                copies.append(copy)
    if beside is not None:
        beside()
    for copy in copies:
        copy.wait()


def assemble_own_kernel(table, own_0, own_1, whole, extras, blocks, done):
    assemble([(0, 0, (own_0, own_1))], table, done, blocks, whole, extras)


def assemble_middle_kernel(table, far_0, far_1, own_0, own_1, whole_in, whole, extras, blocks, done):
    del whole_in
    batches = [(0, 1, (far_0, far_1)), (1, 0, (own_0, own_1))]
    assemble(batches, table, done, blocks, whole, extras)


def assemble_last_kernel(
    table, far_0, far_1, late, late_far, index, returned, direct, extras_own, extras_middle, whole_in,
    whole, bias_out, input_weights, state_weights, input_bias, state_bias, weight_in, bias_in, grad_states,
    extras_last, extras, blocks, done,
):
    del whole_in

    def beside():
        narrow = weight_in.shape[0]
        weight_in[...] = late[:narrow, :] + late_far[:narrow, :]
        bias_in[...] = late[narrow, :] + late_far[narrow, :]
        collect(index, returned, direct, grad_states)
        places = table.shape[1] // 2
        extra = extras_own.shape[0] // places
        for value, halves in (
            (extras_own, ((0, 0),)),
            (extras_middle, ((0, 1), (1, 0))),
            (extras_last, ((1, 1),)),
        ):
            for batch, (second, far) in enumerate(halves):
                for place in range(places):
                    row = (batch * places + place) * extra
                    piece = piece_of(table, second, far, 1, place)
                    extras[pl.ds(pl.multiple_of(piece * extra, 8), extra), :] = value[
                        row : row + extra, :
                    ].astype(F32)
        width = extras.shape[1]
        bias_out[...] = extras[0:width, :]
        for block in range(3):
            lanes = slice(block * width, (block + 1) * width)
            input_weights[:, lanes] = extras[(1 + block) * width : (2 + block) * width, :]
            state_weights[:, lanes] = extras[(4 + block) * width : (5 + block) * width, :]
            input_bias[lanes] = extras[7 * width + block, :]
            state_bias[lanes] = extras[7 * width + 3 + block, :]

    assemble([(1, 1, (far_0, far_1))], table, done, blocks, whole, extras_last, beside)


def on_device(
    states,
    node_count,
    edge_features,
    edge_count,
    target_rows,
    source_slots,
    send_rows,
    send_count,
    edge_weight_in,
    edge_bias_in,
    edge_weight_out,
    edge_bias_out,
    input_weights,
    state_weights,
    input_bias,
    state_bias,
    grad_output,
):
    nodes, width = states.shape
    edges, narrow = edge_features.shape
    devices = lax.axis_size("graph")
    received_rows = send_rows.shape[1]
    per_peer = received_rows // devices
    groups = nodes // GROUP
    padded = edges + WINDOW
    shape = jax.ShapeDtypeStruct
    bias_matrix = edge_bias_out.reshape(width, width)

    outgoing, index = call(
        pick_kernel,
        (shape((received_rows, width), LOW), shape((1, received_rows), jnp.int32)),
        [VMEM] * 3,
    )(send_rows, send_count, states)
    received = lax.all_to_all(
        outgoing.reshape(devices, per_peer, width), "graph", split_axis=0, concat_axis=0, tiled=True
    ).reshape(received_rows, width)

    assert received_rows == SLOTS
    rows = jnp.arange(edges, dtype=jnp.int32)
    packed = pack_key(target_rows, source_slots, rows, nodes, received_rows, edges)
    packed = lax.sort(jnp.where(rows < edge_count[0], packed, np.iinfo(np.int32).max), is_stable=False)
    limits = pack_key(jnp.arange(groups, dtype=jnp.int32) * GROUP, 0, 0, nodes, received_rows, edges)
    starts = jnp.sum((packed[None, :] < limits[:, None]).astype(jnp.int32), axis=1)
    starts = jnp.concatenate([starts, edge_count])
    step_count = steps_size(groups, edges)
    steps, target, slots, order, hidden_t, preact_t, sorted_features = call(
        first_kernel,
        (
            shape((step_count,), jnp.int32),
            shape((1, padded), jnp.int32),
            shape((1, edges), jnp.int32),
            shape((1, edges), jnp.int32),
            shape((2 * width, padded), LOW),
            shape((width, edges), F32),
            shape((edges, width), LOW),
        ),
        [SMEM] * 3 + [VMEM] * 4,
        [
            pltpu.VMEM((2 * width, padded), LOW),
            pltpu.VMEM((width, edges), F32),
            pltpu.VMEM((edges, width), LOW),
            pltpu.SemaphoreType.DMA((12,)),
        ],
        out_specs=[SMEM] + [VMEM] * 3 + [ANY] * 3,
        micros=6,
    )(
        starts, node_count, edge_count, packed, edge_features.T, edge_weight_in, edge_bias_in
    )

    tables = place_tables(devices)
    inverse = [np.argsort(t).astype(np.int32) for t in tables]
    half = devices // 2
    out_table = jnp.asarray(np.stack([tables[0], inverse[1][tables[0]] % half]))
    extra = max(16, -(-(7 * width + 6) // (devices * 16)) * 16)
    piece_0 = (width // devices) * (width // 2)
    piece_1 = piece_0 + extra
    new_states, direct, grad_low, by_bias, source_t, keep_0, send_0, keep_1, send_1 = call(
        node_kernel,
        (
            shape((nodes, width), F32),
            shape((nodes, width), F32),
            shape((nodes, width), LOW),
            shape((nodes, width), LOW),
            shape((2 * width, padded), LOW),
            shape((half * piece_0, width), LOW),
            shape((half * piece_0, width), LOW),
            shape((half * piece_1, width), LOW),
            shape((half * piece_1, width), LOW),
        ),
        [SMEM] * 3 + [VMEM] * 3 + [ANY] * 2 + [VMEM] * 7,
        [
            pltpu.VMEM((width, nodes, width), LOW),
            pltpu.VMEM((padded, width), LOW),
            pltpu.VMEM((width, padded), F32),
            pltpu.VMEM((devices * extra, width), F32),
            pltpu.VMEM((nodes, width), F32),
            pltpu.VMEM((nodes, width), F32),
            pltpu.VMEM((2 * width, padded), LOW),
            pltpu.VMEM((width, width * width), LOW),
            pltpu.VMEM((2 * width, padded), LOW),
            pltpu.VMEM((half * piece_0, width), LOW),
            pltpu.VMEM((half * piece_0, width), LOW),
            pltpu.VMEM((half * piece_1, width), LOW),
            pltpu.VMEM((half * piece_1, width), LOW),
            pltpu.SemaphoreType.DMA((2,)),
            pltpu.SemaphoreType.DMA((5,)),
        ],
        out_specs=[VMEM] * 4 + [ANY] * 5,
        micros=24,
    )(
        steps, out_table, node_count, target, slots, received, hidden_t, edge_weight_out,
        bias_matrix, states, input_weights, state_weights, input_bias, state_bias, grad_output,
    )

    late_rows = 32
    scratch = [
        pltpu.VMEM((nodes * (width + 4) + 16, width), F32),
        pltpu.VMEM((width, width * width), LOW),
        pltpu.VMEM((2 * width, padded), LOW),
    ]
    signals = [pltpu.SemaphoreType.DMA((8,)), pltpu.SemaphoreType.DMA]
    edge_array = shape((width, padded), F32)
    kept = {}

    def tie(value, before):
        return lax.optimization_barrier((value, before))[0]

    def source_work(before):
        kept["source"] = call(
            source_kernel,
            shape((width, padded), LOW),
            [SMEM] + [VMEM] * 2 + [ANY, VMEM, ANY],
            scratch + [pltpu.VMEM((width, padded), F32)] + signals,
            micros=15,
        )(steps, target, tie(grad_low, before), edge_weight_out, by_bias, hidden_t)
        return kept["source"]

    def scatter_work(before):
        kept["slots"] = call(
            scatter_kernel, shape((received_rows, width), LOW), [VMEM] * 2, micros=4, limit=24
        )(slots, tie(kept["source"], before))
        return kept["slots"]

    def hidden_work(before):
        kept["hidden"] = call(
            hidden_kernel,
            edge_array,
            [SMEM] + [VMEM] * 2 + [ANY, ANY],
            scratch + signals,
            micros=12,
        )(steps, target, tie(grad_low, before), edge_weight_out, source_t)
        return kept["hidden"]

    def send_back(before):
        slots = tie(kept["slots"], before)
        kept["returned"] = lax.all_to_all(
            slots.reshape(devices, per_peer, width), "graph", split_axis=0, concat_axis=0, tiled=True
        ).reshape(received_rows, width)
        return slots

    def arrive(before):
        return kept["returned"]

    def features_work(before):
        kept["features"], kept["late"] = call(
            features_kernel,
            (shape((narrow, edges), F32), shape((late_rows, width), F32)),
            [VMEM] * 5,
            micros=6,
            limit=20,
        )(order, tie(kept["hidden"], before), preact_t, sorted_features, edge_weight_in)
        return kept["features"]

    def add_late(bit):
        def work(before):
            late = tie(kept["late"], before)
            kept["late"] = late + swap(late, bit, devices)
            return kept["late"]

        return work

    def last_late(bit):
        def work(before):
            kept["late far"] = swap(tie(kept["late"], before), bit, devices)
            return kept["late far"]

        return work

    def add_late_soon(bit):
        def work(before):
            kept["late"] = kept["late"] + swap(kept["late"], bit, devices)
            return kept["late"]

        return work

    table = jnp.asarray(np.stack([t[: devices // 2] for t in tables]))
    per_piece = width // devices
    places = devices // 4
    whole_array = shape((width, width * width), F32)

    def blocks(quarters):
        count = quarters * devices // 2
        return [
            pltpu.VMEM((count, width // 2, per_piece * width), F32),
            pltpu.SemaphoreType.DMA((count,)),
        ]

    def assemble_own(own):
        kept["whole"] = call(
            assemble_own_kernel,
            (whole_array, shape((places * extra, width), LOW)),
            [SMEM] + [VMEM] * 2,
            blocks(1),
            out_specs=[ANY, VMEM],
            micros=3,
            limit=24,
        )(table, *own)
        return kept["whole"]

    def assemble_middle(far, own):
        whole, kept["extras"] = kept["whole"]
        kept["whole"] = call(
            assemble_middle_kernel,
            (whole_array, shape((2 * places * extra, width), LOW)),
            [SMEM] + [VMEM] * 4 + [ANY],
            blocks(2),
            out_specs=[ANY, VMEM],
            micros=4,
            limit=24,
            aliases={5: 0},
        )(table, *far, *own, whole)
        return kept["whole"]

    last = sum_pieces(
        (keep_0, keep_1),
        (send_0, send_1),
        devices,
        [[source_work], [], [scatter_work], [hidden_work], [features_work], [send_back, add_late(0)], [arrive, add_late(4), add_late_soon(3), add_late_soon(2)], [last_late(1)]],
        assemble_own,
        assemble_middle,
    )
    whole, extras = kept["whole"]
    whole, grad_bias_out, grad_in_w, grad_st_w, grad_in_b, grad_st_b, grad_w_in, grad_b_in, grad_states = call(
        assemble_last_kernel,
        (
            whole_array,
            shape((width, width), F32),
            shape((width, 3 * width), F32),
            shape((width, 3 * width), F32),
            shape((3 * width,), F32),
            shape((3 * width,), F32),
            shape((narrow, width), F32),
            shape((width,), F32),
            shape((nodes, width), F32),
        ),
        [SMEM] + [VMEM] * 9 + [ANY],
        [pltpu.VMEM((places * extra, width), LOW), pltpu.VMEM((devices * extra, width), F32)] + blocks(1),
        out_specs=[ANY] + [VMEM] * 8,
        micros=4,
        limit=24,
        aliases={10: 0},
    )(
        table, *last, kept["late"], kept["late far"], index, kept["returned"], direct, kept["extras"],
        extras, whole,
    )
    return (
        new_states,
        grad_states,
        kept["features"].T,
        grad_w_in,
        grad_b_in,
        whole,
        grad_bias_out.reshape(width * width),
        grad_in_w,
        grad_st_w,
        grad_in_b,
        grad_st_b,
    )


def solution(mesh):
    in_specs = (
        P("graph", None),
        P("graph"),
        P("graph", None),
        P("graph"),
        P("graph"),
        P("graph"),
        P("graph", None),
        P("graph", None),
        P(),
        P(),
        P(),
        P(),
        P(),
        P(),
        P(),
        P(),
        P("graph", None),
    )
    out_specs = (
        P("graph", None),
        P("graph", None),
        P("graph", None),
        P(),
        P(),
        P(),
        P(),
        P(),
        P(),
        P(),
        P(),
    )
    return jax.shard_map(
        on_device, mesh=mesh, in_specs=in_specs, out_specs=out_specs, check_vma=False
    )
```
